128 devices in a mesh: gx: 4 (over z), gy: 4 (over x_hi, core), gz: 8 (over x_lo, y).
Axes of the slice: x: 4 (x_hi: 2, x_lo: 2; x = x_hi * 2 + x_lo), y: 4, z: 4, core: 2. Of those that a mesh axis runs over, the one named last changes fastest.
Arguments:
- coords: float32 [3, 4, 4096, 128], P(None, 'gx', ('gy', 'gz')), may hold values from 0 to 11
- charges: float32 [4, 4096, 128], P('gx', ('gy', 'gz')), may hold values from -1.5 to 1.5
- atom_types: int32 [4, 4096, 128], P('gx', ('gy', 'gz')), may hold values from 0 to 63
- lj_sigma: float32 [64], replicated, may hold values from 2 to 4
- lj_epsilon: float32 [64], replicated, may hold values from 0.02 to 0.25
- tile_list: int32 [4, 4, 8, 2, 512], P('gx', 'gy', 'gz'), may hold values from -1 to 3455, as said below
Outputs:
- forces: float32 [3, 4, 4096, 128], P(None, 'gx', ('gy', 'gz'))
The draws below stay inside these ranges and needn't reach their ends.
Inputs may be any that keep to these rules, and one draw needn't show every extreme that they name: tile_list[x, y, z, 0, t] is a block of brick (x, y, z) (0 to 127) and tile_list[x, y, z, 1, t] a block of its neighbourhood whose cell touches the home block's cell or is that cell (cell indices differ by at most one along each dimension, counted across brick faces periodically); on each brick the listed tiles come first and the remaining slots hold -1 in both rows; at least 256 tiles are listed on every brick and all 512 on some brick; tiles may repeat.
All inputs are finite; a program needn't handle non-finite values.
Results may differ from the reference program's by a relative error of at most 0.0003.
Values sent between devices are 32-bit elements; how exact they have to be, the bound alone decides.
No kernel may reach another device: no remote copies, remote signals or barrier semaphores. Data moves between devices by JAX's collectives and lax.ppermute only.
A program may use at most 128 MiB of HBM per device.

```python
import math
import jax
import jax.numpy as jnp
from jax import lax

GRID = 4
LAYERS = 8
BLOCKS = 128
TILES = 512
TYPES = 64
ATOMS_BLOCK = 128
SLAB = 4096
N_GX = 4
N_GY = 4
N_GZ = 8


def draw_tile_list(key, part):
    devices = N_GX * N_GY * N_GZ
    key_home, key_step, key_count, key_full = jax.random.split(jax.random.fold_in(key, 7), 4)
    home_ids = jax.random.randint(key_home, (devices, TILES), 0, BLOCKS)
    step = jax.random.randint(key_step, (devices, TILES), 0, 27)
    cell_x = home_ids // (GRID * LAYERS) + step // 9 - 1
    cell_y = home_ids // LAYERS % GRID + step // 3 % 3 - 1
    cell_z = home_ids % LAYERS + step % 3 - 1
    off_x = (cell_x >= GRID).astype(jnp.int32) - (cell_x < 0).astype(jnp.int32)
    off_y = (cell_y >= GRID).astype(jnp.int32) - (cell_y < 0).astype(jnp.int32)
    off_z = (cell_z >= LAYERS).astype(jnp.int32) - (cell_z < 0).astype(jnp.int32)
    cell_x = cell_x - off_x * GRID
    cell_y = cell_y - off_y * GRID
    cell_z = cell_z - off_z * LAYERS
    slot = 9 * (off_x + 1) + 3 * (off_y + 1) + (off_z + 1)
    source_ids = slot * BLOCKS + (cell_x * GRID + cell_y) * LAYERS + cell_z
    listed = jax.random.randint(key_count, (devices,), TILES // 2, TILES + 1)
    fullest = jax.random.randint(key_full, (), 0, devices)
    listed = jnp.where(jnp.arange(devices) == fullest, TILES, listed)
    alive = jnp.arange(TILES)[None, :] < listed[:, None]
    home_ids = jnp.where(alive, home_ids, -1)
    source_ids = jnp.where(alive, source_ids, -1)
    return jnp.stack([home_ids, source_ids], 1).reshape(N_GX, N_GY, N_GZ, 2, TILES).astype(jnp.int32)


def touch_ends(values, own_key, least, largest):
    index_at = [jax.random.randint(jax.random.fold_in(own_key, axis), (), 0, length) for axis, length in enumerate(values.shape)]
    main_axis = values.shape.index(max(values.shape))
    next_to = index_at[:main_axis] + [(index_at[main_axis] + 1) % values.shape[main_axis]] + index_at[main_axis + 1:]
    return values.at[tuple(index_at)].set(least).at[tuple(next_to)].set(largest)


def block_levels(own_key, extent, cuts, least, largest):
    def one(position, parts):
        draws = jax.random.uniform(jax.random.fold_in(jax.random.fold_in(own_key, 6), position), (parts,), jnp.float32, least / len(cuts), largest / len(cuts))
        return jnp.repeat(jnp.exp(draws), extent[position] // parts).reshape((-1,) + (1,) * (len(extent) - position - 1))

    gain = one(*cuts[0])
    for cut in cuts[1:]:
        gain = gain * one(*cut)
    return gain


def normal_values(own_key, extent, spread, bound, shards=(), kind=jnp.bfloat16):
    array = spread * jax.random.normal(own_key, extent, jnp.float32)
    if shards:
        array = array * block_levels(own_key, extent, shards, -0.22, 0.18)
    return jnp.clip(array, -bound, bound).astype(kind)


def setup_inputs(seed: int = 0) -> dict:
    splits = jax.random.split(jax.random.key(seed), 7)
    return {
        "coords": jnp.clip(11.0 * jax.random.uniform(splits[0], (3, N_GX, SLAB, ATOMS_BLOCK), jnp.float32) ** block_levels(splits[0], (3, N_GX, SLAB, ATOMS_BLOCK), ((1, 4), (2, 32)), -0.2, 0.2), 0.0, 11.0),
        "charges": normal_values(splits[1], (N_GX, SLAB, ATOMS_BLOCK), 0.3, 1.5, ((0, 4), (1, 32)), jnp.float32),
        "atom_types": touch_ends(jax.random.randint(splits[2], (N_GX, SLAB, ATOMS_BLOCK), 0, TYPES), jax.random.fold_in(splits[2], 1), 0, TYPES - 1).astype(jnp.int32),
        "lj_sigma": jnp.clip(jax.random.uniform(splits[3], (TYPES,), jnp.float32, 2.0, 4.0), 2.0, 4.0),
        "lj_epsilon": jnp.clip(jnp.exp(jax.random.uniform(splits[4], (TYPES,), jnp.float32, math.log(0.02), math.log(0.25))), 0.02, 0.25),
        "tile_list": draw_tile_list(jax.random.fold_in(splits[6], 71), 0),
    }


cell_edge = 11.0
cutoff = 9.0
soft_core = 16.0
coulomb = 332.0636

def radial(softened, sigma_pair, eps_pair, charge_pair):
    ratio = sigma_pair * sigma_pair / softened
    cubed = ratio * ratio * ratio
    return 24.0 * eps_pair * (2.0 * cubed * cubed - cubed) / softened + charge_pair / (softened * jnp.sqrt(softened))

def tile_forces(home_block, source_block):
    delta = home_block[:3, :, :, None] - source_block[:3, :, None, :]
    dist_sq = lax.optimization_barrier(jnp.sum(delta * delta, axis=0))
    softened = dist_sq + soft_core
    sigma_pair = 0.5 * (home_block[4][:, :, None] + source_block[4][:, None, :])
    eps_pair = home_block[5][:, :, None] * source_block[5][:, None, :]
    charge_pair = coulomb * home_block[3][:, :, None] * source_block[3][:, None, :]
    limit = jnp.full_like(softened, cutoff * cutoff + soft_core)
    shifted = radial(softened, sigma_pair, eps_pair, charge_pair) - radial(limit, sigma_pair, eps_pair, charge_pair)
    strength = jnp.where(dist_sq < cutoff * cutoff, shifted, jnp.zeros_like(shifted))
    return lax.optimization_barrier(jnp.sum(strength[None] * delta, axis=3))

def brick_forces(home_atoms, region, tile_ids):
    count = tile_ids.shape[1]
    group = min(64, count)
    grouped = tile_ids.reshape(2, count // group, group).transpose(1, 0, 2)
    blocks = home_atoms.shape[1]
    rows = jnp.arange(blocks, dtype=jnp.int32)

    def advance(totals, pair_ids):
        home_block = jnp.take(home_atoms, jnp.maximum(pair_ids[0], 0), axis=1)
        source_block = jnp.take(region, jnp.maximum(pair_ids[1], 0), axis=1)
        pushes = tile_forces(home_block, source_block)
        selector = (pair_ids[0][None, :] == rows[:, None]).astype(totals.dtype)
        added = jnp.einsum('bg,cga->cba', selector, pushes, precision=lax.Precision.HIGHEST)
        return (totals + added, None)
    start = jnp.zeros((3,) + home_atoms.shape[1:], home_atoms.dtype)
    return lax.scan(advance, start, grouped)[0]

def cell_corners(dtype, grid, layers):
    block = jnp.arange(grid * grid * layers, dtype=jnp.int32)
    return jnp.stack([block // (grid * layers), block // layers % grid, block % layers]).astype(dtype) * cell_edge

def slot_offsets(dtype, grid, layers):
    slot = jnp.arange(27, dtype=jnp.int32)
    steps = jnp.stack([(slot // 9 - 1) * grid, (slot // 3 % 3 - 1) * grid, (slot % 3 - 1) * layers])
    return steps.astype(dtype) * cell_edge

def reference(coords, charges, atom_types, lj_sigma, lj_epsilon, tile_list):
    atoms = jnp.concatenate([coords, charges[None], lj_sigma[atom_types][None], jnp.sqrt(lj_epsilon)[atom_types][None]], 0)
    per_brick = atoms.reshape(6, N_GX, BLOCKS, N_GY, N_GZ, ATOMS_BLOCK).transpose(1, 3, 4, 0, 2, 5)
    corners = cell_corners(coords.dtype, GRID, LAYERS)
    per_brick = jnp.concatenate([per_brick[:, :, :, :3] + corners[:, :, None], per_brick[:, :, :, 3:]], 3)
    offsets = slot_offsets(coords.dtype, GRID, LAYERS)
    slots = jnp.arange(27, dtype=jnp.int32)

    def one_brick(brick):
        xpos = brick // (N_GY * N_GZ)
        ypos = brick // N_GZ % N_GY
        zpos = brick % N_GZ
        nearby = per_brick[(xpos + slots // 9 - 1) % N_GX, (ypos + slots // 3 % 3 - 1) % N_GY, (zpos + slots % 3 - 1) % N_GZ]
        region = jnp.concatenate([nearby[:, :3] + offsets.T[:, :, None, None], nearby[:, 3:]], 1)
        region = region.transpose(1, 0, 2, 3).reshape(6, 27 * BLOCKS, ATOMS_BLOCK)
        return brick_forces(per_brick[xpos, ypos, zpos], region, tile_list[xpos, ypos, zpos])
    result = lax.map(one_brick, jnp.arange(N_GX * N_GY * N_GZ, dtype=jnp.int32))
    result = result.reshape(N_GX, N_GY, N_GZ, 3, BLOCKS, ATOMS_BLOCK).transpose(3, 0, 4, 1, 2, 5)
    return result.reshape(3, N_GX, BLOCKS * N_GY * N_GZ, ATOMS_BLOCK)
```

```python
import math

import jax
import jax.numpy as jnp
import numpy as np
from jax import lax
from jax.experimental import pallas as pl
from jax.experimental.pallas import tpu as pltpu
from jax.sharding import PartitionSpec as P

F32 = jnp.float32
BF16 = jnp.bfloat16

GRID = 4
LAYERS = 8
CELL = 11.0
LIMIT = 97.0
COULOMB = 332.0636

ROW_X, ROW_Y, ROW_Z, ROW_C, ROW_TYPE, ROW_Q, ROW_ONE, ROW_CC = range(8)
TYPES = 64
ORDER = 13
NX = 32
NY = 48
NZ = TYPES + 32
BATCH = 4


def placements():
    home = np.zeros((32, NX), np.float32)
    src_w = np.zeros((NX, 32), np.float32)
    src_c = np.zeros((NX, 32), np.float32)
    at = 0

    def term(row, part):
        return part * 8 + row

    for row in (ROW_X, ROW_Y, ROW_Z):
        for i, j in ((0, 0), (0, 1), (1, 0), (1, 1), (0, 2), (2, 0)):
            home[term(row, i), at] = 1.0
            src_w[at, term(row, j)] = -2.0
            at += 1
    for part in range(3):
        home[term(ROW_Q, part), at] = 1.0
        src_w[at, term(ROW_ONE, 0)] = 1.0
        at += 1
    for part in range(3):
        home[term(ROW_ONE, 0), at] = 1.0
        src_w[at, term(ROW_Q, part)] = 1.0
        at += 1
    home[term(ROW_ONE, 0), at] = 1.0
    src_w[at, term(ROW_ONE, 0)] = 16.0
    at += 1
    for i, j in ((0, 0), (0, 1), (1, 0), (1, 1), (0, 2), (2, 0)):
        home[term(ROW_CC, i), at] = 1.0
        src_c[at, term(ROW_C, j)] = 1.0
        at += 1
    place_r = np.zeros((16, 32), np.float32)
    for k, row in enumerate((ROW_X, ROW_Y, ROW_Z)):
        for part in range(3):
            place_r[3 * k + part, term(row, part)] = 1.0
    place_r[9, term(ROW_ONE, 0)] = 1.0
    return home, src_w, src_c, place_r


def weights(lj_sigma, lj_epsilon):
    root = jnp.sqrt(lj_epsilon)
    half = 0.5 * lj_sigma
    powers = [jnp.ones_like(half)]
    for _ in range(ORDER - 1):
        powers.append(powers[-1] * half)

    def halves(table):
        high = lax.reduce_precision(table, 8, 7)
        return high, table - high

    h_high, h_low = halves(jnp.stack([root * p for p in powers]))
    zero = jnp.zeros_like(half)
    p12 = jnp.stack([root * powers[12 - k] * (48.0 * math.comb(12, k)) for k in range(ORDER)])
    p6 = jnp.stack(
        [root * powers[6 - k] * (24.0 * math.comb(6, k)) if k <= 6 else zero for k in range(ORDER)]
    )
    pad = jnp.zeros((NY - 3 * ORDER, TYPES), F32)
    home_y = jnp.concatenate([h_high, h_high, h_low, pad])
    src_y = []
    for table in (p12, p6):
        high, low = halves(table)
        src_y += [high, low, high, pad]
    home_x, src_w, src_c, place_r = placements()
    home = jnp.zeros((NZ, 256), F32)
    home = home.at[TYPES:, :NX].set(home_x).at[:TYPES, 128 : 128 + NY].set(home_y.T)
    fixed = jnp.concatenate([jnp.zeros((2 * NX + 16, TYPES)), np.concatenate([src_w, src_c, place_r])], 1)
    lj = jnp.concatenate([jnp.concatenate(src_y), jnp.zeros((2 * NY, 32), F32)], 1)
    source = jnp.concatenate([fixed, lj])
    return home.astype(BF16), source.astype(BF16)


def unpack_kernel(arrived, out):
    row = lax.broadcasted_iota(jnp.int32, (8, 128), 0)

    def body(s, carry):
        rows = arrived[s]
        cell_x, cell_y, cell_z = s // 8, s // 2 % 4, s % 2 * 4
        for k in range(4):
            block = jnp.concatenate([rows[5 * k : 5 * k + 5], jnp.zeros((3, 128), F32)])
            off_x = cell_x.astype(F32) * CELL - 2 * CELL
            off_y = cell_y.astype(F32) * CELL - 2 * CELL
            off_z = (cell_z + k).astype(F32) * CELL - 4 * CELL
            off = jnp.where(row == ROW_X, off_x, 0.0) + jnp.where(row == ROW_Y, off_y, 0.0)
            out[4 * s + k] = block + (off + jnp.where(row == ROW_Z, off_z, 0.0))
        return carry

    lax.fori_loop(0, 32, body, 0)


def powers_of(w):
    u = lax.rsqrt(w)
    inv = u * u
    inv2 = inv * inv
    inv4 = inv2 * inv2
    return inv4 * (inv2 * inv), inv4, u * inv


def pair_kernel(steps, ids, own, region, w_home, w_src, out, lx, ly, rx, ry, rr, acc, buf_a, buf_b):
    row = lax.broadcasted_iota(jnp.int32, (8, 128), 0)
    kind = lax.broadcasted_iota(jnp.int32, (TYPES, 128), 0)

    def factors(block, off_x, off_y, off_z):
        off = jnp.where(row == ROW_X, off_x, 0.0) + jnp.where(row == ROW_Y, off_y, 0.0)
        moved = block + (off + jnp.where(row == ROW_Z, off_z, 0.0))
        square = jnp.sum(jnp.where(row < 3, moved * moved, 0.0), axis=0, keepdims=True)
        moved = jnp.where(row == ROW_Q, square, jnp.where(row == ROW_ONE, 1.0, moved))
        moved = jnp.where(row == ROW_CC, COULOMB * block[ROW_C : ROW_C + 1], moved)
        high = moved.astype(BF16).astype(F32)
        rest = moved - high
        mid = rest.astype(BF16).astype(F32)
        hot = jnp.where(block[ROW_TYPE : ROW_TYPE + 1].astype(jnp.int32) == kind, 1.0, 0.0)
        return jnp.concatenate([hot, high, mid, rest - mid, jnp.zeros((8, 128), F32)]).astype(BF16)

    def prepare_source(p, carry):
        px, py, pz = p // 60, p // 10 % 6, p % 10

        def off(at, length, span):
            side = (at == length + 1).astype(F32) - (at == 0).astype(F32)
            return side * span

        z = factors(region[p], off(px, 4, 44.0), off(py, 4, 44.0), off(pz, 8, 88.0))
        made = jnp.dot(w_src[...], z, preferred_element_type=F32).astype(BF16)
        rx[p, :, :128] = made[:NX]
        rx[p, :, 128:] = made[NX : 2 * NX]
        rr[p, :, :128] = made[2 * NX : 2 * NX + 16]
        rr[p, :, 128:] = made[2 * NX : 2 * NX + 16]
        at = 2 * NX + 16
        ry[p, :, :128] = made[at : at + NY]
        ry[p, :, 128:] = made[at + NY :]
        return carry

    def prepare_home(b, carry):
        z = factors(own[b], 0.0, 0.0, 0.0)
        made = lax.dot_general(z, w_home[...], (((0,), (0,)), ((), ())), preferred_element_type=F32)
        lx[b] = made[:, :128].astype(BF16)
        ly[b] = made[:, 128:].astype(BF16)
        return carry

    lax.fori_loop(0, 360, prepare_source, 0, unroll=4)
    lax.fori_loop(0, 128, prepare_home, 0, unroll=4)
    acc[...] = jnp.zeros_like(acc)
    k7, k4, k3 = powers_of(jnp.full((8, 128), LIMIT, F32))

    def quantities(buf, batch):
        for q in range(BATCH):
            h, j = ids[0, batch * BATCH + q], ids[1, batch * BATCH + q]
            buf[q, 0] = jnp.dot(lx[h][:, :NX], rx[j], preferred_element_type=F32)
            buf[q, 1] = jnp.dot(ly[h][:, :NY], ry[j], preferred_element_type=F32)

    def forces(buf, batch):
        for q in range(BATCH):
            j, h = ids[1, batch * BATCH + q], ids[2, batch * BATCH + q]

            def part(i, side):
                return buf[q, i, :, 128 * side : 128 * side + 128].reshape(16, 8, 128)

            p7, p4, p3 = powers_of(jnp.minimum(part(0, 0), LIMIT))
            push = (p7 - k7) * part(1, 0) - (p4 - k4) * part(1, 1) + (p3 - k3) * part(0, 1)
            push = push.reshape(128, 128)
            high = push.astype(BF16)
            low = (push - high.astype(F32)).astype(BF16)
            acc[h] += lax.dot_general(
                rr[j],
                jnp.concatenate([high, low], 1),
                (((1,), (1,)), ((), ())),
                preferred_element_type=F32,
            )

    pairs = steps[0]
    quantities(buf_a, 0)

    def body(i, carry):
        quantities(buf_b, 2 * i + 1)
        forces(buf_a, 2 * i)
        quantities(buf_a, jnp.minimum(2 * i + 2, 2 * pairs - 1))
        forces(buf_b, 2 * i + 1)
        return carry

    lax.fori_loop(0, pairs, body, 0)
    total = acc[:128, 9]
    for c in range(3):
        weighed = acc[:128, 3 * c] + acc[:128, 3 * c + 1] + acc[:128, 3 * c + 2]
        out[c] = own[:, c] * total - weighed


def extended(block, sides):
    for axis, dim in sides:
        count = lax.axis_size(axis)
        forward = [(i, (i + 1) % count) for i in range(count)]
        backward = [(target, source) for source, target in forward]
        low = lax.ppermute(
            lax.slice_in_dim(block, block.shape[dim] - 1, None, axis=dim), axis, forward
        )
        high = lax.ppermute(lax.slice_in_dim(block, 0, 1, axis=dim), axis, backward)
        block = jnp.concatenate([low, block, high], axis=dim)
    return block


def per_device(coords, charges, atom_types, lj_sigma, lj_epsilon, tile_list):
    blocks, width = coords.shape[2], coords.shape[3]
    peers = lax.axis_size("gy") * lax.axis_size("gz")
    rows = jnp.concatenate([coords[:, 0], charges, atom_types.astype(F32)], 0)
    outgoing = rows.reshape(5, 4, peers, width).transpose(2, 1, 0, 3).reshape(peers, 20, width)
    arrived = lax.all_to_all(outgoing, ("gy", "gz"), split_axis=0, concat_axis=0, tiled=True)
    own = pl.pallas_call(
        unpack_kernel,
        out_shape=jax.ShapeDtypeStruct((blocks, 8, width), F32),
    )(arrived)
    region = extended(
        own.reshape(GRID, GRID, LAYERS, 8, width), (("gx", 0), ("gy", 1), ("gz", 2))
    ).reshape(360, 8, width)

    home, source = tile_list[0, 0, 0, 0], tile_list[0, 0, 0, 1]
    slot, member = source // blocks, source % blocks
    place_x = member // (GRID * LAYERS) + (slot // 9 - 1) * GRID + 1
    place_y = member // LAYERS % GRID + (slot // 3 % 3 - 1) * GRID + 1
    place_z = member % LAYERS + (slot % 3 - 1) * LAYERS + 1
    place = (place_x * (GRID + 2) + place_y) * (LAYERS + 2) + place_z
    listed = home >= 0
    ids = jnp.stack(
        [jnp.maximum(home, 0), jnp.where(listed, place, 0), jnp.where(listed, home, blocks)]
    )
    count = jnp.sum(listed.astype(jnp.int32))
    steps = ((count + 2 * BATCH - 1) // (2 * BATCH)).reshape(1)
    w_home, w_src = weights(lj_sigma, lj_epsilon)

    vmem = pl.BlockSpec(memory_space=pltpu.VMEM)
    smem = pl.BlockSpec(memory_space=pltpu.SMEM)
    totals = pl.pallas_call(
        pair_kernel,
        out_shape=jax.ShapeDtypeStruct((3, blocks, width), F32),
        in_specs=[smem, smem, vmem, vmem, vmem, vmem],
        out_specs=vmem,
        scratch_shapes=[
            pltpu.VMEM((blocks, 128, 128), BF16),
            pltpu.VMEM((blocks, 128, 128), BF16),
            pltpu.VMEM((360, NX, 256), BF16),
            pltpu.VMEM((360, NY, 256), BF16),
            pltpu.VMEM((360, 16, 256), BF16),
            pltpu.VMEM((blocks + 8, 16, 128), F32),
            pltpu.VMEM((BATCH, 2, 128, 256), F32),
            pltpu.VMEM((BATCH, 2, 128, 256), F32),
        ],
        compiler_params=pltpu.CompilerParams(vmem_limit_bytes=48 << 20),
    )(steps, ids, own, region, w_home, w_src)
    sending = totals.reshape(3, peers, 4, width).transpose(1, 0, 2, 3).reshape(peers, 12, width)
    back = lax.all_to_all(sending, ("gy", "gz"), split_axis=0, concat_axis=0, tiled=True)
    return back.reshape(peers, 3, 4, width).transpose(1, 2, 0, 3).reshape(3, 1, blocks, width)


def solution(mesh):
    return jax.shard_map(
        per_device,
        mesh=mesh,
        in_specs=(
            P(None, "gx", ("gy", "gz"), None),
            P("gx", ("gy", "gz"), None),
            P("gx", ("gy", "gz"), None),
            P(),
            P(),
            P("gx", "gy", "gz", None, None),
        ),
        out_specs=P(None, "gx", ("gy", "gz"), None),
        check_vma=False,
    )
```

```python
import math

import jax
import jax.numpy as jnp
import numpy as np
from jax import lax
from jax.experimental import pallas as pl
from jax.experimental.pallas import tpu as pltpu
from jax.sharding import PartitionSpec as P

F32 = jnp.float32
BF16 = jnp.bfloat16

GRID = 4
LAYERS = 8
CELL = 11.0
LIMIT = 97.0
COULOMB = 332.0636

ROW_X, ROW_Y, ROW_Z, ROW_C, ROW_TYPE, ROW_Q, ROW_ONE, ROW_CC = range(8)
TYPES = 64
ORDER = 13
NX = 32
NY = 48
NZ = TYPES + 32
BATCH = 4
NEAR = 240
SENT = 56


def placements():
    home = np.zeros((32, NX), np.float32)
    src_w = np.zeros((NX, 32), np.float32)
    src_c = np.zeros((NX, 32), np.float32)
    at = 0

    def term(row, part):
        return part * 8 + row

    for row in (ROW_X, ROW_Y, ROW_Z):
        for i, j in ((0, 0), (0, 1), (1, 0), (1, 1), (0, 2), (2, 0)):
            home[term(row, i), at] = 1.0
            src_w[at, term(row, j)] = -2.0
            at += 1
    for part in range(3):
        home[term(ROW_Q, part), at] = 1.0
        src_w[at, term(ROW_ONE, 0)] = 1.0
        at += 1
    for part in range(3):
        home[term(ROW_ONE, 0), at] = 1.0
        src_w[at, term(ROW_Q, part)] = 1.0
        at += 1
    home[term(ROW_ONE, 0), at] = 1.0
    src_w[at, term(ROW_ONE, 0)] = 16.0
    at += 1
    for i, j in ((0, 0), (0, 1), (1, 0), (1, 1), (0, 2), (2, 0)):
        home[term(ROW_CC, i), at] = 1.0
        src_c[at, term(ROW_C, j)] = 1.0
        at += 1
    place_r = np.zeros((16, 32), np.float32)
    for k, row in enumerate((ROW_X, ROW_Y, ROW_Z)):
        for part in range(3):
            place_r[3 * k + part, term(row, part)] = 1.0
    place_r[9, term(ROW_ONE, 0)] = 1.0
    return home, src_w, src_c, place_r


def weights(lj_sigma, lj_epsilon):
    root = jnp.sqrt(lj_epsilon)
    half = 0.5 * lj_sigma
    powers = [jnp.ones_like(half)]
    for _ in range(ORDER - 1):
        powers.append(powers[-1] * half)

    def halves(table):
        high = lax.reduce_precision(table, 8, 7)
        return high, table - high

    h_high, h_low = halves(jnp.stack([root * p for p in powers]))
    zero = jnp.zeros_like(half)
    p12 = jnp.stack([root * powers[12 - k] * (48.0 * math.comb(12, k)) for k in range(ORDER)])
    p6 = jnp.stack(
        [root * powers[6 - k] * (24.0 * math.comb(6, k)) if k <= 6 else zero for k in range(ORDER)]
    )
    pad = jnp.zeros((NY - 3 * ORDER, TYPES), F32)
    home_y = jnp.concatenate([h_high, h_high, h_low, pad])
    src_y = []
    for table in (p12, p6):
        high, low = halves(table)
        src_y += [high, low, high, pad]
    home_x, src_w, src_c, place_r = placements()
    home_x = np.pad(home_x, ((TYPES, 0), (0, 128 - NX)))
    home = jnp.concatenate([home_x, jnp.pad(home_y.T, ((0, NZ - TYPES), (0, 128 - NY)))], 1)
    fixed = jnp.concatenate([jnp.zeros((2 * NX + 16, TYPES)), np.concatenate([src_w, src_c, place_r])], 1)
    lj = jnp.concatenate([jnp.concatenate(src_y), jnp.zeros((2 * NY, 32), F32)], 1)
    source = jnp.concatenate([fixed, lj])
    return home.astype(BF16), source.astype(BF16)


def pack_kernel(half_hi, side, coords, charges, types, out):
    upper = half_hi[0] == 1
    back_y = side[0] == 3
    kinds = types[...].astype(F32)

    def next_y(value):
        ahead = jnp.concatenate([value[8:], value[:8]])
        behind = jnp.concatenate([value[24:], value[:24]])
        return jnp.where(back_y, behind, ahead)

    for q in range(5):
        for cell in range(5):

            def rows(k):
                if q < 3:
                    return coords[q, 32 * k : 32 * k + 32]
                return charges[32 * k : 32 * k + 32] if q == 3 else kinds[32 * k : 32 * k + 32]

            if cell < 4:
                value = rows(cell)
            else:
                ahead = pltpu.roll(rows(0).reshape(4, 8, 128), 7, 1)
                behind = pltpu.roll(rows(3).reshape(4, 8, 128), 1, 1)
                value = jnp.where(upper, behind, ahead).reshape(32, 128)
            out[pl.ds(5 * cell + q, 32, stride=SENT), :] = value
            out[pl.ds(25 + 5 * cell + q, 32, stride=SENT), :] = next_y(value)


def unpack_kernel(arrived, out):
    row = lax.broadcasted_iota(jnp.int32, (8, 128), 0)

    def body(s, carry):
        cell_x, cell_y, upper = s // 8, s // 2 % 4, s % 2
        for c in range(10):
            place_y = cell_y + 1
            if c >= 5:
                place_y = jnp.where(cell_y == 0, GRID + 1, 0)
            place_z = upper * 4 + c % 5 + 1 if c % 5 < 4 else jnp.where(upper == 1, 0, LAYERS + 1)
            place = (cell_x * (GRID + 2) + place_y) * (LAYERS + 2) + place_z
            if c >= 5:
                inner = jnp.logical_and(cell_y > 0, cell_y < GRID - 1)
                place = jnp.where(inner, NEAR, place)
            block = jnp.concatenate([arrived[s, 5 * c : 5 * c + 5], jnp.zeros((3, 128), F32)])
            off_x = cell_x.astype(F32) * CELL - 2 * CELL
            off_y = place_y.astype(F32) * CELL - 3 * CELL
            off_z = place_z.astype(F32) * CELL - 5 * CELL
            off = jnp.where(row == ROW_X, off_x, 0.0) + jnp.where(row == ROW_Y, off_y, 0.0)
            out[place] = block + (off + jnp.where(row == ROW_Z, off_z, 0.0))
        return carry

    lax.fori_loop(0, 32, body, 0, unroll=2)


def powers_of(w):
    u = lax.rsqrt(w)
    inv = u * u
    inv2 = inv * inv
    inv4 = inv2 * inv2
    return inv4 * (inv2 * inv), inv4, u * inv


def factors(block, off_x=None):
    row = lax.broadcasted_iota(jnp.int32, (8, 128), 0)
    kind = lax.broadcasted_iota(jnp.int32, (TYPES, 128), 0)
    moved = block if off_x is None else block + jnp.where(row == ROW_X, off_x, 0.0)
    square = jnp.sum(jnp.where(row < 3, moved * moved, 0.0), axis=0, keepdims=True)
    moved = jnp.where(row == ROW_Q, square, jnp.where(row == ROW_ONE, 1.0, moved))
    moved = jnp.where(row == ROW_CC, COULOMB * block[ROW_C : ROW_C + 1], moved)
    high = moved.astype(BF16).astype(F32)
    rest = moved - high
    mid = rest.astype(BF16).astype(F32)
    hot = jnp.where(block[ROW_TYPE : ROW_TYPE + 1].astype(jnp.int32) == kind, 1.0, 0.0)
    return jnp.concatenate([hot, high, mid, rest - mid, jnp.zeros((8, 128), F32)]).astype(BF16)


def store_source(p, z, w_src, rx, ry, rr):
    made = jnp.dot(w_src[...], z, preferred_element_type=F32).astype(BF16)
    rx[p, :, :128] = made[:NX]
    rx[p, :, 128:] = made[NX : 2 * NX]
    rr[p, :, :128] = made[2 * NX : 2 * NX + 16]
    rr[p, :, 128:] = made[2 * NX : 2 * NX + 16]
    at = 2 * NX + 16
    ry[p, :, :128] = made[at : at + NY]
    ry[p, :, 128:] = made[at + NY :]


def store_home(b, z, w_home, lx, ly):
    made = lax.dot_general(z, w_home[...], (((0,), (0,)), ((), ())), preferred_element_type=F32)
    lx[b] = made[:, :128].astype(BF16)
    ly[b] = made[:, 128:].astype(BF16)


def all_tiles(first, pairs, ids, lx, ly, rx, ry, rr, acc, buf_a, buf_b):
    k7, k4, k3 = powers_of(jnp.full((8, 128), LIMIT, F32))

    def quantities(buf, batch):
        for q in range(BATCH):
            h, j = ids[0, batch * BATCH + q], ids[1, batch * BATCH + q]
            buf[q, 0] = jnp.dot(lx[h][:, :NX], rx[j], preferred_element_type=F32)
            buf[q, 1] = jnp.dot(ly[h][:, :NY], ry[j], preferred_element_type=F32)

    def forces(buf, batch):
        for q in range(BATCH):
            j, h = ids[1, batch * BATCH + q], ids[2, batch * BATCH + q]

            def part(i, side):
                return buf[q, i, :, 128 * side : 128 * side + 128].reshape(16, 8, 128)

            p7, p4, p3 = powers_of(jnp.minimum(part(0, 0), LIMIT))
            push = (p7 - k7) * part(1, 0) - (p4 - k4) * part(1, 1) + (p3 - k3) * part(0, 1)
            push = push.reshape(128, 128)
            high = push.astype(BF16)
            low = (push - high.astype(F32)).astype(BF16)
            acc[h] += lax.dot_general(
                rr[j],
                jnp.concatenate([high, low], 1),
                (((1,), (1,)), ((), ())),
                preferred_element_type=F32,
            )

    @pl.when(pairs > 0)
    def _():
        last = 2 * (first + pairs) - 1
        quantities(buf_a, 2 * first)

        def body(i, carry):
            quantities(buf_b, 2 * i + 1)
            forces(buf_a, 2 * i)
            quantities(buf_a, jnp.minimum(2 * i + 2, last))
            forces(buf_b, 2 * i + 1)
            return carry

        lax.fori_loop(first, first + pairs, body, 0)


def near_place(b):
    return (b // (GRID * LAYERS) * (GRID + 2) + b // LAYERS % GRID + 1) * (LAYERS + 2) + b % LAYERS + 1


def near_kernel(steps, ids, region, w_home, w_src, acc, lx, ly, rx, ry, rr, buf_a, buf_b):
    def owned(b, carry):
        p = near_place(b)
        z = factors(region[p])
        store_source(p, z, w_src, rx, ry, rr)
        store_home(b, z, w_home, lx, ly)
        return carry

    def rim(i, carry):
        side, at = i // 28, i % 28
        place_y = jnp.where(at < 10, 0, jnp.where(at < 20, GRID + 1, 1 + (at - 20) // 2))
        place_z = jnp.where(at < 20, at % 10, (at - 20) % 2 * (LAYERS + 1))
        p = (side * (GRID + 2) + place_y) * (LAYERS + 2) + place_z
        store_source(p, factors(region[p]), w_src, rx, ry, rr)
        return carry

    lax.fori_loop(0, 128, owned, 0, unroll=8)
    lax.fori_loop(0, 112, rim, 0, unroll=8)
    acc[...] = jnp.zeros_like(acc)
    all_tiles(0, steps[0], ids, lx, ly, rx, ry, rr, acc, buf_a, buf_b)


def far_kernel(steps, ids, low, high, region, w_src, lx, ly, acc, out, acc_out, rx, ry, rr, buf_a, buf_b):
    def prepare(p, carry):
        store_source(p, factors(low[p], -44.0), w_src, rx, ry, rr)
        store_source(p + 60, factors(high[p], 44.0), w_src, rx, ry, rr)
        return carry

    lax.fori_loop(0, 60, prepare, 0, unroll=4)
    all_tiles(steps[0], steps[1], ids, lx, ly, rx, ry, rr, acc_out, buf_a, buf_b)
    for x in range(GRID):
        for y in range(GRID):
            b = (x * GRID + y) * LAYERS
            p = (x * (GRID + 2) + y + 1) * (LAYERS + 2) + 1
            total = acc_out[b : b + LAYERS, 9]
            for c in range(3):
                weighed = acc_out[b : b + LAYERS, 3 * c] + acc_out[b : b + LAYERS, 3 * c + 1]
                weighed = weighed + acc_out[b : b + LAYERS, 3 * c + 2]
                out[c, b : b + LAYERS] = region[p : p + LAYERS, c] * total - weighed


def tile_lists(tiles, blocks):
    home, source = tiles[0], tiles[1]
    slot, member = source // blocks, source % blocks
    step_x = slot // 9 - 1
    place_y = member // LAYERS % GRID + (slot // 3 % 3 - 1) * GRID + 1
    place_z = member % LAYERS + (slot % 3 - 1) * LAYERS + 1
    plane = place_y * (LAYERS + 2) + place_z
    side = jnp.where(step_x == 0, member // (GRID * LAYERS), (step_x + 1) // 2)
    listed = home >= 0
    near = listed & (step_x == 0)
    far = listed & (step_x != 0)
    unit = 2 * BATCH
    order = jnp.arange(home.shape[0])
    upto = order[None, :] <= order[:, None]
    near_at = jnp.sum(jnp.where(upto & near[None, :], 1, 0), 1)
    far_at = jnp.sum(jnp.where(upto & far[None, :], 1, 0), 1)
    near_steps = (jnp.sum(near.astype(jnp.int32)) + unit - 1) // unit
    far_steps = (jnp.sum(far.astype(jnp.int32)) + unit - 1) // unit
    at = jnp.where(near, near_at - 1, jnp.where(far, near_steps * unit + far_at - 1, -1))
    code = home * 256 + side * 60 + plane + 1
    slots = jnp.arange(home.shape[0] + 2 * unit)
    found = jnp.sum(jnp.where(slots[:, None] == at[None, :], code[None, :], 0), 1)
    real = found > 0
    code = jnp.maximum(found - 1, 0)
    ids = jnp.stack([code // 256, code % 256, jnp.where(real, code // 256, blocks)])
    return jnp.stack([near_steps, far_steps]), ids


def per_device(coords, charges, atom_types, lj_sigma, lj_epsilon, tile_list):
    blocks, width = coords.shape[2], coords.shape[3]
    peers = lax.axis_size("gy") * lax.axis_size("gz")
    vmem = pl.BlockSpec(memory_space=pltpu.VMEM)
    smem = pl.BlockSpec(memory_space=pltpu.SMEM)
    gz = lax.axis_index("gz")
    small = pltpu.CompilerParams(vmem_limit_bytes=8 << 20)
    outgoing = pl.pallas_call(
        pack_kernel,
        out_shape=jax.ShapeDtypeStruct((peers * SENT, width), F32),
        in_specs=[smem, smem, vmem, vmem, vmem],
        out_specs=vmem,
        compiler_params=small,
    )((gz % 2).reshape(1), (gz // 2).reshape(1), coords[:, 0], charges[0], atom_types[0])
    arrived = lax.all_to_all(
        outgoing.reshape(peers, SENT, width), ("gy", "gz"), split_axis=0, concat_axis=0, tiled=True
    )
    steps, ids = tile_lists(tile_list[0, 0, 0], blocks)
    w_home, w_src = weights(lj_sigma, lj_epsilon)
    region = pl.pallas_call(
        unpack_kernel,
        out_shape=jax.ShapeDtypeStruct((NEAR + 1, 8, width), F32),
        in_specs=[vmem],
        out_specs=vmem,
        compiler_params=small,
    )(arrived)
    count = lax.axis_size("gx")
    forward = [(i, (i + 1) % count) for i in range(count)]
    backward = [(target, source) for source, target in forward]
    low = lax.ppermute(region[180:240], "gx", forward)
    high = lax.ppermute(region[:60], "gx", backward)

    def source_scratch(n):
        return [
            pltpu.VMEM((n, NX, 256), BF16),
            pltpu.VMEM((n, NY, 256), BF16),
            pltpu.VMEM((n, 16, 256), BF16),
            pltpu.VMEM((BATCH, 2, 128, 256), F32),
            pltpu.VMEM((BATCH, 2, 128, 256), F32),
        ]

    acc_shape = jax.ShapeDtypeStruct((blocks + 1, 16, width), F32)
    factor_shape = jax.ShapeDtypeStruct((blocks, 128, 128), BF16)
    acc, lx, ly = pl.pallas_call(
        near_kernel,
        out_shape=[acc_shape, factor_shape, factor_shape],
        in_specs=[smem, smem, vmem, vmem, vmem],
        out_specs=[vmem] * 3,
        scratch_shapes=source_scratch(NEAR),
        compiler_params=pltpu.CompilerParams(vmem_limit_bytes=28 << 20),
        cost_estimate=pl.CostEstimate(flops=10**10, bytes_accessed=10**7, transcendentals=10**6),
    )(steps, ids, region, w_home, w_src)
    totals, _ = pl.pallas_call(
        far_kernel,
        out_shape=[jax.ShapeDtypeStruct((3, blocks, width), F32), acc_shape],
        in_specs=[smem, smem] + [vmem] * 7,
        out_specs=[vmem] * 2,
        scratch_shapes=source_scratch(120),
        input_output_aliases={8: 1},
        compiler_params=pltpu.CompilerParams(vmem_limit_bytes=24 << 20),
    )(steps, ids, low, high, region, w_src, lx, ly, acc)
    sending = totals.reshape(3, peers, 4, width).transpose(1, 0, 2, 3).reshape(peers, 12, width)
    back = lax.all_to_all(sending, ("gy", "gz"), split_axis=0, concat_axis=0, tiled=True)
    return back.reshape(peers, 3, 4, width).transpose(1, 2, 0, 3).reshape(3, 1, blocks, width)


def solution(mesh):
    return jax.shard_map(
        per_device,
        mesh=mesh,
        in_specs=(
            P(None, "gx", ("gy", "gz"), None),
            P("gx", ("gy", "gz"), None),
            P("gx", ("gy", "gz"), None),
            P(),
            P(),
            P("gx", "gy", "gz", None, None),
        ),
        out_specs=P(None, "gx", ("gy", "gz"), None),
        check_vma=False,
    )
```

```python
import math

import jax
import jax.numpy as jnp
import numpy as np
from jax import lax
from jax.experimental import pallas as pl
from jax.experimental.pallas import tpu as pltpu
from jax.sharding import PartitionSpec as P

F32 = jnp.float32
BF16 = jnp.bfloat16

GRID = 4
LAYERS = 8
CELL = 11.0
LIMIT = 97.0
COULOMB = 332.0636

ROW_X, ROW_Y, ROW_Z, ROW_C, ROW_TYPE, ROW_Q, ROW_ONE, ROW_CC = range(8)
TYPES = 64
ORDER = 13
NX = 32
NY = 48
NZ = TYPES + 32
BATCH = 4
GROUP = 8
FAR_GROUP = 10
NEAR = 240
SENT = 56


def placements():
    home = np.zeros((32, NX), np.float32)
    src_w = np.zeros((NX, 32), np.float32)
    src_c = np.zeros((NX, 32), np.float32)
    at = 0

    def term(row, part):
        return part * 8 + row

    for row in (ROW_X, ROW_Y, ROW_Z):
        for i, j in ((0, 0), (0, 1), (1, 0), (1, 1), (0, 2), (2, 0)):
            home[term(row, i), at] = 1.0
            src_w[at, term(row, j)] = -2.0
            at += 1
    for part in range(3):
        home[term(ROW_Q, part), at] = 1.0
        src_w[at, term(ROW_ONE, 0)] = 1.0
        at += 1
    for part in range(3):
        home[term(ROW_ONE, 0), at] = 1.0
        src_w[at, term(ROW_Q, part)] = 1.0
        at += 1
    home[term(ROW_ONE, 0), at] = 1.0
    src_w[at, term(ROW_ONE, 0)] = 16.0
    at += 1
    for i, j in ((0, 0), (0, 1), (1, 0), (1, 1), (0, 2), (2, 0)):
        home[term(ROW_CC, i), at] = 1.0
        src_c[at, term(ROW_C, j)] = 1.0
        at += 1
    place_r = np.zeros((16, 32), np.float32)
    for k, row in enumerate((ROW_X, ROW_Y, ROW_Z)):
        for part in range(3):
            place_r[3 * k + part, term(row, part)] = 1.0
    place_r[9, term(ROW_ONE, 0)] = 1.0
    return home, src_w, src_c, place_r


def weights(lj_sigma, lj_epsilon):
    root = jnp.sqrt(lj_epsilon)
    half = 0.5 * lj_sigma
    powers = [jnp.ones_like(half)]
    for _ in range(ORDER - 1):
        powers.append(powers[-1] * half)

    def halves(table):
        high = lax.reduce_precision(table, 8, 7)
        return high, table - high

    h_high, h_low = halves(jnp.stack([root * p for p in powers]))
    zero = jnp.zeros_like(half)
    p12 = jnp.stack([root * powers[12 - k] * (48.0 * math.comb(12, k)) for k in range(ORDER)])
    p6 = jnp.stack(
        [root * powers[6 - k] * (24.0 * math.comb(6, k)) if k <= 6 else zero for k in range(ORDER)]
    )
    pad = jnp.zeros((NY - 3 * ORDER, TYPES), F32)
    home_y = jnp.concatenate([h_high, h_high, h_low, pad])
    src_y = []
    for table in (p12, p6):
        high, low = halves(table)
        src_y += [high, low, high, pad]
    home_x, src_w, src_c, place_r = placements()
    home_x = np.pad(home_x, ((TYPES, 0), (0, 128 - NX)))
    home = jnp.concatenate([home_x, jnp.pad(home_y.T, ((0, NZ - TYPES), (0, 128 - NY)))], 1)
    fixed = jnp.concatenate([jnp.zeros((2 * NX + 16, TYPES)), np.concatenate([src_w, src_c, place_r])], 1)
    lj = jnp.concatenate([jnp.concatenate(src_y), jnp.zeros((2 * NY, 32), F32)], 1)
    source = jnp.concatenate([fixed, lj])
    return home.astype(BF16), source.astype(BF16)


def pack_kernel(half_hi, side, coords_in, charges_in, types_in, out, coords, charges, types, sems):
    copies = [
        pltpu.make_async_copy(source, target, sems.at[i])
        for i, (source, target) in enumerate(
            ((coords_in, coords), (charges_in, charges), (types_in, types))
        )
    ]
    for copy in copies:
        copy.start()
    for copy in copies:
        copy.wait()
    upper = half_hi[0] == 1
    back_y = side[0] == 3
    kinds = types[...].astype(F32)

    def next_y(value):
        ahead = jnp.concatenate([value[8:], value[:8]])
        behind = jnp.concatenate([value[24:], value[:24]])
        return jnp.where(back_y, behind, ahead)

    for q in range(5):
        for cell in range(5):

            def rows(k):
                if q < 3:
                    return coords[q, 32 * k : 32 * k + 32]
                return charges[32 * k : 32 * k + 32] if q == 3 else kinds[32 * k : 32 * k + 32]

            if cell < 4:
                value = rows(cell)
            else:
                ahead = pltpu.roll(rows(0).reshape(4, 8, 128), 7, 1)
                behind = pltpu.roll(rows(3).reshape(4, 8, 128), 1, 1)
                value = jnp.where(upper, behind, ahead).reshape(32, 128)
            out[pl.ds(5 * cell + q, 32, stride=SENT), :] = value
            out[pl.ds(25 + 5 * cell + q, 32, stride=SENT), :] = next_y(value)


def unpack_kernel(arrived, out):
    row = lax.broadcasted_iota(jnp.int32, (8, 128), 0)

    def body(s, carry):
        cell_x, cell_y, upper = s // 8, s // 2 % 4, s % 2
        for c in range(10):
            place_y = cell_y + 1
            if c >= 5:
                place_y = jnp.where(cell_y == 0, GRID + 1, 0)
            place_z = upper * 4 + c % 5 + 1 if c % 5 < 4 else jnp.where(upper == 1, 0, LAYERS + 1)
            place = (cell_x * (GRID + 2) + place_y) * (LAYERS + 2) + place_z
            if c >= 5:
                inner = jnp.logical_and(cell_y > 0, cell_y < GRID - 1)
                place = jnp.where(inner, NEAR, place)
            block = jnp.concatenate([arrived[s, 5 * c : 5 * c + 5], jnp.zeros((3, 128), F32)])
            off_x = cell_x.astype(F32) * CELL - 2 * CELL
            off_y = place_y.astype(F32) * CELL - 3 * CELL
            off_z = place_z.astype(F32) * CELL - 5 * CELL
            off = jnp.where(row == ROW_X, off_x, 0.0) + jnp.where(row == ROW_Y, off_y, 0.0)
            out[place] = block + (off + jnp.where(row == ROW_Z, off_z, 0.0))
        return carry

    lax.fori_loop(0, 32, body, 0, unroll=2)


def powers_of(w):
    u = lax.rsqrt(w)
    inv = u * u
    inv2 = inv * inv
    inv4 = inv2 * inv2
    return inv4 * (inv2 * inv), inv4, u * inv


def factors(block, off_x=None):
    row = lax.broadcasted_iota(jnp.int32, (8, 128), 0)
    kind = lax.broadcasted_iota(jnp.int32, (TYPES, 128), 0)
    moved = block if off_x is None else block + jnp.where(row == ROW_X, off_x, 0.0)
    square = jnp.sum(jnp.where(row < 3, moved * moved, 0.0), axis=0, keepdims=True)
    moved = jnp.where(row == ROW_Q, square, jnp.where(row == ROW_ONE, 1.0, moved))
    moved = jnp.where(row == ROW_CC, COULOMB * block[ROW_C : ROW_C + 1], moved)
    high = moved.astype(BF16).astype(F32)
    rest = moved - high
    mid = rest.astype(BF16).astype(F32)
    hot = jnp.where(block[ROW_TYPE : ROW_TYPE + 1].astype(jnp.int32) == kind, 1.0, 0.0)
    return jnp.concatenate([hot, high, mid, rest - mid, jnp.zeros((8, 128), F32)]).astype(BF16)


def store_source(places, z, w_src, rx, ry, rr):
    made = jnp.dot(w_src[...], z, preferred_element_type=F32).astype(BF16)
    for g, p in enumerate(places):
        own = made[:, 128 * g : 128 * g + 128]
        rx[p, :, :128] = own[:NX]
        rx[p, :, 128:] = own[NX : 2 * NX]
        rr[p, :, :128] = own[2 * NX : 2 * NX + 16]
        rr[p, :, 128:] = own[2 * NX : 2 * NX + 16]
        at = 2 * NX + 16
        ry[p, :, :128] = own[at : at + NY]
        ry[p, :, 128:] = own[at + NY :]


def store_home(first, z, w_home, lx, ly):
    made = lax.dot_general(z, w_home[...], (((0,), (0,)), ((), ())), preferred_element_type=F32)
    made = made.astype(BF16)
    for g in range(GROUP):
        own = made[128 * g : 128 * g + 128]
        lx[first + g] = own[:, :128]
        ly[first + g] = own[:, 128:]


def all_tiles(first, pairs, ids, lx, ly, rx, ry, rr, acc, buf_a, buf_b):
    k7, k4, k3 = powers_of(jnp.full((8, 128), LIMIT, F32))

    def quantities(buf, batch):
        for q in range(BATCH):
            h, j = ids[0, batch * BATCH + q], ids[1, batch * BATCH + q]
            buf[q, 0] = jnp.dot(lx[h][:, :NX], rx[j], preferred_element_type=F32)
            buf[q, 1] = jnp.dot(ly[h][:, :NY], ry[j], preferred_element_type=F32)

    def forces(buf, batch):
        for q in range(BATCH):
            j, h = ids[1, batch * BATCH + q], ids[2, batch * BATCH + q]

            def part(i, side):
                return buf[q, i, :, 128 * side : 128 * side + 128].reshape(16, 8, 128)

            p7, p4, p3 = powers_of(jnp.minimum(part(0, 0), LIMIT))
            push = (p7 - k7) * part(1, 0) - (p4 - k4) * part(1, 1) + (p3 - k3) * part(0, 1)
            push = push.reshape(128, 128)
            high = push.astype(BF16)
            low = (push - high.astype(F32)).astype(BF16)
            acc[h] += lax.dot_general(
                rr[j],
                jnp.concatenate([high, low], 1),
                (((1,), (1,)), ((), ())),
                preferred_element_type=F32,
            )

    @pl.when(pairs > 0)
    def _():
        last = 2 * (first + pairs) - 1
        quantities(buf_a, 2 * first)

        def body(i, carry):
            quantities(buf_b, 2 * i + 1)
            forces(buf_a, 2 * i)
            quantities(buf_a, jnp.minimum(2 * i + 2, last))
            forces(buf_b, 2 * i + 1)
            return carry

        lax.fori_loop(first, first + pairs, body, 0)


def near_place(b):
    return (b // (GRID * LAYERS) * (GRID + 2) + b // LAYERS % GRID + 1) * (LAYERS + 2) + b % LAYERS + 1


def near_kernel(steps, ids, region, w_home, w_src, acc, lx, ly, rx, ry, rr, buf_a, buf_b):
    def owned(i, carry):
        first = near_place(i * GROUP)
        places = [first + g for g in range(GROUP)]
        z = jnp.concatenate([factors(region[p]) for p in places], 1)
        store_source(places, z, w_src, rx, ry, rr)
        store_home(i * GROUP, z, w_home, lx, ly)
        return carry

    def rim_place(i):
        side, at = i // 28, i % 28
        place_y = jnp.where(at < 10, 0, jnp.where(at < 20, GRID + 1, 1 + (at - 20) // 2))
        place_z = jnp.where(at < 20, at % 10, (at - 20) % 2 * (LAYERS + 1))
        return (side * (GRID + 2) + place_y) * (LAYERS + 2) + place_z

    def rim(i, carry):
        places = [rim_place(i * GROUP + g) for g in range(GROUP)]
        z = jnp.concatenate([factors(region[p]) for p in places], 1)
        store_source(places, z, w_src, rx, ry, rr)
        return carry

    lax.fori_loop(0, 128 // GROUP, owned, 0, unroll=4)
    lax.fori_loop(0, 112 // GROUP, rim, 0, unroll=7)
    acc[...] = jnp.zeros_like(acc)
    all_tiles(0, steps[0], ids, lx, ly, rx, ry, rr, acc, buf_a, buf_b)


def far_kernel(steps, ids, low, high, region, w_src, lx, ly, acc, out, acc_out, rx, ry, rr, buf_a, buf_b):
    def prepare(i, carry):
        for k, (plane, off_x) in enumerate(((low, -44.0), (high, 44.0))):
            places = [i * FAR_GROUP + g for g in range(FAR_GROUP)]
            z = jnp.concatenate([factors(plane[p], off_x) for p in places], 1)
            store_source([p + 60 * k for p in places], z, w_src, rx, ry, rr)
        return carry

    lax.fori_loop(0, 60 // FAR_GROUP, prepare, 0, unroll=2)
    all_tiles(steps[0], steps[1], ids, lx, ly, rx, ry, rr, acc_out, buf_a, buf_b)
    for x in range(GRID):
        for y in range(GRID):
            b = (x * GRID + y) * LAYERS
            p = (x * (GRID + 2) + y + 1) * (LAYERS + 2) + 1
            total = acc_out[b : b + LAYERS, 9]
            for c in range(3):
                weighed = acc_out[b : b + LAYERS, 3 * c] + acc_out[b : b + LAYERS, 3 * c + 1]
                weighed = weighed + acc_out[b : b + LAYERS, 3 * c + 2]
                out[c, b : b + LAYERS] = region[p : p + LAYERS, c] * total - weighed


def tile_lists(tiles, blocks):
    home, source = tiles[0], tiles[1]
    slot, member = source // blocks, source % blocks
    step_x = slot // 9 - 1
    place_y = member // LAYERS % GRID + (slot // 3 % 3 - 1) * GRID + 1
    place_z = member % LAYERS + (slot % 3 - 1) * LAYERS + 1
    plane = place_y * (LAYERS + 2) + place_z
    side = jnp.where(step_x == 0, member // (GRID * LAYERS), (step_x + 1) // 2)
    listed = home >= 0
    near = listed & (step_x == 0)
    far = listed & (step_x != 0)
    unit = 2 * BATCH
    order = jnp.arange(home.shape[0])
    upto = order[None, :] <= order[:, None]
    near_at = jnp.sum(jnp.where(upto & near[None, :], 1, 0), 1)
    far_at = jnp.sum(jnp.where(upto & far[None, :], 1, 0), 1)
    near_steps = (jnp.sum(near.astype(jnp.int32)) + unit - 1) // unit
    far_steps = (jnp.sum(far.astype(jnp.int32)) + unit - 1) // unit
    at = jnp.where(near, near_at - 1, jnp.where(far, near_steps * unit + far_at - 1, -1))
    code = home * 256 + side * 60 + plane + 1
    slots = jnp.arange(home.shape[0] + 2 * unit)
    found = jnp.sum(jnp.where(slots[:, None] == at[None, :], code[None, :], 0), 1)
    real = found > 0
    code = jnp.maximum(found - 1, 0)
    ids = jnp.stack([code // 256, code % 256, jnp.where(real, code // 256, blocks)])
    return jnp.stack([near_steps, far_steps]), ids


def per_device(coords, charges, atom_types, lj_sigma, lj_epsilon, tile_list):
    blocks, width = coords.shape[2], coords.shape[3]
    peers = lax.axis_size("gy") * lax.axis_size("gz")
    vmem = pl.BlockSpec(memory_space=pltpu.VMEM)
    smem = pl.BlockSpec(memory_space=pltpu.SMEM)
    gz = lax.axis_index("gz")
    small = pltpu.CompilerParams(vmem_limit_bytes=8 << 20)
    outgoing = pl.pallas_call(
        pack_kernel,
        out_shape=jax.ShapeDtypeStruct((peers * SENT, width), F32),
        in_specs=[smem, smem] + [pl.BlockSpec(memory_space=pl.ANY)] * 3,
        out_specs=vmem,
        scratch_shapes=[
            pltpu.VMEM((3, blocks, width), F32),
            pltpu.VMEM((blocks, width), F32),
            pltpu.VMEM((blocks, width), jnp.int32),
            pltpu.SemaphoreType.DMA((3,)),
        ],
        compiler_params=pltpu.CompilerParams(vmem_limit_bytes=65011712),
    )((gz % 2).reshape(1), (gz // 2).reshape(1), coords[:, 0], charges[0], atom_types[0])
    arrived = lax.all_to_all(
        outgoing.reshape(peers, SENT, width), ("gy", "gz"), split_axis=0, concat_axis=0, tiled=True
    )
    steps, ids = tile_lists(tile_list[0, 0, 0], blocks)
    w_home, w_src = weights(lj_sigma, lj_epsilon)
    region = pl.pallas_call(
        unpack_kernel,
        out_shape=jax.ShapeDtypeStruct((NEAR + 1, 8, width), F32),
        in_specs=[vmem],
        out_specs=vmem,
        compiler_params=small,
    )(arrived)
    count = lax.axis_size("gx")
    forward = [(i, (i + 1) % count) for i in range(count)]
    backward = [(target, source) for source, target in forward]
    low = lax.ppermute(region[180:240], "gx", forward)
    high = lax.ppermute(region[:60], "gx", backward)

    def source_scratch(n):
        return [
            pltpu.VMEM((n, NX, 256), BF16),
            pltpu.VMEM((n, NY, 256), BF16),
            pltpu.VMEM((n, 16, 256), BF16),
            pltpu.VMEM((BATCH, 2, 128, 256), F32),
            pltpu.VMEM((BATCH, 2, 128, 256), F32),
        ]

    acc_shape = jax.ShapeDtypeStruct((blocks + 1, 16, width), F32)
    factor_shape = jax.ShapeDtypeStruct((blocks, 128, 128), BF16)
    acc, lx, ly = pl.pallas_call(
        near_kernel,
        out_shape=[acc_shape, factor_shape, factor_shape],
        in_specs=[smem, smem, vmem, vmem, vmem],
        out_specs=[vmem] * 3,
        scratch_shapes=source_scratch(NEAR),
        compiler_params=pltpu.CompilerParams(vmem_limit_bytes=28 << 20),
        cost_estimate=pl.CostEstimate(flops=10**10, bytes_accessed=10**7, transcendentals=10**6),
    )(steps, ids, region, w_home, w_src)
    totals, _ = pl.pallas_call(
        far_kernel,
        out_shape=[jax.ShapeDtypeStruct((3, blocks, width), F32), acc_shape],
        in_specs=[smem, smem] + [vmem] * 7,
        out_specs=[vmem] * 2,
        scratch_shapes=source_scratch(120),
        input_output_aliases={8: 1},
        compiler_params=pltpu.CompilerParams(vmem_limit_bytes=24 << 20),
    )(steps, ids, low, high, region, w_src, lx, ly, acc)
    sending = totals.reshape(3, peers, 4, width).transpose(1, 0, 2, 3).reshape(peers, 12, width)
    back = lax.all_to_all(sending, ("gy", "gz"), split_axis=0, concat_axis=0, tiled=True)
    return back.reshape(peers, 3, 4, width).transpose(1, 2, 0, 3).reshape(3, 1, blocks, width)


def solution(mesh):
    return jax.shard_map(
        per_device,
        mesh=mesh,
        in_specs=(
            P(None, "gx", ("gy", "gz"), None),
            P("gx", ("gy", "gz"), None),
            P("gx", ("gy", "gz"), None),
            P(),
            P(),
            P("gx", "gy", "gz", None, None),
        ),
        out_specs=P(None, "gx", ("gy", "gz"), None),
        check_vma=False,
    )
```

```python
import math

import jax
import jax.numpy as jnp
import numpy as np
from jax import lax
from jax.experimental import pallas as pl
from jax.experimental.pallas import tpu as pltpu
from jax.sharding import PartitionSpec as P

F32 = jnp.float32
BF16 = jnp.bfloat16

GRID = 4
LAYERS = 8
CELL = 11.0
LIMIT = 97.0
COULOMB = 332.0636

ROW_X, ROW_Y, ROW_Z, ROW_C, ROW_TYPE, ROW_Q, ROW_ONE, ROW_CC = range(8)
TYPES = 64
ORDER = 13
NX = 32
NY = 48
NZ = TYPES + 32
BATCH = 4
GROUP = 8
FAR_GROUP = 10
NEAR = 240
SENT = 56


def placements():
    home = np.zeros((32, NX), np.float32)
    src_w = np.zeros((NX, 32), np.float32)
    src_c = np.zeros((NX, 32), np.float32)
    at = 0

    def term(row, part):
        return part * 8 + row

    for row in (ROW_X, ROW_Y, ROW_Z):
        for i, j in ((0, 0), (0, 1), (1, 0), (1, 1), (0, 2), (2, 0)):
            home[term(row, i), at] = 1.0
            src_w[at, term(row, j)] = -2.0
            at += 1
    for part in range(3):
        home[term(ROW_Q, part), at] = 1.0
        src_w[at, term(ROW_ONE, 0)] = 1.0
        at += 1
    for part in range(3):
        home[term(ROW_ONE, 0), at] = 1.0
        src_w[at, term(ROW_Q, part)] = 1.0
        at += 1
    home[term(ROW_ONE, 0), at] = 1.0
    src_w[at, term(ROW_ONE, 0)] = 16.0
    at += 1
    for i, j in ((0, 0), (0, 1), (1, 0), (1, 1), (0, 2), (2, 0)):
        home[term(ROW_CC, i), at] = 1.0
        src_c[at, term(ROW_C, j)] = 1.0
        at += 1
    place_r = np.zeros((16, 32), np.float32)
    for k, row in enumerate((ROW_X, ROW_Y, ROW_Z)):
        for part in range(3):
            place_r[4 * part + k, term(row, part)] = 1.0
    place_r[3, term(ROW_ONE, 0)] = 1.0
    return home, src_w, src_c, place_r


def weights(lj_sigma, lj_epsilon):
    root = jnp.sqrt(lj_epsilon)
    half = 0.5 * lj_sigma
    powers = [jnp.ones_like(half)]
    for _ in range(ORDER - 1):
        powers.append(powers[-1] * half)

    def halves(table):
        high = lax.reduce_precision(table, 8, 7)
        return high, table - high

    h_high, h_low = halves(jnp.stack([root * p for p in powers]))
    zero = jnp.zeros_like(half)
    p12 = jnp.stack([root * powers[12 - k] * (48.0 * math.comb(12, k)) for k in range(ORDER)])
    p6 = jnp.stack(
        [root * powers[6 - k] * (24.0 * math.comb(6, k)) if k <= 6 else zero for k in range(ORDER)]
    )
    pad = jnp.zeros((NY - 3 * ORDER, TYPES), F32)
    home_y = jnp.concatenate([h_high, h_high, h_low, pad])
    src_y = []
    for table in (p12, p6):
        high, low = halves(table)
        src_y += [high, low, high, pad]
    home_x, src_w, src_c, place_r = placements()
    home_x = np.pad(home_x, ((TYPES, 0), (0, 128 - NX)))
    home = jnp.concatenate([home_x, jnp.pad(home_y.T, ((0, NZ - TYPES), (0, 128 - NY)))], 1)
    fixed = jnp.concatenate([jnp.zeros((2 * NX + 16, TYPES)), np.concatenate([src_w, src_c, place_r])], 1)
    lj = jnp.concatenate([jnp.concatenate(src_y), jnp.zeros((2 * NY, 32), F32)], 1)
    source = jnp.concatenate([fixed, lj])
    return home.astype(BF16), source.astype(BF16)


def pack_kernel(half_hi, side, coords_in, charges_in, types_in, out, coords, charges, types, sems):
    copies = [
        pltpu.make_async_copy(source, target, sems.at[i])
        for i, (source, target) in enumerate(
            ((coords_in, coords), (charges_in, charges), (types_in, types))
        )
    ]
    for copy in copies:
        copy.start()
    for copy in copies:
        copy.wait()
    upper = half_hi[0] == 1
    back_y = side[0] == 3
    kinds = types[...].astype(F32)

    def next_y(value):
        ahead = jnp.concatenate([value[8:], value[:8]])
        behind = jnp.concatenate([value[24:], value[:24]])
        return jnp.where(back_y, behind, ahead)

    for q in range(5):
        for cell in range(5):

            def rows(k):
                if q < 3:
                    return coords[q, 32 * k : 32 * k + 32]
                return charges[32 * k : 32 * k + 32] if q == 3 else kinds[32 * k : 32 * k + 32]

            if cell < 4:
                value = rows(cell)
            else:
                ahead = pltpu.roll(rows(0).reshape(4, 8, 128), 7, 1)
                behind = pltpu.roll(rows(3).reshape(4, 8, 128), 1, 1)
                value = jnp.where(upper, behind, ahead).reshape(32, 128)
            out[pl.ds(5 * cell + q, 32, stride=SENT), :] = value
            out[pl.ds(25 + 5 * cell + q, 32, stride=SENT), :] = next_y(value)


def unpack_kernel(arrived, out):
    row = lax.broadcasted_iota(jnp.int32, (8, 128), 0)

    def body(s, carry):
        cell_x, cell_y, upper = s // 8, s // 2 % 4, s % 2
        for c in range(10):
            place_y = cell_y + 1
            if c >= 5:
                place_y = jnp.where(cell_y == 0, GRID + 1, 0)
            place_z = upper * 4 + c % 5 + 1 if c % 5 < 4 else jnp.where(upper == 1, 0, LAYERS + 1)
            place = (cell_x * (GRID + 2) + place_y) * (LAYERS + 2) + place_z
            if c >= 5:
                inner = jnp.logical_and(cell_y > 0, cell_y < GRID - 1)
                place = jnp.where(inner, NEAR, place)
            block = jnp.concatenate([arrived[s, 5 * c : 5 * c + 5], jnp.zeros((3, 128), F32)])
            off_x = cell_x.astype(F32) * CELL - 2 * CELL
            off_y = place_y.astype(F32) * CELL - 3 * CELL
            off_z = place_z.astype(F32) * CELL - 5 * CELL
            off = jnp.where(row == ROW_X, off_x, 0.0) + jnp.where(row == ROW_Y, off_y, 0.0)
            out[place] = block + (off + jnp.where(row == ROW_Z, off_z, 0.0))
        return carry

    lax.fori_loop(0, 32, body, 0, unroll=2)


def powers_of(w):
    u = lax.rsqrt(w)
    inv = u * u
    inv2 = inv * inv
    inv4 = inv2 * inv2
    return inv4 * (inv2 * inv), inv4, u * inv


def factors(block, off_x=None):
    row = lax.broadcasted_iota(jnp.int32, (8, 128), 0)
    kind = lax.broadcasted_iota(jnp.int32, (TYPES, 128), 0)
    moved = block if off_x is None else block + jnp.where(row == ROW_X, off_x, 0.0)
    square = jnp.sum(jnp.where(row < 3, moved * moved, 0.0), axis=0, keepdims=True)
    moved = jnp.where(row == ROW_Q, square, jnp.where(row == ROW_ONE, 1.0, moved))
    moved = jnp.where(row == ROW_CC, COULOMB * block[ROW_C : ROW_C + 1], moved)
    high = moved.astype(BF16).astype(F32)
    rest = moved - high
    mid = rest.astype(BF16).astype(F32)
    hot = jnp.where(block[ROW_TYPE : ROW_TYPE + 1].astype(jnp.int32) == kind, 1.0, 0.0)
    return jnp.concatenate([hot, high, mid, rest - mid, jnp.zeros((8, 128), F32)]).astype(BF16)


def store_source(places, z, w_src, rx, ry, rr):
    made = jnp.dot(w_src[...], z, preferred_element_type=F32).astype(BF16)
    for g, p in enumerate(places):
        own = made[:, 128 * g : 128 * g + 128]
        rx[p, :, :128] = own[:NX]
        rx[p, :, 128:] = own[NX : 2 * NX]
        rr[p, :, :128] = own[2 * NX : 2 * NX + 16]
        rr[p, :, 128:] = own[2 * NX : 2 * NX + 16]
        at = 2 * NX + 16
        ry[p, :, :128] = own[at : at + NY]
        ry[p, :, 128:] = own[at + NY :]


def store_home(first, z, w_home, lx, ly):
    made = lax.dot_general(z, w_home[...], (((0,), (0,)), ((), ())), preferred_element_type=F32)
    made = made.astype(BF16)
    for g in range(GROUP):
        own = made[128 * g : 128 * g + 128]
        lx[first + g] = own[:, :128]
        ly[first + g] = own[:, 128:]


def all_tiles(first, pairs, ids, lx, ly, rx, ry, rr, acc, buf_a, buf_b):
    k7, k4, k3 = powers_of(jnp.full((8, 128), LIMIT, F32))

    def quantities(buf, batch, q):
        h, j = ids[0, batch * BATCH + q], ids[1, batch * BATCH + q]
        buf[q, 0] = jnp.dot(lx[h][:, :NX], rx[j], preferred_element_type=F32)
        buf[q, 1] = jnp.dot(ly[h][:, :NY], ry[j], preferred_element_type=F32)

    def forces(buf, batch, q):
        j, h = ids[1, batch * BATCH + q], ids[2, batch * BATCH + q]

        def part(i, side):
            return buf[q, i, :, 128 * side : 128 * side + 128].reshape(16, 8, 128)

        p7, p4, p3 = powers_of(jnp.minimum(part(0, 0), LIMIT))
        push = (p7 - k7) * part(1, 0) - (p4 - k4) * part(1, 1) + (p3 - k3) * part(0, 1)
        push = push.reshape(128, 128)
        high = push.astype(BF16)
        low = (push - high.astype(F32)).astype(BF16)
        acc[h] += lax.dot_general(
            rr[j],
            jnp.concatenate([high, low], 1),
            (((1,), (1,)), ((), ())),
            preferred_element_type=F32,
        )

    def both(buf_next, buf_now, batch_next, batch_now):
        for q in range(BATCH):
            quantities(buf_next, batch_next, q)
            forces(buf_now, batch_now, q)

    @pl.when(pairs > 0)
    def _():
        last = 2 * (first + pairs) - 1
        for q in range(BATCH):
            quantities(buf_a, 2 * first, q)

        def body(i, carry):
            both(buf_b, buf_a, 2 * i + 1, 2 * i)
            both(buf_a, buf_b, jnp.minimum(2 * i + 2, last), 2 * i + 1)
            return carry

        lax.fori_loop(first, first + pairs, body, 0)


def near_place(b):
    return (b // (GRID * LAYERS) * (GRID + 2) + b // LAYERS % GRID + 1) * (LAYERS + 2) + b % LAYERS + 1


def near_kernel(steps, ids, region, w_home, w_src, acc, lx, ly, rx, ry, rr, buf_a, buf_b):
    def owned(i, carry):
        first = near_place(i * GROUP)
        places = [first + g for g in range(GROUP)]
        z = jnp.concatenate([factors(region[p]) for p in places], 1)
        store_source(places, z, w_src, rx, ry, rr)
        store_home(i * GROUP, z, w_home, lx, ly)
        return carry

    def rim_place(i):
        side, at = i // 28, i % 28
        place_y = jnp.where(at < 10, 0, jnp.where(at < 20, GRID + 1, 1 + (at - 20) // 2))
        place_z = jnp.where(at < 20, at % 10, (at - 20) % 2 * (LAYERS + 1))
        return (side * (GRID + 2) + place_y) * (LAYERS + 2) + place_z

    def rim(i, carry):
        places = [rim_place(i * GROUP + g) for g in range(GROUP)]
        z = jnp.concatenate([factors(region[p]) for p in places], 1)
        store_source(places, z, w_src, rx, ry, rr)
        return carry

    lax.fori_loop(0, 128 // GROUP, owned, 0, unroll=4)
    lax.fori_loop(0, 112 // GROUP, rim, 0, unroll=7)
    acc[...] = jnp.zeros_like(acc)
    all_tiles(0, steps[0], ids, lx, ly, rx, ry, rr, acc, buf_a, buf_b)


def far_kernel(steps, ids, low, high, region, w_src, lx, ly, acc, out, acc_out, rx, ry, rr, buf_a, buf_b):
    def prepare(i, carry):
        for k, (plane, off_x) in enumerate(((low, -44.0), (high, 44.0))):
            places = [i * FAR_GROUP + g for g in range(FAR_GROUP)]
            z = jnp.concatenate([factors(plane[p], off_x) for p in places], 1)
            store_source([p + 60 * k for p in places], z, w_src, rx, ry, rr)
        return carry

    lax.fori_loop(0, 60 // FAR_GROUP, prepare, 0, unroll=2)
    all_tiles(steps[0], steps[1], ids, lx, ly, rx, ry, rr, acc_out, buf_a, buf_b)

    def finish(s, carry):
        first = near_place(4 * s)
        for k in range(4):
            sums = acc_out[4 * s + k]
            head, tail = sums[:8], sums[8:]
            weighed = head + pltpu.roll(head, 4, 0) + tail
            out[s, 3 * k : 3 * k + 3] = (region[first + k] * head[3:4] - weighed)[:3]
        return carry

    lax.fori_loop(0, 32, finish, 0, unroll=4)


def tile_lists(tiles, blocks):
    home, source = tiles[0], tiles[1]
    slot, member = source // blocks, source % blocks
    step_x = slot // 9 - 1
    place_y = member // LAYERS % GRID + (slot // 3 % 3 - 1) * GRID + 1
    place_z = member % LAYERS + (slot % 3 - 1) * LAYERS + 1
    plane = place_y * (LAYERS + 2) + place_z
    side = jnp.where(step_x == 0, member // (GRID * LAYERS), (step_x + 1) // 2)
    listed = home >= 0
    near = listed & (step_x == 0)
    far = listed & (step_x != 0)
    unit = 2 * BATCH
    order = jnp.arange(home.shape[0])
    upto = order[None, :] <= order[:, None]
    near_at = jnp.sum(jnp.where(upto & near[None, :], 1, 0), 1)
    far_at = jnp.sum(jnp.where(upto & far[None, :], 1, 0), 1)
    near_steps = (jnp.sum(near.astype(jnp.int32)) + unit - 1) // unit
    far_steps = (jnp.sum(far.astype(jnp.int32)) + unit - 1) // unit
    at = jnp.where(near, near_at - 1, jnp.where(far, near_steps * unit + far_at - 1, -1))
    code = home * 256 + side * 60 + plane + 1
    slots = jnp.arange(home.shape[0] + 2 * unit)
    found = jnp.sum(jnp.where(slots[:, None] == at[None, :], code[None, :], 0), 1)
    real = found > 0
    code = jnp.maximum(found - 1, 0)
    ids = jnp.stack([code // 256, code % 256, jnp.where(real, code // 256, blocks)])
    return jnp.stack([near_steps, far_steps]), ids


def per_device(coords, charges, atom_types, lj_sigma, lj_epsilon, tile_list):
    blocks, width = coords.shape[2], coords.shape[3]
    peers = lax.axis_size("gy") * lax.axis_size("gz")
    vmem = pl.BlockSpec(memory_space=pltpu.VMEM)
    smem = pl.BlockSpec(memory_space=pltpu.SMEM)
    gz = lax.axis_index("gz")
    small = pltpu.CompilerParams(vmem_limit_bytes=8 << 20)
    outgoing = pl.pallas_call(
        pack_kernel,
        out_shape=jax.ShapeDtypeStruct((peers * SENT, width), F32),
        in_specs=[smem, smem] + [pl.BlockSpec(memory_space=pl.ANY)] * 3,
        out_specs=vmem,
        scratch_shapes=[
            pltpu.VMEM((3, blocks, width), F32),
            pltpu.VMEM((blocks, width), F32),
            pltpu.VMEM((blocks, width), jnp.int32),
            pltpu.SemaphoreType.DMA((3,)),
        ],
        compiler_params=pltpu.CompilerParams(vmem_limit_bytes=65011712),
    )((gz % 2).reshape(1), (gz // 2).reshape(1), coords[:, 0], charges[0], atom_types[0])
    arrived = lax.all_to_all(
        outgoing.reshape(peers, SENT, width), ("gy", "gz"), split_axis=0, concat_axis=0, tiled=True
    )
    steps, ids = tile_lists(tile_list[0, 0, 0], blocks)
    w_home, w_src = weights(lj_sigma, lj_epsilon)
    region = pl.pallas_call(
        unpack_kernel,
        out_shape=jax.ShapeDtypeStruct((NEAR + 1, 8, width), F32),
        in_specs=[vmem],
        out_specs=vmem,
        compiler_params=small,
    )(arrived)
    count = lax.axis_size("gx")
    forward = [(i, (i + 1) % count) for i in range(count)]
    backward = [(target, source) for source, target in forward]
    low = lax.ppermute(region[180:240], "gx", forward)
    high = lax.ppermute(region[:60], "gx", backward)

    def source_scratch(n):
        return [
            pltpu.VMEM((n, NX, 256), BF16),
            pltpu.VMEM((n, NY, 256), BF16),
            pltpu.VMEM((n, 16, 256), BF16),
            pltpu.VMEM((BATCH, 2, 128, 256), F32),
            pltpu.VMEM((BATCH, 2, 128, 256), F32),
        ]

    acc_shape = jax.ShapeDtypeStruct((blocks + 1, 16, width), F32)
    factor_shape = jax.ShapeDtypeStruct((blocks, 128, 128), BF16)
    acc, lx, ly = pl.pallas_call(
        near_kernel,
        out_shape=[acc_shape, factor_shape, factor_shape],
        in_specs=[smem, smem, vmem, vmem, vmem],
        out_specs=[vmem] * 3,
        scratch_shapes=source_scratch(NEAR),
        compiler_params=pltpu.CompilerParams(vmem_limit_bytes=28 << 20),
        cost_estimate=pl.CostEstimate(flops=10**10, bytes_accessed=10**7, transcendentals=10**6),
    )(steps, ids, region, w_home, w_src)
    totals, _ = pl.pallas_call(
        far_kernel,
        out_shape=[jax.ShapeDtypeStruct((peers, 12, width), F32), acc_shape],
        in_specs=[smem, smem] + [vmem] * 7,
        out_specs=[vmem] * 2,
        scratch_shapes=source_scratch(120),
        input_output_aliases={8: 1},
        compiler_params=pltpu.CompilerParams(vmem_limit_bytes=24 << 20),
    )(steps, ids, low, high, region, w_src, lx, ly, acc)
    back = lax.all_to_all(totals, ("gy", "gz"), split_axis=0, concat_axis=0, tiled=True)
    return back.reshape(peers, 4, 3, width).transpose(2, 1, 0, 3).reshape(3, 1, blocks, width)


def solution(mesh):
    return jax.shard_map(
        per_device,
        mesh=mesh,
        in_specs=(
            P(None, "gx", ("gy", "gz"), None),
            P("gx", ("gy", "gz"), None),
            P("gx", ("gy", "gz"), None),
            P(),
            P(),
            P("gx", "gy", "gz", None, None),
        ),
        out_specs=P(None, "gx", ("gy", "gz"), None),
        check_vma=False,
    )
```

```python
import math

import jax
import jax.numpy as jnp
import numpy as np
from jax import lax
from jax.experimental import pallas as pl
from jax.experimental.pallas import tpu as pltpu
from jax.sharding import PartitionSpec as P

F32 = jnp.float32
BF16 = jnp.bfloat16

GRID = 4
LAYERS = 8
CELL = 11.0
LIMIT = 97.0
COULOMB = 332.0636

ROW_X, ROW_Y, ROW_Z, ROW_C, ROW_TYPE, ROW_Q, ROW_ONE, ROW_CC = range(8)
TYPES = 64
ORDER = 13
NX = 32
NY = 48
NZ = TYPES + 32
BATCH = 4
GROUP = 8
FAR_GROUP = 10
NEAR = 240
SENT = 56


def placements():
    home = np.zeros((32, NX), np.float32)
    src_w = np.zeros((NX, 32), np.float32)
    src_c = np.zeros((NX, 32), np.float32)
    at = 0

    def term(row, part):
        return part * 8 + row

    for row in (ROW_X, ROW_Y, ROW_Z):
        for i, j in ((0, 0), (0, 1), (1, 0), (1, 1), (0, 2), (2, 0)):
            home[term(row, i), at] = 1.0
            src_w[at, term(row, j)] = -2.0
            at += 1
    for part in range(3):
        home[term(ROW_Q, part), at] = 1.0
        src_w[at, term(ROW_ONE, 0)] = 1.0
        at += 1
    for part in range(3):
        home[term(ROW_ONE, 0), at] = 1.0
        src_w[at, term(ROW_Q, part)] = 1.0
        at += 1
    home[term(ROW_ONE, 0), at] = 1.0
    src_w[at, term(ROW_ONE, 0)] = 16.0
    at += 1
    for i, j in ((0, 0), (0, 1), (1, 0), (1, 1), (0, 2), (2, 0)):
        home[term(ROW_CC, i), at] = 1.0
        src_c[at, term(ROW_C, j)] = 1.0
        at += 1
    place_r = np.zeros((16, 32), np.float32)
    for k, row in enumerate((ROW_X, ROW_Y, ROW_Z)):
        for part in range(3):
            place_r[4 * part + k, term(row, part)] = 1.0
    place_r[3, term(ROW_ONE, 0)] = 1.0
    return home, src_w, src_c, place_r


def weights(lj_sigma, lj_epsilon):
    root = jnp.sqrt(lj_epsilon)
    half = 0.5 * lj_sigma
    powers = [jnp.ones_like(half)]
    for _ in range(ORDER - 1):
        powers.append(powers[-1] * half)

    def halves(table):
        high = lax.reduce_precision(table, 8, 7)
        return high, table - high

    h_high, h_low = halves(jnp.stack([root * p for p in powers]))
    zero = jnp.zeros_like(half)
    p12 = jnp.stack([root * powers[12 - k] * (48.0 * math.comb(12, k)) for k in range(ORDER)])
    p6 = jnp.stack(
        [root * powers[6 - k] * (24.0 * math.comb(6, k)) if k <= 6 else zero for k in range(ORDER)]
    )
    pad = jnp.zeros((NY - 3 * ORDER, TYPES), F32)
    home_y = jnp.concatenate([h_high, h_high, h_low, pad])
    src_y = []
    for table in (p12, p6):
        high, low = halves(table)
        src_y += [high, low, high, pad]
    home_x, src_w, src_c, place_r = placements()
    home_x = np.pad(home_x, ((TYPES, 0), (0, 128 - NX)))
    home = jnp.concatenate([home_x, jnp.pad(home_y.T, ((0, NZ - TYPES), (0, 128 - NY)))], 1)
    fixed = jnp.concatenate([jnp.zeros((2 * NX + 16, TYPES)), np.concatenate([src_w, src_c, place_r])], 1)
    lj = jnp.concatenate([jnp.concatenate(src_y), jnp.zeros((2 * NY, 32), F32)], 1)
    source = jnp.concatenate([fixed, lj])
    return home.astype(BF16), source.astype(BF16)


def pack_kernel(half_hi, side, coords_in, charges_in, types_in, out, coords, charges, types, sems):
    copies = [
        pltpu.make_async_copy(source, target, sems.at[i])
        for i, (source, target) in enumerate(
            ((coords_in, coords), (charges_in, charges), (types_in, types))
        )
    ]
    for copy in copies:
        copy.start()
    for copy in copies:
        copy.wait()
    upper = half_hi[0] == 1
    back_y = side[0] == 3
    kinds = types[...].astype(F32)

    def next_y(value):
        ahead = jnp.concatenate([value[8:], value[:8]])
        behind = jnp.concatenate([value[24:], value[:24]])
        return jnp.where(back_y, behind, ahead)

    for q in range(5):
        for cell in range(5):

            def rows(k):
                if q < 3:
                    return coords[q, 32 * k : 32 * k + 32]
                return charges[32 * k : 32 * k + 32] if q == 3 else kinds[32 * k : 32 * k + 32]

            if cell < 4:
                value = rows(cell)
            else:
                ahead = pltpu.roll(rows(0).reshape(4, 8, 128), 7, 1)
                behind = pltpu.roll(rows(3).reshape(4, 8, 128), 1, 1)
                value = jnp.where(upper, behind, ahead).reshape(32, 128)
            out[pl.ds(5 * cell + q, 32, stride=SENT), :] = value
            out[pl.ds(25 + 5 * cell + q, 32, stride=SENT), :] = next_y(value)


def unpack_kernel(arrived, out):
    row = lax.broadcasted_iota(jnp.int32, (8, 128), 0)

    def body(s, carry):
        cell_x, cell_y, upper = s // 8, s // 2 % 4, s % 2
        for c in range(10):
            place_y = cell_y + 1
            if c >= 5:
                place_y = jnp.where(cell_y == 0, GRID + 1, 0)
            place_z = upper * 4 + c % 5 + 1 if c % 5 < 4 else jnp.where(upper == 1, 0, LAYERS + 1)
            place = (cell_x * (GRID + 2) + place_y) * (LAYERS + 2) + place_z
            if c >= 5:
                inner = jnp.logical_and(cell_y > 0, cell_y < GRID - 1)
                place = jnp.where(inner, NEAR, place)
            block = jnp.concatenate([arrived[s, 5 * c : 5 * c + 5], jnp.zeros((3, 128), F32)])
            off_x = cell_x.astype(F32) * CELL - 2 * CELL
            off_y = place_y.astype(F32) * CELL - 3 * CELL
            off_z = place_z.astype(F32) * CELL - 5 * CELL
            off = jnp.where(row == ROW_X, off_x, 0.0) + jnp.where(row == ROW_Y, off_y, 0.0)
            out[place] = block + (off + jnp.where(row == ROW_Z, off_z, 0.0))
        return carry

    lax.fori_loop(0, 32, body, 0, unroll=2)


def powers_of(w):
    u = lax.rsqrt(w)
    inv = u * u
    inv2 = inv * inv
    inv4 = inv2 * inv2
    return inv4 * (inv2 * inv), inv4, u * inv


def factors(block, off_x=None):
    row = lax.broadcasted_iota(jnp.int32, (8, 128), 0)
    kind = lax.broadcasted_iota(jnp.int32, (TYPES, 128), 0)
    moved = block if off_x is None else block + jnp.where(row == ROW_X, off_x, 0.0)
    square = jnp.sum(jnp.where(row < 3, moved * moved, 0.0), axis=0, keepdims=True)
    moved = jnp.where(row == ROW_Q, square, jnp.where(row == ROW_ONE, 1.0, moved))
    moved = jnp.where(row == ROW_CC, COULOMB * block[ROW_C : ROW_C + 1], moved)
    high = moved.astype(BF16).astype(F32)
    rest = moved - high
    mid = rest.astype(BF16).astype(F32)
    hot = jnp.where(block[ROW_TYPE : ROW_TYPE + 1].astype(jnp.int32) == kind, 1.0, 0.0)
    return jnp.concatenate([hot, high, mid, rest - mid, jnp.zeros((8, 128), F32)]).astype(BF16)


def store_source(places, z, w_src, rx, ry, rr):
    made = jnp.dot(w_src[...], z, preferred_element_type=F32).astype(BF16)
    for g, p in enumerate(places):
        own = made[:, 128 * g : 128 * g + 128]
        rx[p, :, :128] = own[:NX]
        rx[p, :, 128:] = own[NX : 2 * NX]
        rr[p, :, :128] = own[2 * NX : 2 * NX + 16]
        rr[p, :, 128:] = own[2 * NX : 2 * NX + 16]
        at = 2 * NX + 16
        ry[p, :, :128] = own[at : at + NY]
        ry[p, :, 128:] = own[at + NY :]


def store_home(first, z, w_home, lx, ly):
    made = lax.dot_general(z, w_home[...], (((0,), (0,)), ((), ())), preferred_element_type=F32)
    made = made.astype(BF16)
    for g in range(GROUP):
        own = made[128 * g : 128 * g + 128]
        lx[first + g] = own[:, :128]
        ly[first + g] = own[:, 128:]


def all_tiles(first, pairs, ids, lx, ly, rx, ry, rr, acc, buf_a, buf_b):
    k7, k4, k3 = powers_of(jnp.full((8, 128), LIMIT, F32))

    def quantities(buf, batch, q):
        h, j = ids[0, batch * BATCH + q], ids[1, batch * BATCH + q]
        buf[q, 0] = jnp.dot(lx[h][:, :NX], rx[j], preferred_element_type=F32)
        buf[q, 1] = jnp.dot(ly[h][:, :NY], ry[j], preferred_element_type=F32)

    def forces(buf, batch, q):
        j, h = ids[1, batch * BATCH + q], ids[2, batch * BATCH + q]

        def part(i, side):
            return buf[q, i, :, 128 * side : 128 * side + 128].reshape(16, 8, 128)

        p7, p4, p3 = powers_of(jnp.minimum(part(0, 0), LIMIT))
        push = (p7 - k7) * part(1, 0) - (p4 - k4) * part(1, 1) + (p3 - k3) * part(0, 1)
        push = push.reshape(128, 128)
        high = push.astype(BF16)
        low = (push - high.astype(F32)).astype(BF16)
        once = lax.dot_general(
            rr[j],
            jnp.concatenate([high, low], 1),
            (((1,), (1,)), ((), ())),
            preferred_element_type=F32,
        )
        acc[h] += once * ids[3, batch * BATCH + q].astype(F32)

    def both(buf_next, buf_now, batch_next, batch_now):
        for q in range(BATCH):
            quantities(buf_next, batch_next, q)
            forces(buf_now, batch_now, q)

    @pl.when(pairs > 0)
    def _():
        last = 2 * (first + pairs) - 1
        for q in range(BATCH):
            quantities(buf_a, 2 * first, q)

        def body(i, carry):
            both(buf_b, buf_a, 2 * i + 1, 2 * i)
            both(buf_a, buf_b, jnp.minimum(2 * i + 2, last), 2 * i + 1)
            return carry

        lax.fori_loop(first, first + pairs, body, 0)


def near_place(b):
    return (b // (GRID * LAYERS) * (GRID + 2) + b // LAYERS % GRID + 1) * (LAYERS + 2) + b % LAYERS + 1


def near_kernel(steps, ids, region, w_home, w_src, acc, lx, ly, rx, ry, rr, buf_a, buf_b):
    def owned(i, carry):
        first = near_place(i * GROUP)
        places = [first + g for g in range(GROUP)]
        z = jnp.concatenate([factors(region[p]) for p in places], 1)
        store_source(places, z, w_src, rx, ry, rr)
        store_home(i * GROUP, z, w_home, lx, ly)
        return carry

    def rim_place(i):
        side, at = i // 28, i % 28
        place_y = jnp.where(at < 10, 0, jnp.where(at < 20, GRID + 1, 1 + (at - 20) // 2))
        place_z = jnp.where(at < 20, at % 10, (at - 20) % 2 * (LAYERS + 1))
        return (side * (GRID + 2) + place_y) * (LAYERS + 2) + place_z

    def rim(i, carry):
        places = [rim_place(i * GROUP + g) for g in range(GROUP)]
        z = jnp.concatenate([factors(region[p]) for p in places], 1)
        store_source(places, z, w_src, rx, ry, rr)
        return carry

    lax.fori_loop(0, 128 // GROUP, owned, 0, unroll=4)
    lax.fori_loop(0, 112 // GROUP, rim, 0, unroll=7)
    acc[...] = jnp.zeros_like(acc)
    all_tiles(0, steps[0], ids, lx, ly, rx, ry, rr, acc, buf_a, buf_b)


def far_kernel(steps, ids, low, high, region, w_src, lx, ly, acc, out, acc_out, rx, ry, rr, buf_a, buf_b):
    def prepare(i, carry):
        for k, (plane, off_x) in enumerate(((low, -44.0), (high, 44.0))):
            places = [i * FAR_GROUP + g for g in range(FAR_GROUP)]
            z = jnp.concatenate([factors(plane[p], off_x) for p in places], 1)
            store_source([p + 60 * k for p in places], z, w_src, rx, ry, rr)
        return carry

    lax.fori_loop(0, 60 // FAR_GROUP, prepare, 0, unroll=2)
    all_tiles(steps[0], steps[1], ids, lx, ly, rx, ry, rr, acc_out, buf_a, buf_b)

    def finish(s, carry):
        first = near_place(4 * s)
        for k in range(4):
            sums = acc_out[4 * s + k]
            head, tail = sums[:8], sums[8:]
            weighed = head + pltpu.roll(head, 4, 0) + tail
            out[s, 3 * k : 3 * k + 3] = (region[first + k] * head[3:4] - weighed)[:3]
        return carry

    lax.fori_loop(0, 32, finish, 0, unroll=4)


def tile_lists(tiles, blocks):
    home, source = tiles[0], tiles[1]
    slot, member = source // blocks, source % blocks
    step_x = slot // 9 - 1
    place_y = member // LAYERS % GRID + (slot // 3 % 3 - 1) * GRID + 1
    place_z = member % LAYERS + (slot % 3 - 1) * LAYERS + 1
    plane = place_y * (LAYERS + 2) + place_z
    side = jnp.where(step_x == 0, member // (GRID * LAYERS), (step_x + 1) // 2)
    listed = home >= 0
    unit = 2 * BATCH
    order = jnp.arange(home.shape[0])
    upto = order[None, :] <= order[:, None]
    key = home * (27 * blocks) + source
    same = key[None, :] == key[:, None]
    times = jnp.sum(jnp.where(same, 1, 0), 1)
    first = jnp.sum(jnp.where(same & upto, 1, 0), 1) == 1
    near = listed & first & (step_x == 0)
    far = listed & first & (step_x != 0)
    near_at = jnp.sum(jnp.where(upto & near[None, :], 1, 0), 1)
    far_at = jnp.sum(jnp.where(upto & far[None, :], 1, 0), 1)
    near_steps = (jnp.sum(near.astype(jnp.int32)) + unit - 1) // unit
    far_steps = (jnp.sum(far.astype(jnp.int32)) + unit - 1) // unit
    at = jnp.where(near, near_at - 1, jnp.where(far, near_steps * unit + far_at - 1, -1))
    code = home * 256 + side * 60 + plane + 1
    slots = jnp.arange(home.shape[0] + 2 * unit)
    found = jnp.sum(jnp.where(slots[:, None] == at[None, :], code[None, :], 0), 1)
    times = jnp.sum(jnp.where(slots[:, None] == at[None, :], times[None, :], 0), 1)
    real = found > 0
    code = jnp.maximum(found - 1, 0)
    ids = jnp.stack([code // 256, code % 256, jnp.where(real, code // 256, blocks), times])
    return jnp.stack([near_steps, far_steps]), ids


def per_device(coords, charges, atom_types, lj_sigma, lj_epsilon, tile_list):
    blocks, width = coords.shape[2], coords.shape[3]
    peers = lax.axis_size("gy") * lax.axis_size("gz")
    vmem = pl.BlockSpec(memory_space=pltpu.VMEM)
    smem = pl.BlockSpec(memory_space=pltpu.SMEM)
    gz = lax.axis_index("gz")
    small = pltpu.CompilerParams(vmem_limit_bytes=8 << 20)
    outgoing = pl.pallas_call(
        pack_kernel,
        out_shape=jax.ShapeDtypeStruct((peers * SENT, width), F32),
        in_specs=[smem, smem] + [pl.BlockSpec(memory_space=pl.ANY)] * 3,
        out_specs=vmem,
        scratch_shapes=[
            pltpu.VMEM((3, blocks, width), F32),
            pltpu.VMEM((blocks, width), F32),
            pltpu.VMEM((blocks, width), jnp.int32),
            pltpu.SemaphoreType.DMA((3,)),
        ],
        compiler_params=pltpu.CompilerParams(vmem_limit_bytes=65011712),
    )((gz % 2).reshape(1), (gz // 2).reshape(1), coords[:, 0], charges[0], atom_types[0])
    arrived = lax.all_to_all(
        outgoing.reshape(peers, SENT, width), ("gy", "gz"), split_axis=0, concat_axis=0, tiled=True
    )
    steps, ids = tile_lists(tile_list[0, 0, 0], blocks)
    w_home, w_src = weights(lj_sigma, lj_epsilon)
    region = pl.pallas_call(
        unpack_kernel,
        out_shape=jax.ShapeDtypeStruct((NEAR + 1, 8, width), F32),
        in_specs=[vmem],
        out_specs=vmem,
        compiler_params=small,
    )(arrived)
    count = lax.axis_size("gx")
    forward = [(i, (i + 1) % count) for i in range(count)]
    backward = [(target, source) for source, target in forward]
    low = lax.ppermute(region[180:240], "gx", forward)
    high = lax.ppermute(region[:60], "gx", backward)

    def source_scratch(n):
        return [
            pltpu.VMEM((n, NX, 256), BF16),
            pltpu.VMEM((n, NY, 256), BF16),
            pltpu.VMEM((n, 16, 256), BF16),
            pltpu.VMEM((BATCH, 2, 128, 256), F32),
            pltpu.VMEM((BATCH, 2, 128, 256), F32),
        ]

    acc_shape = jax.ShapeDtypeStruct((blocks + 1, 16, width), F32)
    factor_shape = jax.ShapeDtypeStruct((blocks, 128, 128), BF16)
    acc, lx, ly = pl.pallas_call(
        near_kernel,
        out_shape=[acc_shape, factor_shape, factor_shape],
        in_specs=[smem, smem, vmem, vmem, vmem],
        out_specs=[vmem] * 3,
        scratch_shapes=source_scratch(NEAR),
        compiler_params=pltpu.CompilerParams(vmem_limit_bytes=28 << 20),
        cost_estimate=pl.CostEstimate(flops=10**10, bytes_accessed=10**7, transcendentals=10**6),
    )(steps, ids, region, w_home, w_src)
    totals, _ = pl.pallas_call(
        far_kernel,
        out_shape=[jax.ShapeDtypeStruct((peers, 12, width), F32), acc_shape],
        in_specs=[smem, smem] + [vmem] * 7,
        out_specs=[vmem] * 2,
        scratch_shapes=source_scratch(120),
        input_output_aliases={8: 1},
        compiler_params=pltpu.CompilerParams(vmem_limit_bytes=24 << 20),
    )(steps, ids, low, high, region, w_src, lx, ly, acc)
    back = lax.all_to_all(totals, ("gy", "gz"), split_axis=0, concat_axis=0, tiled=True)
    return back.reshape(peers, 4, 3, width).transpose(2, 1, 0, 3).reshape(3, 1, blocks, width)


def solution(mesh):
    return jax.shard_map(
        per_device,
        mesh=mesh,
        in_specs=(
            P(None, "gx", ("gy", "gz"), None),
            P("gx", ("gy", "gz"), None),
            P("gx", ("gy", "gz"), None),
            P(),
            P(),
            P("gx", "gy", "gz", None, None),
        ),
        out_specs=P(None, "gx", ("gy", "gz"), None),
        check_vma=False,
    )
```

```python
import math

import jax
import jax.numpy as jnp
import numpy as np
from jax import lax
from jax.experimental import pallas as pl
from jax.experimental.pallas import tpu as pltpu
from jax.sharding import PartitionSpec as P

F32 = jnp.float32
BF16 = jnp.bfloat16

GRID = 4
LAYERS = 8
CELL = 11.0
LIMIT = 97.0
SCALE = LIMIT**-0.5
SOFT = 16.0 / LIMIT
COULOMB = 332.0636 / LIMIT
FACTOR_12 = 48.0 * LIMIT**-6.5
FACTOR_6 = 24.0 * LIMIT**-3.5

ROW_X, ROW_Y, ROW_Z, ROW_C, ROW_TYPE, ROW_Q, ROW_ONE, ROW_CC = range(8)
ROW_SOFT = ROW_TYPE
TYPES = 64
ORDER = 13
NX = 32
NY = 48
NZ = TYPES + 32
BATCH = 4
GROUP = 8
FAR_GROUP = 10
NEAR = 240
SENT = 56


def placements():
    home = np.zeros((32, NX), np.float32)
    src_w = np.zeros((NX, 32), np.float32)
    src_c = np.zeros((NX, 32), np.float32)
    at = 0

    def term(row, part):
        return part * 8 + row

    for row in (ROW_X, ROW_Y, ROW_Z):
        for i, j in ((0, 0), (0, 1), (1, 0), (1, 1), (0, 2), (2, 0)):
            home[term(row, i), at] = 1.0
            src_w[at, term(row, j)] = -2.0
            at += 1
    for part in range(3):
        home[term(ROW_SOFT, part), at] = 1.0
        src_w[at, term(ROW_ONE, 0)] = 1.0
        at += 1
    for part in range(3):
        home[term(ROW_ONE, 0), at] = 1.0
        src_w[at, term(ROW_Q, part)] = 1.0
        at += 1
    for i, j in ((0, 0), (0, 1), (1, 0), (1, 1), (0, 2), (2, 0)):
        home[term(ROW_CC, i), at] = 1.0
        src_c[at, term(ROW_C, j)] = 1.0
        at += 1
    place_r = np.zeros((16, 32), np.float32)
    for k, row in enumerate((ROW_X, ROW_Y, ROW_Z)):
        for part in range(3):
            place_r[4 * part + k, term(row, part)] = 1.0
    place_r[3, term(ROW_ONE, 0)] = 1.0
    return home, src_w, src_c, place_r


def weights(lj_sigma, lj_epsilon):
    root = jnp.sqrt(lj_epsilon)
    half = 0.5 * lj_sigma
    powers = [jnp.ones_like(half)]
    for _ in range(ORDER - 1):
        powers.append(powers[-1] * half)

    def halves(table):
        high = lax.reduce_precision(table, 8, 7)
        return high, table - high

    h_high, h_low = halves(jnp.stack([root * p for p in powers]))
    zero = jnp.zeros_like(half)
    p12 = jnp.stack([root * powers[12 - k] * (FACTOR_12 * math.comb(12, k)) for k in range(ORDER)])
    p6 = jnp.stack(
        [root * powers[6 - k] * (FACTOR_6 * math.comb(6, k)) if k <= 6 else zero for k in range(ORDER)]
    )
    pad = jnp.zeros((NY - 3 * ORDER, TYPES), F32)
    home_y = jnp.concatenate([h_high, h_high, h_low, pad])
    src_y = []
    for table in (p12, p6):
        high, low = halves(table)
        src_y += [high, low, high, pad]
    home_x, src_w, src_c, place_r = placements()
    home_x = np.pad(home_x, ((TYPES, 0), (0, 128 - NX)))
    home = jnp.concatenate([home_x, jnp.pad(home_y.T, ((0, NZ - TYPES), (0, 128 - NY)))], 1)
    fixed = jnp.concatenate([jnp.zeros((2 * NX + 16, TYPES)), np.concatenate([src_w, src_c, place_r])], 1)
    lj = jnp.concatenate([jnp.concatenate(src_y), jnp.zeros((2 * NY, 32), F32)], 1)
    source = jnp.concatenate([fixed, lj])
    return home.astype(BF16), source.astype(BF16)


def pack_kernel(half_hi, side, coords_in, charges_in, types_in, out, coords, charges, types, sems):
    copies = [
        pltpu.make_async_copy(source, target, sems.at[i])
        for i, (source, target) in enumerate(
            ((coords_in, coords), (charges_in, charges), (types_in, types))
        )
    ]
    for copy in copies:
        copy.start()
    for copy in copies:
        copy.wait()
    upper = half_hi[0] == 1
    back_y = side[0] == 3
    kinds = types[...].astype(F32)

    def next_y(value):
        ahead = jnp.concatenate([value[8:], value[:8]])
        behind = jnp.concatenate([value[24:], value[:24]])
        return jnp.where(back_y, behind, ahead)

    for q in range(5):
        for cell in range(5):

            def rows(k):
                if q < 3:
                    return coords[q, 32 * k : 32 * k + 32]
                return charges[32 * k : 32 * k + 32] if q == 3 else kinds[32 * k : 32 * k + 32]

            if cell < 4:
                value = rows(cell)
            else:
                ahead = pltpu.roll(rows(0).reshape(4, 8, 128), 7, 1)
                behind = pltpu.roll(rows(3).reshape(4, 8, 128), 1, 1)
                value = jnp.where(upper, behind, ahead).reshape(32, 128)
            out[pl.ds(5 * cell + q, 32, stride=SENT), :] = value
            out[pl.ds(25 + 5 * cell + q, 32, stride=SENT), :] = next_y(value)


def unpack_kernel(arrived, out):
    row = lax.broadcasted_iota(jnp.int32, (8, 128), 0)

    def body(s, carry):
        cell_x, cell_y, upper = s // 8, s // 2 % 4, s % 2
        for c in range(10):
            place_y = cell_y + 1
            if c >= 5:
                place_y = jnp.where(cell_y == 0, GRID + 1, 0)
            place_z = upper * 4 + c % 5 + 1 if c % 5 < 4 else jnp.where(upper == 1, 0, LAYERS + 1)
            place = (cell_x * (GRID + 2) + place_y) * (LAYERS + 2) + place_z
            if c >= 5:
                inner = jnp.logical_and(cell_y > 0, cell_y < GRID - 1)
                place = jnp.where(inner, NEAR, place)
            block = jnp.concatenate([arrived[s, 5 * c : 5 * c + 5], jnp.zeros((3, 128), F32)])
            off_x = cell_x.astype(F32) * CELL - 2 * CELL
            off_y = place_y.astype(F32) * CELL - 3 * CELL
            off_z = place_z.astype(F32) * CELL - 5 * CELL
            off = jnp.where(row == ROW_X, off_x, 0.0) + jnp.where(row == ROW_Y, off_y, 0.0)
            block = block + (off + jnp.where(row == ROW_Z, off_z, 0.0))
            out[place] = block * jnp.where(row < 3, SCALE, 1.0)
        return carry

    lax.fori_loop(0, 32, body, 0, unroll=2)


def factors(block, off_x=None):
    row = lax.broadcasted_iota(jnp.int32, (8, 128), 0)
    kind = lax.broadcasted_iota(jnp.int32, (TYPES, 128), 0)
    moved = block if off_x is None else block + jnp.where(row == ROW_X, off_x, 0.0)
    square = jnp.sum(jnp.where(row < 3, moved * moved, 0.0), axis=0, keepdims=True)
    moved = jnp.where(row == ROW_Q, square, jnp.where(row == ROW_ONE, 1.0, moved))
    moved = jnp.where(row == ROW_SOFT, square + SOFT, moved)
    moved = jnp.where(row == ROW_CC, COULOMB * block[ROW_C : ROW_C + 1], moved)
    high = moved.astype(BF16).astype(F32)
    rest = moved - high
    mid = rest.astype(BF16).astype(F32)
    hot = jnp.where(block[ROW_TYPE : ROW_TYPE + 1].astype(jnp.int32) == kind, 1.0, 0.0)
    return jnp.concatenate([hot, high, mid, rest - mid, jnp.zeros((8, 128), F32)]).astype(BF16)


def store_source(places, z, w_src, rx, ry, rr):
    made = jnp.dot(w_src[...], z, preferred_element_type=F32).astype(BF16)
    for g, p in enumerate(places):
        own = made[:, 128 * g : 128 * g + 128]
        rx[p, :, :128] = own[:NX]
        rx[p, :, 128:] = own[NX : 2 * NX]
        rr[p, :, :128] = own[2 * NX : 2 * NX + 16]
        rr[p, :, 128:] = own[2 * NX : 2 * NX + 16]
        at = 2 * NX + 16
        ry[p, :, :128] = own[at : at + NY]
        ry[p, :, 128:] = own[at + NY :]


def store_home(first, z, w_home, lx, ly):
    made = lax.dot_general(z, w_home[...], (((0,), (0,)), ((), ())), preferred_element_type=F32)
    made = made.astype(BF16)
    for g in range(GROUP):
        own = made[128 * g : 128 * g + 128]
        lx[first + g] = own[:, :128]
        ly[first + g] = own[:, 128:]


def all_tiles(first, pairs, ids, lx, ly, rx, ry, rr, acc, buf_a, buf_b):
    def quantities(buf, batch, q):
        h, j = ids[0, batch * BATCH + q], ids[1, batch * BATCH + q]
        buf[q, 0] = jnp.dot(lx[h][:, :NX], rx[j], preferred_element_type=F32)
        buf[q, 1] = jnp.dot(ly[h][:, :NY], ry[j], preferred_element_type=F32)

    def forces(buf, batch, q):
        j, h = ids[1, batch * BATCH + q], ids[2, batch * BATCH + q]

        def part(i, side):
            return buf[q, i, :, 128 * side : 128 * side + 128].reshape(16, 8, 128)

        u = lax.rsqrt(jnp.minimum(part(0, 0), 1.0))
        inv = u * u
        inv3 = inv * inv * inv
        c12, c6, charge = part(1, 0), part(1, 1), part(0, 1)
        push = inv * (inv3 * (inv3 * c12 - c6) + u * charge) - ((c12 - c6) + charge)
        push = push.reshape(128, 128)
        high = push.astype(BF16)
        low = (push - high.astype(F32)).astype(BF16)
        once = lax.dot_general(
            rr[j],
            jnp.concatenate([high, low], 1),
            (((1,), (1,)), ((), ())),
            preferred_element_type=F32,
        )
        acc[h] += once * ids[3, batch * BATCH + q].astype(F32)

    def both(buf_next, buf_now, batch_next, batch_now):
        for q in range(BATCH):
            quantities(buf_next, batch_next, q)
            forces(buf_now, batch_now, q)

    @pl.when(pairs > 0)
    def _():
        last = 2 * (first + pairs) - 1
        for q in range(BATCH):
            quantities(buf_a, 2 * first, q)

        def body(i, carry):
            both(buf_b, buf_a, 2 * i + 1, 2 * i)
            both(buf_a, buf_b, jnp.minimum(2 * i + 2, last), 2 * i + 1)
            return carry

        lax.fori_loop(first, first + pairs, body, 0)


def near_place(b):
    return (b // (GRID * LAYERS) * (GRID + 2) + b // LAYERS % GRID + 1) * (LAYERS + 2) + b % LAYERS + 1


def near_kernel(steps, ids, region, w_home, w_src, acc, lx, ly, rx, ry, rr, buf_a, buf_b):
    def owned(i, carry):
        first = near_place(i * GROUP)
        places = [first + g for g in range(GROUP)]
        z = jnp.concatenate([factors(region[p]) for p in places], 1)
        store_source(places, z, w_src, rx, ry, rr)
        store_home(i * GROUP, z, w_home, lx, ly)
        return carry

    def rim_place(i):
        side, at = i // 28, i % 28
        place_y = jnp.where(at < 10, 0, jnp.where(at < 20, GRID + 1, 1 + (at - 20) // 2))
        place_z = jnp.where(at < 20, at % 10, (at - 20) % 2 * (LAYERS + 1))
        return (side * (GRID + 2) + place_y) * (LAYERS + 2) + place_z

    def rim(i, carry):
        places = [rim_place(i * GROUP + g) for g in range(GROUP)]
        z = jnp.concatenate([factors(region[p]) for p in places], 1)
        store_source(places, z, w_src, rx, ry, rr)
        return carry

    lax.fori_loop(0, 128 // GROUP, owned, 0, unroll=4)
    lax.fori_loop(0, 112 // GROUP, rim, 0, unroll=7)
    acc[...] = jnp.zeros_like(acc)
    all_tiles(0, steps[0], ids, lx, ly, rx, ry, rr, acc, buf_a, buf_b)


def far_kernel(steps, ids, low, high, region, w_src, lx, ly, acc, out, acc_out, rx, ry, rr, buf_a, buf_b):
    def prepare(i, carry):
        for k, (plane, off_x) in enumerate(((low, -44.0), (high, 44.0))):
            places = [i * FAR_GROUP + g for g in range(FAR_GROUP)]
            z = jnp.concatenate([factors(plane[p], off_x * SCALE) for p in places], 1)
            store_source([p + 60 * k for p in places], z, w_src, rx, ry, rr)
        return carry

    lax.fori_loop(0, 60 // FAR_GROUP, prepare, 0, unroll=2)
    all_tiles(steps[0], steps[1], ids, lx, ly, rx, ry, rr, acc_out, buf_a, buf_b)

    def finish(s, carry):
        first = near_place(4 * s)
        for k in range(4):
            sums = acc_out[4 * s + k]
            head, tail = sums[:8], sums[8:]
            weighed = head + pltpu.roll(head, 4, 0) + tail
            out[s, 3 * k : 3 * k + 3] = (region[first + k] * head[3:4] - weighed)[:3]
        return carry

    lax.fori_loop(0, 32, finish, 0, unroll=4)


def tile_lists(tiles, blocks):
    home, source = tiles[0], tiles[1]
    slot, member = source // blocks, source % blocks
    step_x = slot // 9 - 1
    place_y = member // LAYERS % GRID + (slot // 3 % 3 - 1) * GRID + 1
    place_z = member % LAYERS + (slot % 3 - 1) * LAYERS + 1
    plane = place_y * (LAYERS + 2) + place_z
    side = jnp.where(step_x == 0, member // (GRID * LAYERS), (step_x + 1) // 2)
    listed = home >= 0
    unit = 2 * BATCH
    order = jnp.arange(home.shape[0])
    upto = order[None, :] <= order[:, None]
    key = home * (27 * blocks) + source
    same = key[None, :] == key[:, None]
    times = jnp.sum(jnp.where(same, 1, 0), 1)
    first = jnp.sum(jnp.where(same & upto, 1, 0), 1) == 1
    near = listed & first & (step_x == 0)
    far = listed & first & (step_x != 0)
    near_at = jnp.sum(jnp.where(upto & near[None, :], 1, 0), 1)
    far_at = jnp.sum(jnp.where(upto & far[None, :], 1, 0), 1)
    near_steps = (jnp.sum(near.astype(jnp.int32)) + unit - 1) // unit
    far_steps = (jnp.sum(far.astype(jnp.int32)) + unit - 1) // unit
    at = jnp.where(near, near_at - 1, jnp.where(far, near_steps * unit + far_at - 1, -1))
    code = home * 256 + side * 60 + plane + 1
    slots = jnp.arange(home.shape[0] + 2 * unit)
    found = jnp.sum(jnp.where(slots[:, None] == at[None, :], code[None, :], 0), 1)
    times = jnp.sum(jnp.where(slots[:, None] == at[None, :], times[None, :], 0), 1)
    real = found > 0
    code = jnp.maximum(found - 1, 0)
    ids = jnp.stack([code // 256, code % 256, jnp.where(real, code // 256, blocks), times])
    return jnp.stack([near_steps, far_steps]), ids


def per_device(coords, charges, atom_types, lj_sigma, lj_epsilon, tile_list):
    blocks, width = coords.shape[2], coords.shape[3]
    peers = lax.axis_size("gy") * lax.axis_size("gz")
    vmem = pl.BlockSpec(memory_space=pltpu.VMEM)
    smem = pl.BlockSpec(memory_space=pltpu.SMEM)
    gz = lax.axis_index("gz")
    small = pltpu.CompilerParams(vmem_limit_bytes=8 << 20)
    outgoing = pl.pallas_call(
        pack_kernel,
        out_shape=jax.ShapeDtypeStruct((peers * SENT, width), F32),
        in_specs=[smem, smem] + [pl.BlockSpec(memory_space=pl.ANY)] * 3,
        out_specs=vmem,
        scratch_shapes=[
            pltpu.VMEM((3, blocks, width), F32),
            pltpu.VMEM((blocks, width), F32),
            pltpu.VMEM((blocks, width), jnp.int32),
            pltpu.SemaphoreType.DMA((3,)),
        ],
        compiler_params=pltpu.CompilerParams(vmem_limit_bytes=65011712),
    )((gz % 2).reshape(1), (gz // 2).reshape(1), coords[:, 0], charges[0], atom_types[0])
    arrived = lax.all_to_all(
        outgoing.reshape(peers, SENT, width), ("gy", "gz"), split_axis=0, concat_axis=0, tiled=True
    )
    steps, ids = tile_lists(tile_list[0, 0, 0], blocks)
    w_home, w_src = weights(lj_sigma, lj_epsilon)
    region = pl.pallas_call(
        unpack_kernel,
        out_shape=jax.ShapeDtypeStruct((NEAR + 1, 8, width), F32),
        in_specs=[vmem],
        out_specs=vmem,
        compiler_params=small,
    )(arrived)
    count = lax.axis_size("gx")
    forward = [(i, (i + 1) % count) for i in range(count)]
    backward = [(target, source) for source, target in forward]
    low = lax.ppermute(region[180:240], "gx", forward)
    high = lax.ppermute(region[:60], "gx", backward)

    def source_scratch(n):
        return [
            pltpu.VMEM((n, NX, 256), BF16),
            pltpu.VMEM((n, NY, 256), BF16),
            pltpu.VMEM((n, 16, 256), BF16),
            pltpu.VMEM((BATCH, 2, 128, 256), F32),
            pltpu.VMEM((BATCH, 2, 128, 256), F32),
        ]

    acc_shape = jax.ShapeDtypeStruct((blocks + 1, 16, width), F32)
    factor_shape = jax.ShapeDtypeStruct((blocks, 128, 128), BF16)
    acc, lx, ly = pl.pallas_call(
        near_kernel,
        out_shape=[acc_shape, factor_shape, factor_shape],
        in_specs=[smem, smem, vmem, vmem, vmem],
        out_specs=[vmem] * 3,
        scratch_shapes=source_scratch(NEAR),
        compiler_params=pltpu.CompilerParams(vmem_limit_bytes=28 << 20),
        cost_estimate=pl.CostEstimate(flops=10**10, bytes_accessed=10**7, transcendentals=10**6),
    )(steps, ids, region, w_home, w_src)
    totals, _ = pl.pallas_call(
        far_kernel,
        out_shape=[jax.ShapeDtypeStruct((peers, 12, width), F32), acc_shape],
        in_specs=[smem, smem] + [vmem] * 7,
        out_specs=[vmem] * 2,
        scratch_shapes=source_scratch(120),
        input_output_aliases={8: 1},
        compiler_params=pltpu.CompilerParams(vmem_limit_bytes=24 << 20),
    )(steps, ids, low, high, region, w_src, lx, ly, acc)
    back = lax.all_to_all(totals, ("gy", "gz"), split_axis=0, concat_axis=0, tiled=True)
    return back.reshape(peers, 4, 3, width).transpose(2, 1, 0, 3).reshape(3, 1, blocks, width)


def solution(mesh):
    return jax.shard_map(
        per_device,
        mesh=mesh,
        in_specs=(
            P(None, "gx", ("gy", "gz"), None),
            P("gx", ("gy", "gz"), None),
            P("gx", ("gy", "gz"), None),
            P(),
            P(),
            P("gx", "gy", "gz", None, None),
        ),
        out_specs=P(None, "gx", ("gy", "gz"), None),
        check_vma=False,
    )
```

```python
import math

import jax
import jax.numpy as jnp
import numpy as np
from jax import lax
from jax.experimental import pallas as pl
from jax.experimental.pallas import tpu as pltpu
from jax.sharding import PartitionSpec as P

F32 = jnp.float32
BF16 = jnp.bfloat16

GRID = 4
LAYERS = 8
CELL = 11.0
LIMIT = 97.0
SCALE = LIMIT**-0.5
SOFT = 16.0 / LIMIT
COULOMB = 332.0636 / LIMIT
FACTOR_12 = 48.0 * LIMIT**-6.5
FACTOR_6 = 24.0 * LIMIT**-3.5

ROW_X, ROW_Y, ROW_Z, ROW_C, ROW_TYPE, ROW_Q, ROW_ONE, ROW_CC = range(8)
ROW_SOFT = ROW_TYPE
TYPES = 64
ORDER = 13
NX = 32
NY = 48
NZ = TYPES + 32
BATCH = 4
GROUP = 8
FAR_GROUP = 10
NEAR = 240
SENT = 56


def placements():
    home = np.zeros((32, NX), np.float32)
    src_w = np.zeros((NX, 32), np.float32)
    src_c = np.zeros((NX, 32), np.float32)
    at = 0

    def term(row, part):
        return part * 8 + row

    for row in (ROW_X, ROW_Y, ROW_Z):
        for i, j in ((0, 0), (0, 1), (1, 0), (1, 1), (0, 2), (2, 0)):
            home[term(row, i), at] = 1.0
            src_w[at, term(row, j)] = -2.0
            at += 1
    for part in range(3):
        home[term(ROW_SOFT, part), at] = 1.0
        src_w[at, term(ROW_ONE, 0)] = 1.0
        at += 1
    for part in range(3):
        home[term(ROW_ONE, 0), at] = 1.0
        src_w[at, term(ROW_Q, part)] = 1.0
        at += 1
    for i, j in ((0, 0), (0, 1), (1, 0), (1, 1), (0, 2), (2, 0)):
        home[term(ROW_CC, i), at] = 1.0
        src_c[at, term(ROW_C, j)] = 1.0
        at += 1
    place_r = np.zeros((16, 32), np.float32)
    for k, row in enumerate((ROW_X, ROW_Y, ROW_Z)):
        for part in range(3):
            place_r[4 * part + k, term(row, part)] = 1.0
    place_r[3, term(ROW_ONE, 0)] = 1.0
    return home, src_w, src_c, place_r


def weights(lj_sigma, lj_epsilon):
    root = jnp.sqrt(lj_epsilon)
    half = 0.5 * lj_sigma
    powers = [jnp.ones_like(half)]
    for _ in range(ORDER - 1):
        powers.append(powers[-1] * half)

    def halves(table):
        high = lax.reduce_precision(table, 8, 7)
        return high, table - high

    h_high, h_low = halves(jnp.stack([root * p for p in powers]))
    zero = jnp.zeros_like(half)
    p12 = jnp.stack([root * powers[12 - k] * (FACTOR_12 * math.comb(12, k)) for k in range(ORDER)])
    p6 = jnp.stack(
        [root * powers[6 - k] * (FACTOR_6 * math.comb(6, k)) if k <= 6 else zero for k in range(ORDER)]
    )
    pad = jnp.zeros((NY - 3 * ORDER, TYPES), F32)
    home_y = jnp.concatenate([h_high, h_high, h_low, pad])
    src_y = []
    for table in (p12, p6):
        high, low = halves(table)
        src_y += [high, low, high, pad]
    home_x, src_w, src_c, place_r = placements()
    home_x = np.pad(home_x, ((TYPES, 0), (0, 128 - NX)))
    home = jnp.concatenate([home_x, jnp.pad(home_y.T, ((0, NZ - TYPES), (0, 128 - NY)))], 1)
    fixed = jnp.concatenate([jnp.zeros((2 * NX + 16, TYPES)), np.concatenate([src_w, src_c, place_r])], 1)
    lj = jnp.concatenate([jnp.concatenate(src_y), jnp.zeros((2 * NY, 32), F32)], 1)
    source = jnp.concatenate([fixed, lj])
    return home.astype(BF16), source.astype(BF16)


def pack_kernel(half_hi, side, coords_in, charges_in, types_in, out, coords, charges, types, sems):
    copies = [
        pltpu.make_async_copy(source, target, sems.at[i])
        for i, (source, target) in enumerate(
            ((coords_in, coords), (charges_in, charges), (types_in, types))
        )
    ]
    for copy in copies:
        copy.start()
    for copy in copies:
        copy.wait()
    upper = half_hi[0] == 1
    back_y = side[0] == 3
    kinds = types[...].astype(F32)

    def next_y(value):
        ahead = jnp.concatenate([value[8:], value[:8]])
        behind = jnp.concatenate([value[24:], value[:24]])
        return jnp.where(back_y, behind, ahead)

    for q in range(5):
        for cell in range(5):

            def rows(k):
                if q < 3:
                    return coords[q, 32 * k : 32 * k + 32]
                return charges[32 * k : 32 * k + 32] if q == 3 else kinds[32 * k : 32 * k + 32]

            if cell < 4:
                value = rows(cell)
            else:
                ahead = pltpu.roll(rows(0).reshape(4, 8, 128), 7, 1)
                behind = pltpu.roll(rows(3).reshape(4, 8, 128), 1, 1)
                value = jnp.where(upper, behind, ahead).reshape(32, 128)
            out[pl.ds(5 * cell + q, 32, stride=SENT), :] = value
            out[pl.ds(25 + 5 * cell + q, 32, stride=SENT), :] = next_y(value)


def unpack_kernel(arrived, out):
    row = lax.broadcasted_iota(jnp.int32, (8, 128), 0)
    scale = jnp.where(row < 3, SCALE, 1.0)

    def body(cell_x, carry):
        off_x = (cell_x.astype(F32) - 2) * (CELL * SCALE)
        for s in range(8):
            cell_y, upper = s // 2, s % 2
            for c in range(10 if cell_y in (0, GRID - 1) else 5):
                place_y = cell_y + 1
                if c >= 5:
                    place_y = GRID + 1 if cell_y == 0 else 0
                place_z = upper * 4 + c % 5 + 1 if c % 5 < 4 else (1 - upper) * (LAYERS + 1)
                off_y = (place_y - 3) * (CELL * SCALE)
                off_z = (place_z - 5) * (CELL * SCALE)
                off = jnp.where(row == ROW_Y, off_y, jnp.where(row == ROW_Z, off_z, 0.0))
                off = jnp.where(row == ROW_X, off_x, off)
                rows = arrived[8 * cell_x + s, 5 * c : 5 * c + 5]
                block = jnp.concatenate([rows, jnp.zeros((3, 128), F32)]) * scale + off
                out[(cell_x * (GRID + 2) + place_y) * (LAYERS + 2) + place_z] = block
        return carry

    lax.fori_loop(0, GRID, body, 0)


def factors(block, off_x=None):
    row = lax.broadcasted_iota(jnp.int32, (8, 128), 0)
    kind = lax.broadcasted_iota(jnp.int32, (TYPES, 128), 0)
    moved = block if off_x is None else block + jnp.where(row == ROW_X, off_x, 0.0)
    square = jnp.sum(jnp.where(row < 3, moved * moved, 0.0), axis=0, keepdims=True)
    moved = jnp.where(row == ROW_Q, square, jnp.where(row == ROW_ONE, 1.0, moved))
    moved = jnp.where(row == ROW_SOFT, square + SOFT, moved)
    moved = jnp.where(row == ROW_CC, COULOMB * block[ROW_C : ROW_C + 1], moved)
    high = moved.astype(BF16).astype(F32)
    rest = moved - high
    mid = rest.astype(BF16).astype(F32)
    hot = jnp.where(block[ROW_TYPE : ROW_TYPE + 1].astype(jnp.int32) == kind, 1.0, 0.0)
    return jnp.concatenate([hot, high, mid, rest - mid, jnp.zeros((8, 128), F32)]).astype(BF16)


def store_source(places, z, w_src, rx, ry, rr):
    made = jnp.dot(w_src[...], z, preferred_element_type=F32).astype(BF16)
    for g, p in enumerate(places):
        own = made[:, 128 * g : 128 * g + 128]
        rx[p, :, :128] = own[:NX]
        rx[p, :, 128:] = own[NX : 2 * NX]
        rr[p, :, :128] = own[2 * NX : 2 * NX + 16]
        rr[p, :, 128:] = own[2 * NX : 2 * NX + 16]
        at = 2 * NX + 16
        ry[p, :, :128] = own[at : at + NY]
        ry[p, :, 128:] = own[at + NY :]


def store_home(first, z, w_home, lx, ly):
    made = lax.dot_general(z, w_home[...], (((0,), (0,)), ((), ())), preferred_element_type=F32)
    made = made.astype(BF16)
    for g in range(GROUP):
        own = made[128 * g : 128 * g + 128]
        lx[first + g] = own[:, :128]
        ly[first + g] = own[:, 128:]


def all_tiles(first, pairs, ids, lx, ly, rx, ry, rr, acc, buf_a, buf_b):
    def quantities(buf, batch, q):
        h, j = ids[0, batch * BATCH + q], ids[1, batch * BATCH + q]
        buf[q, 0] = jnp.dot(lx[h][:, :NX], rx[j], preferred_element_type=F32)
        buf[q, 1] = jnp.dot(ly[h][:, :NY], ry[j], preferred_element_type=F32)

    def forces(buf, batch, q):
        j, h = ids[1, batch * BATCH + q], ids[2, batch * BATCH + q]

        def part(i, side):
            return buf[q, i, :, 128 * side : 128 * side + 128].reshape(16, 8, 128)

        u = lax.rsqrt(jnp.minimum(part(0, 0), 1.0))
        inv = u * u
        inv3 = inv * inv * inv
        c12, c6, charge = part(1, 0), part(1, 1), part(0, 1)
        push = inv * (inv3 * (inv3 * c12 - c6) + u * charge) - ((c12 - c6) + charge)
        push = push.reshape(128, 128)
        high = push.astype(BF16)
        low = (push - high.astype(F32)).astype(BF16)
        once = lax.dot_general(
            rr[j],
            jnp.concatenate([high, low], 1),
            (((1,), (1,)), ((), ())),
            preferred_element_type=F32,
        )
        acc[h] += once * ids[3, batch * BATCH + q].astype(F32)

    def both(buf_next, buf_now, batch_next, batch_now):
        for q in range(BATCH):
            quantities(buf_next, batch_next, q)
            forces(buf_now, batch_now, q)

    @pl.when(pairs > 0)
    def _():
        last = 2 * (first + pairs) - 1
        for q in range(BATCH):
            quantities(buf_a, 2 * first, q)

        def body(i, carry):
            both(buf_b, buf_a, 2 * i + 1, 2 * i)
            both(buf_a, buf_b, jnp.minimum(2 * i + 2, last), 2 * i + 1)
            return carry

        def twice(i, carry):
            body(first + 2 * i, carry)
            return body(first + 2 * i + 1, carry)

        lax.fori_loop(0, pairs // 2, twice, 0)
        lax.fori_loop(first + pairs // 2 * 2, first + pairs, body, 0)


def near_place(b):
    return (b // (GRID * LAYERS) * (GRID + 2) + b // LAYERS % GRID + 1) * (LAYERS + 2) + b % LAYERS + 1


def near_kernel(steps, ids, region, w_home, w_src, acc, lx, ly, rx, ry, rr, buf_a, buf_b):
    def owned(i, carry):
        first = near_place(i * GROUP)
        places = [first + g for g in range(GROUP)]
        z = jnp.concatenate([factors(region[p]) for p in places], 1)
        store_source(places, z, w_src, rx, ry, rr)
        store_home(i * GROUP, z, w_home, lx, ly)
        return carry

    def rim_place(i):
        side, at = i // 28, i % 28
        place_y = jnp.where(at < 10, 0, jnp.where(at < 20, GRID + 1, 1 + (at - 20) // 2))
        place_z = jnp.where(at < 20, at % 10, (at - 20) % 2 * (LAYERS + 1))
        return (side * (GRID + 2) + place_y) * (LAYERS + 2) + place_z

    def rim(i, carry):
        places = [rim_place(i * GROUP + g) for g in range(GROUP)]
        z = jnp.concatenate([factors(region[p]) for p in places], 1)
        store_source(places, z, w_src, rx, ry, rr)
        return carry

    lax.fori_loop(0, 128 // GROUP, owned, 0, unroll=4)
    lax.fori_loop(0, 112 // GROUP, rim, 0, unroll=7)
    acc[...] = jnp.zeros_like(acc)
    all_tiles(0, steps[0], ids, lx, ly, rx, ry, rr, acc, buf_a, buf_b)


def far_kernel(steps, ids, low, high, region, w_src, lx, ly, acc, out, acc_out, rx, ry, rr, buf_a, buf_b):
    def prepare(i, carry):
        for k, (plane, off_x) in enumerate(((low, -44.0), (high, 44.0))):
            places = [i * FAR_GROUP + g for g in range(FAR_GROUP)]
            z = jnp.concatenate([factors(plane[p], off_x * SCALE) for p in places], 1)
            store_source([p + 60 * k for p in places], z, w_src, rx, ry, rr)
        return carry

    lax.fori_loop(0, 60 // FAR_GROUP, prepare, 0, unroll=2)
    all_tiles(steps[0], steps[1], ids, lx, ly, rx, ry, rr, acc_out, buf_a, buf_b)

    def finish(s, carry):
        first = near_place(4 * s)
        for k in range(4):
            sums = acc_out[4 * s + k]
            head, tail = sums[:8], sums[8:]
            weighed = head + pltpu.roll(head, 4, 0) + tail
            out[s, 3 * k : 3 * k + 3] = (region[first + k] * head[3:4] - weighed)[:3]
        return carry

    lax.fori_loop(0, 32, finish, 0, unroll=4)


def tile_lists(tiles, blocks):
    home, source = tiles[0], tiles[1]
    slot, member = source // blocks, source % blocks
    step_x = slot // 9 - 1
    place_y = member // LAYERS % GRID + (slot // 3 % 3 - 1) * GRID + 1
    place_z = member % LAYERS + (slot % 3 - 1) * LAYERS + 1
    plane = place_y * (LAYERS + 2) + place_z
    side = jnp.where(step_x == 0, member // (GRID * LAYERS), (step_x + 1) // 2)
    listed = home >= 0
    unit = 2 * BATCH
    order = jnp.arange(home.shape[0])
    upto = order[None, :] <= order[:, None]
    key = home * (27 * blocks) + source
    same = key[None, :] == key[:, None]
    times = jnp.sum(jnp.where(same, 1, 0), 1)
    first = jnp.sum(jnp.where(same & upto, 1, 0), 1) == 1
    near = listed & first & (step_x == 0)
    far = listed & first & (step_x != 0)
    near_at = jnp.sum(jnp.where(upto & near[None, :], 1, 0), 1)
    far_at = jnp.sum(jnp.where(upto & far[None, :], 1, 0), 1)
    near_steps = (jnp.sum(near.astype(jnp.int32)) + unit - 1) // unit
    far_steps = (jnp.sum(far.astype(jnp.int32)) + unit - 1) // unit
    at = jnp.where(near, near_at - 1, jnp.where(far, near_steps * unit + far_at - 1, -1))
    code = home * 256 + side * 60 + plane + 1
    slots = jnp.arange(home.shape[0] + 2 * unit)
    found = jnp.sum(jnp.where(slots[:, None] == at[None, :], code[None, :], 0), 1)
    times = jnp.sum(jnp.where(slots[:, None] == at[None, :], times[None, :], 0), 1)
    real = found > 0
    code = jnp.maximum(found - 1, 0)
    ids = jnp.stack([code // 256, code % 256, jnp.where(real, code // 256, blocks), times])
    return jnp.stack([near_steps, far_steps]), ids


def per_device(coords, charges, atom_types, lj_sigma, lj_epsilon, tile_list):
    blocks, width = coords.shape[2], coords.shape[3]
    peers = lax.axis_size("gy") * lax.axis_size("gz")
    vmem = pl.BlockSpec(memory_space=pltpu.VMEM)
    smem = pl.BlockSpec(memory_space=pltpu.SMEM)
    gz = lax.axis_index("gz")
    small = pltpu.CompilerParams(vmem_limit_bytes=8 << 20)
    outgoing = pl.pallas_call(
        pack_kernel,
        out_shape=jax.ShapeDtypeStruct((peers * SENT, width), F32),
        in_specs=[smem, smem] + [pl.BlockSpec(memory_space=pl.ANY)] * 3,
        out_specs=vmem,
        scratch_shapes=[
            pltpu.VMEM((3, blocks, width), F32),
            pltpu.VMEM((blocks, width), F32),
            pltpu.VMEM((blocks, width), jnp.int32),
            pltpu.SemaphoreType.DMA((3,)),
        ],
        compiler_params=pltpu.CompilerParams(vmem_limit_bytes=65011712),
    )((gz % 2).reshape(1), (gz // 2).reshape(1), coords[:, 0], charges[0], atom_types[0])
    arrived = lax.all_to_all(
        outgoing.reshape(peers, SENT, width), ("gy", "gz"), split_axis=0, concat_axis=0, tiled=True
    )
    steps, ids = tile_lists(tile_list[0, 0, 0], blocks)
    w_home, w_src = weights(lj_sigma, lj_epsilon)
    region = pl.pallas_call(
        unpack_kernel,
        out_shape=jax.ShapeDtypeStruct((NEAR, 8, width), F32),
        in_specs=[vmem],
        out_specs=vmem,
        compiler_params=small,
    )(arrived)
    count = lax.axis_size("gx")
    forward = [(i, (i + 1) % count) for i in range(count)]
    backward = [(target, source) for source, target in forward]
    low = lax.ppermute(region[180:240], "gx", forward)
    high = lax.ppermute(region[:60], "gx", backward)

    def source_scratch(n):
        return [
            pltpu.VMEM((n, NX, 256), BF16),
            pltpu.VMEM((n, NY, 256), BF16),
            pltpu.VMEM((n, 16, 256), BF16),
            pltpu.VMEM((BATCH, 2, 128, 256), F32),
            pltpu.VMEM((BATCH, 2, 128, 256), F32),
        ]

    acc_shape = jax.ShapeDtypeStruct((blocks + 1, 16, width), F32)
    factor_shape = jax.ShapeDtypeStruct((blocks, 128, 128), BF16)
    acc, lx, ly = pl.pallas_call(
        near_kernel,
        out_shape=[acc_shape, factor_shape, factor_shape],
        in_specs=[smem, smem, vmem, vmem, vmem],
        out_specs=[vmem] * 3,
        scratch_shapes=source_scratch(NEAR),
        compiler_params=pltpu.CompilerParams(vmem_limit_bytes=28 << 20),
        cost_estimate=pl.CostEstimate(flops=10**10, bytes_accessed=10**7, transcendentals=10**6),
    )(steps, ids, region, w_home, w_src)
    totals, _ = pl.pallas_call(
        far_kernel,
        out_shape=[jax.ShapeDtypeStruct((peers, 12, width), F32), acc_shape],
        in_specs=[smem, smem] + [vmem] * 7,
        out_specs=[vmem] * 2,
        scratch_shapes=source_scratch(120),
        input_output_aliases={8: 1},
        compiler_params=pltpu.CompilerParams(vmem_limit_bytes=24 << 20),
    )(steps, ids, low, high, region, w_src, lx, ly, acc)
    back = lax.all_to_all(totals, ("gy", "gz"), split_axis=0, concat_axis=0, tiled=True)
    return back.reshape(peers, 4, 3, width).transpose(2, 1, 0, 3).reshape(3, 1, blocks, width)


def solution(mesh):
    return jax.shard_map(
        per_device,
        mesh=mesh,
        in_specs=(
            P(None, "gx", ("gy", "gz"), None),
            P("gx", ("gy", "gz"), None),
            P("gx", ("gy", "gz"), None),
            P(),
            P(),
            P("gx", "gy", "gz", None, None),
        ),
        out_specs=P(None, "gx", ("gy", "gz"), None),
        check_vma=False,
    )
```

```python
import math

import jax
import jax.numpy as jnp
import numpy as np
from jax import lax
from jax.experimental import pallas as pl
from jax.experimental.pallas import tpu as pltpu
from jax.sharding import PartitionSpec as P

F32 = jnp.float32
BF16 = jnp.bfloat16

GRID = 4
LAYERS = 8
CELL = 11.0
LIMIT = 97.0
SCALE = LIMIT**-0.5
SOFT = 16.0 / LIMIT
COULOMB = 332.0636 / LIMIT
FACTOR_12 = 48.0 * LIMIT**-6.5
FACTOR_6 = 24.0 * LIMIT**-3.5

ROW_X, ROW_Y, ROW_Z, ROW_C, ROW_TYPE, ROW_Q, ROW_ONE, ROW_CC = range(8)
ROW_SOFT = ROW_TYPE
TYPES = 64
ORDER = 13
NX = 32
NY = 48
NZ = TYPES + 32
BATCH = 4
SIZES = (4, 2, 1)
GROUP = 8
FAR_GROUP = 10
NEAR = 240
SENT = 56


def placements():
    home = np.zeros((32, NX), np.float32)
    src_w = np.zeros((NX, 32), np.float32)
    src_c = np.zeros((NX, 32), np.float32)
    at = 0

    def term(row, part):
        return part * 8 + row

    for row in (ROW_X, ROW_Y, ROW_Z):
        for i, j in ((0, 0), (0, 1), (1, 0), (1, 1), (0, 2), (2, 0)):
            home[term(row, i), at] = 1.0
            src_w[at, term(row, j)] = -2.0
            at += 1
    for part in range(3):
        home[term(ROW_SOFT, part), at] = 1.0
        src_w[at, term(ROW_ONE, 0)] = 1.0
        at += 1
    for part in range(3):
        home[term(ROW_ONE, 0), at] = 1.0
        src_w[at, term(ROW_Q, part)] = 1.0
        at += 1
    for i, j in ((0, 0), (0, 1), (1, 0), (1, 1), (0, 2), (2, 0)):
        home[term(ROW_CC, i), at] = 1.0
        src_c[at, term(ROW_C, j)] = 1.0
        at += 1
    place_r = np.zeros((16, 32), np.float32)
    for k, row in enumerate((ROW_X, ROW_Y, ROW_Z)):
        for part in range(3):
            place_r[4 * part + k, term(row, part)] = 1.0
    place_r[3, term(ROW_ONE, 0)] = 1.0
    return home, src_w, src_c, place_r


def weights(lj_sigma, lj_epsilon):
    root = jnp.sqrt(lj_epsilon)
    half = 0.5 * lj_sigma
    powers = [jnp.ones_like(half)]
    for _ in range(ORDER - 1):
        powers.append(powers[-1] * half)

    def halves(table):
        high = lax.reduce_precision(table, 8, 7)
        return high, table - high

    h_high, h_low = halves(jnp.stack([root * p for p in powers]))
    zero = jnp.zeros_like(half)
    p12 = jnp.stack([root * powers[12 - k] * (FACTOR_12 * math.comb(12, k)) for k in range(ORDER)])
    p6 = jnp.stack(
        [root * powers[6 - k] * (FACTOR_6 * math.comb(6, k)) if k <= 6 else zero for k in range(ORDER)]
    )
    pad = jnp.zeros((NY - 3 * ORDER, TYPES), F32)
    home_y = jnp.concatenate([h_high, h_high, h_low, pad])
    src_y = []
    for table in (p12, p6):
        high, low = halves(table)
        src_y += [high, low, high, pad]
    home_x, src_w, src_c, place_r = placements()
    home_x = np.pad(home_x, ((TYPES, 0), (0, 128 - NX)))
    home = jnp.concatenate([home_x, jnp.pad(home_y.T, ((0, NZ - TYPES), (0, 128 - NY)))], 1)
    fixed = jnp.concatenate([jnp.zeros((2 * NX + 16, TYPES)), np.concatenate([src_w, src_c, place_r])], 1)
    lj = jnp.concatenate([jnp.concatenate(src_y), jnp.zeros((2 * NY, 32), F32)], 1)
    source = jnp.concatenate([fixed, lj])
    return home.astype(BF16), source.astype(BF16)


def pack_kernel(half_hi, side, coords_in, charges_in, types_in, out, coords, charges, types, sems):
    copies = [
        pltpu.make_async_copy(source, target, sems.at[i])
        for i, (source, target) in enumerate(
            ((coords_in, coords), (charges_in, charges), (types_in, types))
        )
    ]
    for copy in copies:
        copy.start()
    for copy in copies:
        copy.wait()
    upper = half_hi[0] == 1
    back_y = side[0] == 3
    kinds = types[...].astype(F32)

    def next_y(value):
        ahead = jnp.concatenate([value[8:], value[:8]])
        behind = jnp.concatenate([value[24:], value[:24]])
        return jnp.where(back_y, behind, ahead)

    for q in range(5):
        for cell in range(5):

            def rows(k):
                if q < 3:
                    return coords[q, 32 * k : 32 * k + 32]
                return charges[32 * k : 32 * k + 32] if q == 3 else kinds[32 * k : 32 * k + 32]

            if cell < 4:
                value = rows(cell)
            else:
                ahead = pltpu.roll(rows(0).reshape(4, 8, 128), 7, 1)
                behind = pltpu.roll(rows(3).reshape(4, 8, 128), 1, 1)
                value = jnp.where(upper, behind, ahead).reshape(32, 128)
            out[pl.ds(5 * cell + q, 32, stride=SENT), :] = value
            out[pl.ds(25 + 5 * cell + q, 32, stride=SENT), :] = next_y(value)


def unpack_kernel(arrived, out):
    row = lax.broadcasted_iota(jnp.int32, (8, 128), 0)
    scale = jnp.where(row < 3, SCALE, 1.0)

    def body(cell_x, carry):
        off_x = (cell_x.astype(F32) - 2) * (CELL * SCALE)
        for s in range(8):
            cell_y, upper = s // 2, s % 2
            for c in range(10 if cell_y in (0, GRID - 1) else 5):
                place_y = cell_y + 1
                if c >= 5:
                    place_y = GRID + 1 if cell_y == 0 else 0
                place_z = upper * 4 + c % 5 + 1 if c % 5 < 4 else (1 - upper) * (LAYERS + 1)
                off_y = (place_y - 3) * (CELL * SCALE)
                off_z = (place_z - 5) * (CELL * SCALE)
                off = jnp.where(row == ROW_Y, off_y, jnp.where(row == ROW_Z, off_z, 0.0))
                off = jnp.where(row == ROW_X, off_x, off)
                rows = arrived[8 * cell_x + s, 5 * c : 5 * c + 5]
                block = jnp.concatenate([rows, jnp.zeros((3, 128), F32)]) * scale + off
                out[(cell_x * (GRID + 2) + place_y) * (LAYERS + 2) + place_z] = block
        return carry

    lax.fori_loop(0, GRID, body, 0)


def factors(block, off_x=None):
    row = lax.broadcasted_iota(jnp.int32, (8, 128), 0)
    kind = lax.broadcasted_iota(jnp.int32, (TYPES, 128), 0)
    moved = block if off_x is None else block + jnp.where(row == ROW_X, off_x, 0.0)
    square = jnp.sum(jnp.where(row < 3, moved * moved, 0.0), axis=0, keepdims=True)
    moved = jnp.where(row == ROW_Q, square, jnp.where(row == ROW_ONE, 1.0, moved))
    moved = jnp.where(row == ROW_SOFT, square + SOFT, moved)
    moved = jnp.where(row == ROW_CC, COULOMB * block[ROW_C : ROW_C + 1], moved)
    high = moved.astype(BF16).astype(F32)
    rest = moved - high
    mid = rest.astype(BF16).astype(F32)
    hot = jnp.where(block[ROW_TYPE : ROW_TYPE + 1].astype(jnp.int32) == kind, 1.0, 0.0)
    return jnp.concatenate([hot, high, mid, rest - mid, jnp.zeros((8, 128), F32)]).astype(BF16)


def store_source(places, z, w_src, rx, ry, rr):
    made = jnp.dot(w_src[...], z, preferred_element_type=F32).astype(BF16)
    for g, p in enumerate(places):
        own = made[:, 128 * g : 128 * g + 128]
        rx[p, :, :128] = own[:NX]
        rx[p, :, 128:] = own[NX : 2 * NX]
        rr[p, :, :128] = own[2 * NX : 2 * NX + 16]
        rr[p, :, 128:] = own[2 * NX : 2 * NX + 16]
        at = 2 * NX + 16
        ry[p, :, :128] = own[at : at + NY]
        ry[p, :, 128:] = own[at + NY :]


def store_home(first, z, w_home, lx, ly):
    made = lax.dot_general(z, w_home[...], (((0,), (0,)), ((), ())), preferred_element_type=F32)
    made = made.astype(BF16)
    for g in range(GROUP):
        own = made[128 * g : 128 * g + 128]
        lx[first + g] = own[:, :128]
        ly[first + g] = own[:, 128:]


def all_tiles(first, pairs, ids, lx, ly, rx, ry, rr, acc, buf_a, buf_b):
    def quantities(buf, batch, q):
        h, j = ids[0, batch * BATCH + q], ids[1, batch * BATCH + q]
        buf[q, 0] = jnp.dot(lx[h][:, :NX], rx[j], preferred_element_type=F32)
        buf[q, 1] = jnp.dot(ly[h][:, :NY], ry[j], preferred_element_type=F32)

    def forces(buf, batch, q):
        j, h = ids[1, batch * BATCH + q], ids[2, batch * BATCH + q]

        def part(i, side):
            return buf[q, i, :, 128 * side : 128 * side + 128].reshape(16, 8, 128)

        u = lax.rsqrt(jnp.minimum(part(0, 0), 1.0))
        inv = u * u
        inv3 = inv * inv * inv
        c12, c6, charge = part(1, 0), part(1, 1), part(0, 1)
        push = inv * (inv3 * (inv3 * c12 - c6) + u * charge) - ((c12 - c6) + charge)
        push = push.reshape(128, 128)
        high = push.astype(BF16)
        low = (push - high.astype(F32)).astype(BF16)
        once = lax.dot_general(
            rr[j],
            jnp.concatenate([high, low], 1),
            (((1,), (1,)), ((), ())),
            preferred_element_type=F32,
        )
        acc[h] += once * ids[3, batch * BATCH + q].astype(F32)

    def both(buf_next, buf_now, batch_next, batch_now):
        for q in range(BATCH):
            quantities(buf_next, batch_next, q)
            forces(buf_now, batch_now, q)

    @pl.when(pairs > 0)
    def _():
        last = 2 * (first + pairs) - 1
        for q in range(BATCH):
            quantities(buf_a, 2 * first, q)

        def body(i, carry):
            both(buf_b, buf_a, 2 * i + 1, 2 * i)
            both(buf_a, buf_b, jnp.minimum(2 * i + 2, last), 2 * i + 1)
            return carry

        at = first
        for size in SIZES:

            def several(i, carry, size=size, at=at):
                for k in range(size):
                    body(at + i * size + k, carry)
                return carry

            steps = (first + pairs - at) // size
            lax.fori_loop(0, steps, several, 0)
            at = at + steps * size


def near_place(b):
    return (b // (GRID * LAYERS) * (GRID + 2) + b // LAYERS % GRID + 1) * (LAYERS + 2) + b % LAYERS + 1


def near_kernel(steps, ids, region, w_home, w_src, acc, lx, ly, rx, ry, rr, buf_a, buf_b):
    def owned(i, carry):
        first = near_place(i * GROUP)
        places = [first + g for g in range(GROUP)]
        z = jnp.concatenate([factors(region[p]) for p in places], 1)
        store_source(places, z, w_src, rx, ry, rr)
        store_home(i * GROUP, z, w_home, lx, ly)
        return carry

    def rim_place(i):
        side, at = i // 28, i % 28
        place_y = jnp.where(at < 10, 0, jnp.where(at < 20, GRID + 1, 1 + (at - 20) // 2))
        place_z = jnp.where(at < 20, at % 10, (at - 20) % 2 * (LAYERS + 1))
        return (side * (GRID + 2) + place_y) * (LAYERS + 2) + place_z

    def rim(i, carry):
        places = [rim_place(i * GROUP + g) for g in range(GROUP)]
        z = jnp.concatenate([factors(region[p]) for p in places], 1)
        store_source(places, z, w_src, rx, ry, rr)
        return carry

    lax.fori_loop(0, 128 // GROUP, owned, 0, unroll=8)
    lax.fori_loop(0, 112 // GROUP, rim, 0, unroll=14)
    acc[...] = jnp.zeros_like(acc)
    all_tiles(0, steps[0], ids, lx, ly, rx, ry, rr, acc, buf_a, buf_b)


def far_kernel(steps, ids, low, high, region, w_src, lx, ly, acc, out, acc_out, rx, ry, rr, buf_a, buf_b):
    def prepare(i, carry):
        for k, (plane, off_x) in enumerate(((low, -44.0), (high, 44.0))):
            places = [i * FAR_GROUP + g for g in range(FAR_GROUP)]
            z = jnp.concatenate([factors(plane[p], off_x * SCALE) for p in places], 1)
            store_source([p + 60 * k for p in places], z, w_src, rx, ry, rr)
        return carry

    lax.fori_loop(0, 60 // FAR_GROUP, prepare, 0, unroll=6)
    all_tiles(steps[0], steps[1], ids, lx, ly, rx, ry, rr, acc_out, buf_a, buf_b)

    def finish(s, carry):
        first = near_place(4 * s)
        for k in range(4):
            sums = acc_out[4 * s + k]
            head, tail = sums[:8], sums[8:]
            weighed = head + pltpu.roll(head, 4, 0) + tail
            out[s, 3 * k : 3 * k + 3] = (region[first + k] * head[3:4] - weighed)[:3]
        return carry

    lax.fori_loop(0, 32, finish, 0, unroll=4)


def tile_lists(tiles, blocks):
    home, source = tiles[0], tiles[1]
    slot, member = source // blocks, source % blocks
    step_x = slot // 9 - 1
    place_y = member // LAYERS % GRID + (slot // 3 % 3 - 1) * GRID + 1
    place_z = member % LAYERS + (slot % 3 - 1) * LAYERS + 1
    plane = place_y * (LAYERS + 2) + place_z
    side = jnp.where(step_x == 0, member // (GRID * LAYERS), (step_x + 1) // 2)
    listed = home >= 0
    unit = 2 * BATCH
    order = jnp.arange(home.shape[0])
    upto = order[None, :] <= order[:, None]
    key = home * (27 * blocks) + source
    same = key[None, :] == key[:, None]
    times = jnp.sum(jnp.where(same, 1, 0), 1)
    first = jnp.sum(jnp.where(same & upto, 1, 0), 1) == 1
    near = listed & first & (step_x == 0)
    far = listed & first & (step_x != 0)
    near_at = jnp.sum(jnp.where(upto & near[None, :], 1, 0), 1)
    far_at = jnp.sum(jnp.where(upto & far[None, :], 1, 0), 1)
    near_steps = (jnp.sum(near.astype(jnp.int32)) + unit - 1) // unit
    far_steps = (jnp.sum(far.astype(jnp.int32)) + unit - 1) // unit
    at = jnp.where(near, near_at - 1, jnp.where(far, near_steps * unit + far_at - 1, -1))
    code = home * 256 + side * 60 + plane + 1
    slots = jnp.arange(home.shape[0] + 2 * unit)
    found = jnp.sum(jnp.where(slots[:, None] == at[None, :], code[None, :], 0), 1)
    times = jnp.sum(jnp.where(slots[:, None] == at[None, :], times[None, :], 0), 1)
    real = found > 0
    code = jnp.maximum(found - 1, 0)
    ids = jnp.stack([code // 256, code % 256, jnp.where(real, code // 256, blocks), times])
    return jnp.stack([near_steps, far_steps]), ids


def per_device(coords, charges, atom_types, lj_sigma, lj_epsilon, tile_list):
    blocks, width = coords.shape[2], coords.shape[3]
    peers = lax.axis_size("gy") * lax.axis_size("gz")
    vmem = pl.BlockSpec(memory_space=pltpu.VMEM)
    smem = pl.BlockSpec(memory_space=pltpu.SMEM)
    gz = lax.axis_index("gz")
    small = pltpu.CompilerParams(vmem_limit_bytes=8 << 20)
    outgoing = pl.pallas_call(
        pack_kernel,
        out_shape=jax.ShapeDtypeStruct((peers * SENT, width), F32),
        in_specs=[smem, smem] + [pl.BlockSpec(memory_space=pl.ANY)] * 3,
        out_specs=vmem,
        scratch_shapes=[
            pltpu.VMEM((3, blocks, width), F32),
            pltpu.VMEM((blocks, width), F32),
            pltpu.VMEM((blocks, width), jnp.int32),
            pltpu.SemaphoreType.DMA((3,)),
        ],
        compiler_params=pltpu.CompilerParams(vmem_limit_bytes=65011712),
    )((gz % 2).reshape(1), (gz // 2).reshape(1), coords[:, 0], charges[0], atom_types[0])
    arrived = lax.all_to_all(
        outgoing.reshape(peers, SENT, width), ("gy", "gz"), split_axis=0, concat_axis=0, tiled=True
    )
    steps, ids = tile_lists(tile_list[0, 0, 0], blocks)
    w_home, w_src = weights(lj_sigma, lj_epsilon)
    region = pl.pallas_call(
        unpack_kernel,
        out_shape=jax.ShapeDtypeStruct((NEAR, 8, width), F32),
        in_specs=[vmem],
        out_specs=vmem,
        compiler_params=small,
    )(arrived)
    count = lax.axis_size("gx")
    forward = [(i, (i + 1) % count) for i in range(count)]
    backward = [(target, source) for source, target in forward]
    low = lax.ppermute(region[180:240], "gx", forward)
    high = lax.ppermute(region[:60], "gx", backward)

    def source_scratch(n):
        return [
            pltpu.VMEM((n, NX, 256), BF16),
            pltpu.VMEM((n, NY, 256), BF16),
            pltpu.VMEM((n, 16, 256), BF16),
            pltpu.VMEM((BATCH, 2, 128, 256), F32),
            pltpu.VMEM((BATCH, 2, 128, 256), F32),
        ]

    acc_shape = jax.ShapeDtypeStruct((blocks + 1, 16, width), F32)
    factor_shape = jax.ShapeDtypeStruct((blocks, 128, 128), BF16)
    acc, lx, ly = pl.pallas_call(
        near_kernel,
        out_shape=[acc_shape, factor_shape, factor_shape],
        in_specs=[smem, smem, vmem, vmem, vmem],
        out_specs=[vmem] * 3,
        scratch_shapes=source_scratch(NEAR),
        compiler_params=pltpu.CompilerParams(vmem_limit_bytes=28 << 20),
        cost_estimate=pl.CostEstimate(flops=10**10, bytes_accessed=10**7, transcendentals=10**6),
    )(steps, ids, region, w_home, w_src)
    totals, _ = pl.pallas_call(
        far_kernel,
        out_shape=[jax.ShapeDtypeStruct((peers, 12, width), F32), acc_shape],
        in_specs=[smem, smem] + [vmem] * 7,
        out_specs=[vmem] * 2,
        scratch_shapes=source_scratch(120),
        input_output_aliases={8: 1},
        compiler_params=pltpu.CompilerParams(vmem_limit_bytes=24 << 20),
    )(steps, ids, low, high, region, w_src, lx, ly, acc)
    back = lax.all_to_all(totals, ("gy", "gz"), split_axis=0, concat_axis=0, tiled=True)
    return back.reshape(peers, 4, 3, width).transpose(2, 1, 0, 3).reshape(3, 1, blocks, width)


def solution(mesh):
    return jax.shard_map(
        per_device,
        mesh=mesh,
        in_specs=(
            P(None, "gx", ("gy", "gz"), None),
            P("gx", ("gy", "gz"), None),
            P("gx", ("gy", "gz"), None),
            P(),
            P(),
            P("gx", "gy", "gz", None, None),
        ),
        out_specs=P(None, "gx", ("gy", "gz"), None),
        check_vma=False,
    )
```

```python
import math

import jax
import jax.numpy as jnp
import numpy as np
from jax import lax
from jax.experimental import pallas as pl
from jax.experimental.pallas import tpu as pltpu
from jax.sharding import PartitionSpec as P

F32 = jnp.float32
BF16 = jnp.bfloat16

GRID = 4
LAYERS = 8
CELL = 11.0
LIMIT = 97.0
SCALE = LIMIT**-0.5
SOFT = 16.0 / LIMIT
COULOMB = 332.0636 / LIMIT
FACTOR_12 = 48.0 * LIMIT**-6.5
FACTOR_6 = 24.0 * LIMIT**-3.5

ROW_X, ROW_Y, ROW_Z, ROW_C, ROW_TYPE, ROW_Q, ROW_ONE, ROW_CC = range(8)
ROW_SOFT = ROW_TYPE
TYPES = 64
ORDER = 13
NX = 32
NY = 48
NZ = TYPES + 32
BATCH = 4
NEAR_SIZES = (8, 4, 2, 1)
FAR_SIZES = (4, 2, 1)
GROUP = 8
FAR_GROUP = 10
NEAR = 240
SENT = 56


def placements():
    home = np.zeros((32, NX), np.float32)
    src_w = np.zeros((NX, 32), np.float32)
    src_c = np.zeros((NX, 32), np.float32)
    at = 0

    def term(row, part):
        return part * 8 + row

    for row in (ROW_X, ROW_Y, ROW_Z):
        for i, j in ((0, 0), (0, 1), (1, 0), (1, 1), (0, 2), (2, 0)):
            home[term(row, i), at] = 1.0
            src_w[at, term(row, j)] = -2.0
            at += 1
    for part in range(3):
        home[term(ROW_SOFT, part), at] = 1.0
        src_w[at, term(ROW_ONE, 0)] = 1.0
        at += 1
    for part in range(3):
        home[term(ROW_ONE, 0), at] = 1.0
        src_w[at, term(ROW_Q, part)] = 1.0
        at += 1
    for i, j in ((0, 0), (0, 1), (1, 0), (1, 1), (0, 2), (2, 0)):
        home[term(ROW_CC, i), at] = 1.0
        src_c[at, term(ROW_C, j)] = 1.0
        at += 1
    place_r = np.zeros((16, 32), np.float32)
    for k, row in enumerate((ROW_X, ROW_Y, ROW_Z)):
        for part in range(3):
            place_r[4 * part + k, term(row, part)] = 1.0
    place_r[3, term(ROW_ONE, 0)] = 1.0
    return home, src_w, src_c, place_r


def weights(lj_sigma, lj_epsilon):
    root = jnp.sqrt(lj_epsilon)
    half = 0.5 * lj_sigma
    powers = [jnp.ones_like(half)]
    for _ in range(ORDER - 1):
        powers.append(powers[-1] * half)

    def halves(table):
        high = lax.reduce_precision(table, 8, 7)
        return high, table - high

    h_high, h_low = halves(jnp.stack([root * p for p in powers]))
    zero = jnp.zeros_like(half)
    p12 = jnp.stack([root * powers[12 - k] * (FACTOR_12 * math.comb(12, k)) for k in range(ORDER)])
    p6 = jnp.stack(
        [root * powers[6 - k] * (FACTOR_6 * math.comb(6, k)) if k <= 6 else zero for k in range(ORDER)]
    )
    pad = jnp.zeros((NY - 3 * ORDER, TYPES), F32)
    home_y = jnp.concatenate([h_high, h_high, h_low, pad])
    src_y = []
    for table in (p12, p6):
        high, low = halves(table)
        src_y += [high, low, high, pad]
    home_x, src_w, src_c, place_r = placements()
    home_x = np.pad(home_x, ((TYPES, 0), (0, 128 - NX)))
    home = jnp.concatenate([home_x, jnp.pad(home_y.T, ((0, NZ - TYPES), (0, 128 - NY)))], 1)
    fixed = jnp.concatenate([jnp.zeros((2 * NX + 16, TYPES)), np.concatenate([src_w, src_c, place_r])], 1)
    lj = jnp.concatenate([jnp.concatenate(src_y), jnp.zeros((2 * NY, 32), F32)], 1)
    source = jnp.concatenate([fixed, lj])
    return home.astype(BF16), source.astype(BF16)


def pack_kernel(half_hi, side, coords_in, charges_in, types_in, out, coords, charges, types, sems):
    copies = [
        pltpu.make_async_copy(source, target, sems.at[i])
        for i, (source, target) in enumerate(
            ((coords_in, coords), (charges_in, charges), (types_in, types))
        )
    ]
    for copy in copies:
        copy.start()
    for copy in copies:
        copy.wait()
    upper = half_hi[0] == 1
    back_y = side[0] == 3
    kinds = types[...].astype(F32)

    def next_y(value):
        ahead = jnp.concatenate([value[8:], value[:8]])
        behind = jnp.concatenate([value[24:], value[:24]])
        return jnp.where(back_y, behind, ahead)

    for q in range(5):
        for cell in range(5):

            def rows(k):
                if q < 3:
                    return coords[q, 32 * k : 32 * k + 32]
                return charges[32 * k : 32 * k + 32] if q == 3 else kinds[32 * k : 32 * k + 32]

            if cell < 4:
                value = rows(cell)
            else:
                ahead = pltpu.roll(rows(0).reshape(4, 8, 128), 7, 1)
                behind = pltpu.roll(rows(3).reshape(4, 8, 128), 1, 1)
                value = jnp.where(upper, behind, ahead).reshape(32, 128)
            out[pl.ds(5 * cell + q, 32, stride=SENT), :] = value
            out[pl.ds(25 + 5 * cell + q, 32, stride=SENT), :] = next_y(value)


def unpack_kernel(arrived, out):
    row = lax.broadcasted_iota(jnp.int32, (8, 128), 0)
    scale = jnp.where(row < 3, SCALE, 1.0)

    def body(cell_x, carry):
        off_x = (cell_x.astype(F32) - 2) * (CELL * SCALE)
        for s in range(8):
            cell_y, upper = s // 2, s % 2
            for c in range(10 if cell_y in (0, GRID - 1) else 5):
                place_y = cell_y + 1
                if c >= 5:
                    place_y = GRID + 1 if cell_y == 0 else 0
                place_z = upper * 4 + c % 5 + 1 if c % 5 < 4 else (1 - upper) * (LAYERS + 1)
                off_y = (place_y - 3) * (CELL * SCALE)
                off_z = (place_z - 5) * (CELL * SCALE)
                off = jnp.where(row == ROW_Y, off_y, jnp.where(row == ROW_Z, off_z, 0.0))
                off = jnp.where(row == ROW_X, off_x, off)
                rows = arrived[8 * cell_x + s, 5 * c : 5 * c + 5]
                block = jnp.concatenate([rows, jnp.zeros((3, 128), F32)]) * scale + off
                out[(cell_x * (GRID + 2) + place_y) * (LAYERS + 2) + place_z] = block
        return carry

    lax.fori_loop(0, GRID, body, 0)


def factors(block, off_x=None):
    row = lax.broadcasted_iota(jnp.int32, (8, 128), 0)
    kind = lax.broadcasted_iota(jnp.int32, (TYPES, 128), 0)
    moved = block if off_x is None else block + jnp.where(row == ROW_X, off_x, 0.0)
    square = jnp.sum(jnp.where(row < 3, moved * moved, 0.0), axis=0, keepdims=True)
    moved = jnp.where(row == ROW_Q, square, jnp.where(row == ROW_ONE, 1.0, moved))
    moved = jnp.where(row == ROW_SOFT, square + SOFT, moved)
    moved = jnp.where(row == ROW_CC, COULOMB * block[ROW_C : ROW_C + 1], moved)
    high = moved.astype(BF16).astype(F32)
    rest = moved - high
    mid = rest.astype(BF16).astype(F32)
    hot = jnp.where(block[ROW_TYPE : ROW_TYPE + 1].astype(jnp.int32) == kind, 1.0, 0.0)
    return jnp.concatenate([hot, high, mid, rest - mid, jnp.zeros((8, 128), F32)]).astype(BF16)


def store_source(places, z, w_src, rx, ry, rr):
    made = jnp.dot(w_src[...], z, preferred_element_type=F32).astype(BF16)
    for g, p in enumerate(places):
        own = made[:, 128 * g : 128 * g + 128]
        rx[p, :, :128] = own[:NX]
        rx[p, :, 128:] = own[NX : 2 * NX]
        rr[p, :, :128] = own[2 * NX : 2 * NX + 16]
        rr[p, :, 128:] = own[2 * NX : 2 * NX + 16]
        at = 2 * NX + 16
        ry[p, :, :128] = own[at : at + NY]
        ry[p, :, 128:] = own[at + NY :]


def store_home(first, z, w_home, lx, ly):
    made = lax.dot_general(z, w_home[...], (((0,), (0,)), ((), ())), preferred_element_type=F32)
    made = made.astype(BF16)
    for g in range(GROUP):
        own = made[128 * g : 128 * g + 128]
        lx[first + g] = own[:, :128]
        ly[first + g] = own[:, 128:]


def all_tiles(sizes, first, pairs, ids, lx, ly, rx, ry, rr, acc, buf_a, buf_b):
    def quantities(buf, batch, q):
        h, j = ids[0, batch * BATCH + q], ids[1, batch * BATCH + q]
        buf[q, 0] = jnp.dot(lx[h][:, :NX], rx[j], preferred_element_type=F32)
        buf[q, 1] = jnp.dot(ly[h][:, :NY], ry[j], preferred_element_type=F32)

    def forces(buf, batch, q):
        j, h = ids[1, batch * BATCH + q], ids[2, batch * BATCH + q]

        def part(i, side):
            return buf[q, i, :, 128 * side : 128 * side + 128].reshape(16, 8, 128)

        u = lax.rsqrt(jnp.minimum(part(0, 0), 1.0))
        inv = u * u
        inv3 = inv * inv * inv
        c12, c6, charge = part(1, 0), part(1, 1), part(0, 1)
        push = inv * (inv3 * (inv3 * c12 - c6) + u * charge) - ((c12 - c6) + charge)
        push = push.reshape(128, 128)
        high = push.astype(BF16)
        low = (push - high.astype(F32)).astype(BF16)
        once = lax.dot_general(
            rr[j],
            jnp.concatenate([high, low], 1),
            (((1,), (1,)), ((), ())),
            preferred_element_type=F32,
        )
        acc[h] += once * ids[3, batch * BATCH + q].astype(F32)

    def both(buf_next, buf_now, batch_next, batch_now):
        for q in range(BATCH):
            quantities(buf_next, batch_next, q)
            forces(buf_now, batch_now, q)

    @pl.when(pairs > 0)
    def _():
        last = 2 * (first + pairs) - 1
        for q in range(BATCH):
            quantities(buf_a, 2 * first, q)

        def body(i, carry):
            both(buf_b, buf_a, 2 * i + 1, 2 * i)
            both(buf_a, buf_b, jnp.minimum(2 * i + 2, last), 2 * i + 1)
            return carry

        at = first
        for size in sizes:

            def several(i, carry, size=size, at=at):
                for k in range(size):
                    body(at + i * size + k, carry)
                return carry

            steps = (first + pairs - at) // size
            lax.fori_loop(0, steps, several, 0)
            at = at + steps * size


def near_place(b):
    return (b // (GRID * LAYERS) * (GRID + 2) + b // LAYERS % GRID + 1) * (LAYERS + 2) + b % LAYERS + 1


def near_kernel(steps, ids, region, w_home, w_src, acc, lx, ly, rx, ry, rr, buf_a, buf_b):
    def owned(i, carry):
        first = near_place(i * GROUP)
        places = [first + g for g in range(GROUP)]
        z = jnp.concatenate([factors(region[p]) for p in places], 1)
        store_source(places, z, w_src, rx, ry, rr)
        store_home(i * GROUP, z, w_home, lx, ly)
        return carry

    def rim_place(i):
        side, at = i // 28, i % 28
        place_y = jnp.where(at < 10, 0, jnp.where(at < 20, GRID + 1, 1 + (at - 20) // 2))
        place_z = jnp.where(at < 20, at % 10, (at - 20) % 2 * (LAYERS + 1))
        return (side * (GRID + 2) + place_y) * (LAYERS + 2) + place_z

    def rim(i, carry):
        places = [rim_place(i * GROUP + g) for g in range(GROUP)]
        z = jnp.concatenate([factors(region[p]) for p in places], 1)
        store_source(places, z, w_src, rx, ry, rr)
        return carry

    lax.fori_loop(0, 128 // GROUP, owned, 0, unroll=8)
    lax.fori_loop(0, 112 // GROUP, rim, 0, unroll=14)
    acc[...] = jnp.zeros_like(acc)
    all_tiles(NEAR_SIZES, 0, steps[0], ids, lx, ly, rx, ry, rr, acc, buf_a, buf_b)


def far_kernel(steps, ids, low, high, region, w_src, lx, ly, acc, out, acc_out, rx, ry, rr, buf_a, buf_b):
    def prepare(i, carry):
        for k, (plane, off_x) in enumerate(((low, -44.0), (high, 44.0))):
            places = [i * FAR_GROUP + g for g in range(FAR_GROUP)]
            z = jnp.concatenate([factors(plane[p], off_x * SCALE) for p in places], 1)
            store_source([p + 60 * k for p in places], z, w_src, rx, ry, rr)
        return carry

    lax.fori_loop(0, 60 // FAR_GROUP, prepare, 0, unroll=6)
    all_tiles(FAR_SIZES, steps[0], steps[1], ids, lx, ly, rx, ry, rr, acc_out, buf_a, buf_b)

    def finish(s, carry):
        first = near_place(4 * s)
        for k in range(4):
            sums = acc_out[4 * s + k]
            head, tail = sums[:8], sums[8:]
            weighed = head + pltpu.roll(head, 4, 0) + tail
            out[s, 3 * k : 3 * k + 3] = (region[first + k] * head[3:4] - weighed)[:3]
        return carry

    lax.fori_loop(0, 32, finish, 0, unroll=8)


def tile_lists(tiles, blocks):
    home, source = tiles[0], tiles[1]
    slot, member = source // blocks, source % blocks
    step_x = slot // 9 - 1
    place_y = member // LAYERS % GRID + (slot // 3 % 3 - 1) * GRID + 1
    place_z = member % LAYERS + (slot % 3 - 1) * LAYERS + 1
    plane = place_y * (LAYERS + 2) + place_z
    side = jnp.where(step_x == 0, member // (GRID * LAYERS), (step_x + 1) // 2)
    listed = home >= 0
    unit = 2 * BATCH
    order = jnp.arange(home.shape[0])
    upto = order[None, :] <= order[:, None]
    key = home * (27 * blocks) + source
    same = key[None, :] == key[:, None]
    times = jnp.sum(jnp.where(same, 1, 0), 1)
    first = jnp.sum(jnp.where(same & upto, 1, 0), 1) == 1
    near = listed & first & (step_x == 0)
    far = listed & first & (step_x != 0)
    near_at = jnp.sum(jnp.where(upto & near[None, :], 1, 0), 1)
    far_at = jnp.sum(jnp.where(upto & far[None, :], 1, 0), 1)
    near_steps = (jnp.sum(near.astype(jnp.int32)) + unit - 1) // unit
    far_steps = (jnp.sum(far.astype(jnp.int32)) + unit - 1) // unit
    at = jnp.where(near, near_at - 1, jnp.where(far, near_steps * unit + far_at - 1, -1))
    code = home * 256 + side * 60 + plane + 1
    slots = jnp.arange(home.shape[0] + 2 * unit)
    found = jnp.sum(jnp.where(slots[:, None] == at[None, :], code[None, :], 0), 1)
    times = jnp.sum(jnp.where(slots[:, None] == at[None, :], times[None, :], 0), 1)
    real = found > 0
    code = jnp.maximum(found - 1, 0)
    ids = jnp.stack([code // 256, code % 256, jnp.where(real, code // 256, blocks), times])
    return jnp.stack([near_steps, far_steps]), ids


def per_device(coords, charges, atom_types, lj_sigma, lj_epsilon, tile_list):
    blocks, width = coords.shape[2], coords.shape[3]
    peers = lax.axis_size("gy") * lax.axis_size("gz")
    vmem = pl.BlockSpec(memory_space=pltpu.VMEM)
    smem = pl.BlockSpec(memory_space=pltpu.SMEM)
    gz = lax.axis_index("gz")
    small = pltpu.CompilerParams(vmem_limit_bytes=8 << 20)
    outgoing = pl.pallas_call(
        pack_kernel,
        out_shape=jax.ShapeDtypeStruct((peers * SENT, width), F32),
        in_specs=[smem, smem] + [pl.BlockSpec(memory_space=pl.ANY)] * 3,
        out_specs=vmem,
        scratch_shapes=[
            pltpu.VMEM((3, blocks, width), F32),
            pltpu.VMEM((blocks, width), F32),
            pltpu.VMEM((blocks, width), jnp.int32),
            pltpu.SemaphoreType.DMA((3,)),
        ],
        compiler_params=pltpu.CompilerParams(vmem_limit_bytes=65011712),
    )((gz % 2).reshape(1), (gz // 2).reshape(1), coords[:, 0], charges[0], atom_types[0])
    arrived = lax.all_to_all(
        outgoing.reshape(peers, SENT, width), ("gy", "gz"), split_axis=0, concat_axis=0, tiled=True
    )
    steps, ids = tile_lists(tile_list[0, 0, 0], blocks)
    w_home, w_src = weights(lj_sigma, lj_epsilon)
    region = pl.pallas_call(
        unpack_kernel,
        out_shape=jax.ShapeDtypeStruct((NEAR, 8, width), F32),
        in_specs=[vmem],
        out_specs=vmem,
        compiler_params=small,
    )(arrived)
    count = lax.axis_size("gx")
    forward = [(i, (i + 1) % count) for i in range(count)]
    backward = [(target, source) for source, target in forward]
    low = lax.ppermute(region[180:240], "gx", forward)
    high = lax.ppermute(region[:60], "gx", backward)

    def source_scratch(n):
        return [
            pltpu.VMEM((n, NX, 256), BF16),
            pltpu.VMEM((n, NY, 256), BF16),
            pltpu.VMEM((n, 16, 256), BF16),
            pltpu.VMEM((BATCH, 2, 128, 256), F32),
            pltpu.VMEM((BATCH, 2, 128, 256), F32),
        ]

    acc_shape = jax.ShapeDtypeStruct((blocks + 1, 16, width), F32)
    factor_shape = jax.ShapeDtypeStruct((blocks, 128, 128), BF16)
    acc, lx, ly = pl.pallas_call(
        near_kernel,
        out_shape=[acc_shape, factor_shape, factor_shape],
        in_specs=[smem, smem, vmem, vmem, vmem],
        out_specs=[vmem] * 3,
        scratch_shapes=source_scratch(NEAR),
        compiler_params=pltpu.CompilerParams(vmem_limit_bytes=28 << 20),
        cost_estimate=pl.CostEstimate(flops=10**10, bytes_accessed=10**7, transcendentals=10**6),
    )(steps, ids, region, w_home, w_src)
    totals, _ = pl.pallas_call(
        far_kernel,
        out_shape=[jax.ShapeDtypeStruct((peers, 12, width), F32), acc_shape],
        in_specs=[smem, smem] + [vmem] * 7,
        out_specs=[vmem] * 2,
        scratch_shapes=source_scratch(120),
        input_output_aliases={8: 1},
        compiler_params=pltpu.CompilerParams(vmem_limit_bytes=24 << 20),
    )(steps, ids, low, high, region, w_src, lx, ly, acc)
    back = lax.all_to_all(totals, ("gy", "gz"), split_axis=0, concat_axis=0, tiled=True)
    return back.reshape(peers, 4, 3, width).transpose(2, 1, 0, 3).reshape(3, 1, blocks, width)


def solution(mesh):
    return jax.shard_map(
        per_device,
        mesh=mesh,
        in_specs=(
            P(None, "gx", ("gy", "gz"), None),
            P("gx", ("gy", "gz"), None),
            P("gx", ("gy", "gz"), None),
            P(),
            P(),
            P("gx", "gy", "gz", None, None),
        ),
        out_specs=P(None, "gx", ("gy", "gz"), None),
        check_vma=False,
    )
```

```python
import math

import jax
import jax.numpy as jnp
import numpy as np
from jax import lax
from jax.experimental import pallas as pl
from jax.experimental.pallas import tpu as pltpu
from jax.sharding import PartitionSpec as P

F32 = jnp.float32
BF16 = jnp.bfloat16

GRID = 4
LAYERS = 8
CELL = 11.0
LIMIT = 97.0
SCALE = LIMIT**-0.5
SOFT = 16.0 / LIMIT
COULOMB = 332.0636 / LIMIT
FACTOR_12 = 48.0 * LIMIT**-6.5
FACTOR_6 = 24.0 * LIMIT**-3.5

ROW_X, ROW_Y, ROW_Z, ROW_C, ROW_TYPE, ROW_Q, ROW_ONE, ROW_CC = range(8)
ROW_SOFT = ROW_TYPE
TYPES = 64
ORDER = 13
NX = 32
NY = 48
NZ = TYPES + 32
BATCH = 4
SIZES = (8, 4, 2, 1)
GROUP = 8
FAR_GROUP = 10
NEAR = 240
SENT = 56


def placements():
    home = np.zeros((32, NX), np.float32)
    src_w = np.zeros((NX, 32), np.float32)
    src_c = np.zeros((NX, 32), np.float32)
    at = 0

    def term(row, part):
        return part * 8 + row

    for row in (ROW_X, ROW_Y, ROW_Z):
        for i, j in ((0, 0), (0, 1), (1, 0), (1, 1), (0, 2), (2, 0)):
            home[term(row, i), at] = 1.0
            src_w[at, term(row, j)] = -2.0
            at += 1
    for part in range(3):
        home[term(ROW_SOFT, part), at] = 1.0
        src_w[at, term(ROW_ONE, 0)] = 1.0
        at += 1
    for part in range(3):
        home[term(ROW_ONE, 0), at] = 1.0
        src_w[at, term(ROW_Q, part)] = 1.0
        at += 1
    for i, j in ((0, 0), (0, 1), (1, 0), (1, 1), (0, 2), (2, 0)):
        home[term(ROW_CC, i), at] = 1.0
        src_c[at, term(ROW_C, j)] = 1.0
        at += 1
    place_r = np.zeros((16, 32), np.float32)
    for k, row in enumerate((ROW_X, ROW_Y, ROW_Z)):
        for part in range(3):
            place_r[4 * part + k, term(row, part)] = 1.0
    place_r[3, term(ROW_ONE, 0)] = 1.0
    return home, src_w, src_c, place_r


def weights(lj_sigma, lj_epsilon):
    root = jnp.sqrt(lj_epsilon)
    half = 0.5 * lj_sigma
    powers = [jnp.ones_like(half)]
    for _ in range(ORDER - 1):
        powers.append(powers[-1] * half)

    def halves(table):
        high = lax.reduce_precision(table, 8, 7)
        return high, table - high

    h_high, h_low = halves(jnp.stack([root * p for p in powers]))
    zero = jnp.zeros_like(half)
    p12 = jnp.stack([root * powers[12 - k] * (FACTOR_12 * math.comb(12, k)) for k in range(ORDER)])
    p6 = jnp.stack(
        [root * powers[6 - k] * (FACTOR_6 * math.comb(6, k)) if k <= 6 else zero for k in range(ORDER)]
    )
    pad = jnp.zeros((NY - 3 * ORDER, TYPES), F32)
    home_y = jnp.concatenate([h_high, h_high, h_low, pad])
    src_y = []
    for table in (p12, p6):
        high, low = halves(table)
        src_y += [high, low, high, pad]
    home_x, src_w, src_c, place_r = placements()
    home_x = np.pad(home_x, ((TYPES, 0), (0, 128 - NX)))
    home = jnp.concatenate([home_x, jnp.pad(home_y.T, ((0, NZ - TYPES), (0, 128 - NY)))], 1)
    fixed = jnp.concatenate([jnp.zeros((2 * NX + 16, TYPES)), np.concatenate([src_w, src_c, place_r])], 1)
    lj = jnp.concatenate([jnp.concatenate(src_y), jnp.zeros((2 * NY, 32), F32)], 1)
    source = jnp.concatenate([fixed, lj])
    return home.astype(BF16), source.astype(BF16)


def pack_kernel(half_hi, side, coords_in, charges_in, types_in, out, coords, charges, types, sems):
    copies = [
        pltpu.make_async_copy(source, target, sems.at[i])
        for i, (source, target) in enumerate(
            ((coords_in, coords), (charges_in, charges), (types_in, types))
        )
    ]
    for copy in copies:
        copy.start()
    for copy in copies:
        copy.wait()
    upper = half_hi[0] == 1
    back_y = side[0] == 3
    kinds = types[...].astype(F32)

    def next_y(value):
        ahead = jnp.concatenate([value[8:], value[:8]])
        behind = jnp.concatenate([value[24:], value[:24]])
        return jnp.where(back_y, behind, ahead)

    for q in range(5):
        for cell in range(5):

            def rows(k):
                if q < 3:
                    return coords[q, 32 * k : 32 * k + 32]
                return charges[32 * k : 32 * k + 32] if q == 3 else kinds[32 * k : 32 * k + 32]

            if cell < 4:
                value = rows(cell)
            else:
                ahead = pltpu.roll(rows(0).reshape(4, 8, 128), 7, 1)
                behind = pltpu.roll(rows(3).reshape(4, 8, 128), 1, 1)
                value = jnp.where(upper, behind, ahead).reshape(32, 128)
            out[pl.ds(5 * cell + q, 32, stride=SENT), :] = value
            out[pl.ds(25 + 5 * cell + q, 32, stride=SENT), :] = next_y(value)


def unpack_kernel(arrived, out):
    row = lax.broadcasted_iota(jnp.int32, (8, 128), 0)
    scale = jnp.where(row < 3, SCALE, 1.0)

    def body(cell_x, carry):
        off_x = (cell_x.astype(F32) - 2) * (CELL * SCALE)
        for s in range(8):
            cell_y, upper = s // 2, s % 2
            for c in range(10 if cell_y in (0, GRID - 1) else 5):
                place_y = cell_y + 1
                if c >= 5:
                    place_y = GRID + 1 if cell_y == 0 else 0
                place_z = upper * 4 + c % 5 + 1 if c % 5 < 4 else (1 - upper) * (LAYERS + 1)
                off_y = (place_y - 3) * (CELL * SCALE)
                off_z = (place_z - 5) * (CELL * SCALE)
                off = jnp.where(row == ROW_Y, off_y, jnp.where(row == ROW_Z, off_z, 0.0))
                off = jnp.where(row == ROW_X, off_x, off)
                rows = arrived[8 * cell_x + s, 5 * c : 5 * c + 5]
                block = jnp.concatenate([rows, jnp.zeros((3, 128), F32)]) * scale + off
                out[(cell_x * (GRID + 2) + place_y) * (LAYERS + 2) + place_z] = block
        return carry

    lax.fori_loop(0, GRID, body, 0)


def factors(block, off_x=None):
    row = lax.broadcasted_iota(jnp.int32, (8, 128), 0)
    kind = lax.broadcasted_iota(jnp.int32, (TYPES, 128), 0)
    moved = block if off_x is None else block + jnp.where(row == ROW_X, off_x, 0.0)
    square = jnp.sum(jnp.where(row < 3, moved * moved, 0.0), axis=0, keepdims=True)
    moved = jnp.where(row == ROW_Q, square, jnp.where(row == ROW_ONE, 1.0, moved))
    moved = jnp.where(row == ROW_SOFT, square + SOFT, moved)
    moved = jnp.where(row == ROW_CC, COULOMB * block[ROW_C : ROW_C + 1], moved)
    high = moved.astype(BF16).astype(F32)
    rest = moved - high
    mid = rest.astype(BF16).astype(F32)
    hot = jnp.where(block[ROW_TYPE : ROW_TYPE + 1].astype(jnp.int32) == kind, 1.0, 0.0)
    return jnp.concatenate([hot, high, mid, rest - mid, jnp.zeros((8, 128), F32)]).astype(BF16)


def store_source(places, z, w_src, rx, ry, rr):
    made = jnp.dot(w_src[...], z, preferred_element_type=F32).astype(BF16)
    for g, p in enumerate(places):
        own = made[:, 128 * g : 128 * g + 128]
        rx[p, :, :128] = own[:NX]
        rx[p, :, 128:] = own[NX : 2 * NX]
        rr[p, :, :128] = own[2 * NX : 2 * NX + 16]
        rr[p, :, 128:] = own[2 * NX : 2 * NX + 16]
        at = 2 * NX + 16
        ry[p, :, :128] = own[at : at + NY]
        ry[p, :, 128:] = own[at + NY :]


def store_home(first, z, w_home, lx, ly):
    made = lax.dot_general(z, w_home[...], (((0,), (0,)), ((), ())), preferred_element_type=F32)
    made = made.astype(BF16)
    for g in range(GROUP):
        own = made[128 * g : 128 * g + 128]
        lx[first + g] = own[:, :128]
        ly[first + g] = own[:, 128:]


def all_tiles(sizes, first, pairs, ids, lx, ly, rx, ry, rr, acc, buf_a, buf_b):
    def quantities(buf, batch, q):
        h, j = ids[0, batch * BATCH + q], ids[1, batch * BATCH + q]
        buf[q, 0] = jnp.dot(lx[h][:, :NX], rx[j], preferred_element_type=F32)
        buf[q, 1] = jnp.dot(ly[h][:, :NY], ry[j], preferred_element_type=F32)

    def forces(buf, batch, q):
        j, h = ids[1, batch * BATCH + q], ids[2, batch * BATCH + q]

        def part(i, side):
            return buf[q, i, :, 128 * side : 128 * side + 128].reshape(16, 8, 128)

        w = jnp.minimum(part(0, 0), 1.0)
        u, inv = lax.rsqrt(w), pltpu.reciprocal(w, approx=True)
        inv3 = inv * inv * inv
        c12, c6, charge = part(1, 0), part(1, 1), part(0, 1)
        push = inv * (inv3 * (inv3 * c12 - c6) + u * charge) - ((c12 - c6) + charge)
        push = push.reshape(128, 128)
        high = push.astype(BF16)
        low = (push - high.astype(F32)).astype(BF16)
        once = lax.dot_general(
            rr[j],
            jnp.concatenate([high, low], 1),
            (((1,), (1,)), ((), ())),
            preferred_element_type=F32,
        )
        acc[h] += once * ids[3, batch * BATCH + q].astype(F32)

    def both(buf_next, buf_now, batch_next, batch_now):
        for q in range(BATCH):
            quantities(buf_next, batch_next, q)
            forces(buf_now, batch_now, q)

    @pl.when(pairs > 0)
    def _():
        last = 2 * (first + pairs) - 1
        for q in range(BATCH):
            quantities(buf_a, 2 * first, q)

        def body(i, carry):
            both(buf_b, buf_a, 2 * i + 1, 2 * i)
            both(buf_a, buf_b, jnp.minimum(2 * i + 2, last), 2 * i + 1)
            return carry

        at = first
        for size in sizes:

            def several(i, carry, size=size, at=at):
                for k in range(size):
                    body(at + i * size + k, carry)
                return carry

            steps = (first + pairs - at) // size
            lax.fori_loop(0, steps, several, 0)
            at = at + steps * size


def near_place(b):
    return (b // (GRID * LAYERS) * (GRID + 2) + b // LAYERS % GRID + 1) * (LAYERS + 2) + b % LAYERS + 1


def near_kernel(steps, ids, region, w_home, w_src, acc, lx, ly, rx, ry, rr, buf_a, buf_b):
    def owned(i, carry):
        first = near_place(i * GROUP)
        places = [first + g for g in range(GROUP)]
        z = jnp.concatenate([factors(region[p]) for p in places], 1)
        store_source(places, z, w_src, rx, ry, rr)
        store_home(i * GROUP, z, w_home, lx, ly)
        return carry

    def rim_place(i):
        side, at = i // 28, i % 28
        place_y = jnp.where(at < 10, 0, jnp.where(at < 20, GRID + 1, 1 + (at - 20) // 2))
        place_z = jnp.where(at < 20, at % 10, (at - 20) % 2 * (LAYERS + 1))
        return (side * (GRID + 2) + place_y) * (LAYERS + 2) + place_z

    def rim(i, carry):
        places = [rim_place(i * GROUP + g) for g in range(GROUP)]
        z = jnp.concatenate([factors(region[p]) for p in places], 1)
        store_source(places, z, w_src, rx, ry, rr)
        return carry

    lax.fori_loop(0, 128 // GROUP, owned, 0, unroll=8)
    lax.fori_loop(0, 112 // GROUP, rim, 0, unroll=14)
    acc[...] = jnp.zeros_like(acc)
    all_tiles(SIZES, 0, steps[0], ids, lx, ly, rx, ry, rr, acc, buf_a, buf_b)


def far_kernel(steps, ids, low, high, region, w_src, lx, ly, acc, out, acc_out, rx, ry, rr, buf_a, buf_b):
    def prepare(i, carry):
        for k, (plane, off_x) in enumerate(((low, -44.0), (high, 44.0))):
            places = [i * FAR_GROUP + g for g in range(FAR_GROUP)]
            z = jnp.concatenate([factors(plane[p], off_x * SCALE) for p in places], 1)
            store_source([p + 60 * k for p in places], z, w_src, rx, ry, rr)
        return carry

    lax.fori_loop(0, 60 // FAR_GROUP, prepare, 0, unroll=6)
    all_tiles(SIZES, steps[0], steps[1], ids, lx, ly, rx, ry, rr, acc_out, buf_a, buf_b)

    def finish(s, carry):
        first = near_place(4 * s)
        for k in range(4):
            sums = acc_out[4 * s + k]
            head, tail = sums[:8], sums[8:]
            weighed = head + pltpu.roll(head, 4, 0) + tail
            out[s, 3 * k : 3 * k + 3] = (region[first + k] * head[3:4] - weighed)[:3]
        return carry

    lax.fori_loop(0, 32, finish, 0, unroll=8)


def tile_lists(tiles, blocks):
    home, source = tiles[0], tiles[1]
    slot, member = source // blocks, source % blocks
    step_x = slot // 9 - 1
    place_y = member // LAYERS % GRID + (slot // 3 % 3 - 1) * GRID + 1
    place_z = member % LAYERS + (slot % 3 - 1) * LAYERS + 1
    plane = place_y * (LAYERS + 2) + place_z
    side = jnp.where(step_x == 0, member // (GRID * LAYERS), (step_x + 1) // 2)
    listed = home >= 0
    unit = 2 * BATCH
    order = jnp.arange(home.shape[0])
    upto = order[None, :] <= order[:, None]
    key = home * (27 * blocks) + source
    same = key[None, :] == key[:, None]
    times = jnp.sum(jnp.where(same, 1, 0), 1)
    first = jnp.sum(jnp.where(same & upto, 1, 0), 1) == 1
    near = listed & first & (step_x == 0)
    far = listed & first & (step_x != 0)
    near_at = jnp.sum(jnp.where(upto & near[None, :], 1, 0), 1)
    far_at = jnp.sum(jnp.where(upto & far[None, :], 1, 0), 1)
    near_steps = (jnp.sum(near.astype(jnp.int32)) + unit - 1) // unit
    far_steps = (jnp.sum(far.astype(jnp.int32)) + unit - 1) // unit
    at = jnp.where(near, near_at - 1, jnp.where(far, near_steps * unit + far_at - 1, -1))
    code = home * 256 + side * 60 + plane + 1
    slots = jnp.arange(home.shape[0] + 2 * unit)
    found = jnp.sum(jnp.where(slots[:, None] == at[None, :], code[None, :], 0), 1)
    times = jnp.sum(jnp.where(slots[:, None] == at[None, :], times[None, :], 0), 1)
    real = found > 0
    code = jnp.maximum(found - 1, 0)
    ids = jnp.stack([code // 256, code % 256, jnp.where(real, code // 256, blocks), times])
    return jnp.stack([near_steps, far_steps]), ids


def per_device(coords, charges, atom_types, lj_sigma, lj_epsilon, tile_list):
    blocks, width = coords.shape[2], coords.shape[3]
    peers = lax.axis_size("gy") * lax.axis_size("gz")
    vmem = pl.BlockSpec(memory_space=pltpu.VMEM)
    smem = pl.BlockSpec(memory_space=pltpu.SMEM)
    gz = lax.axis_index("gz")
    small = pltpu.CompilerParams(vmem_limit_bytes=8 << 20)
    outgoing = pl.pallas_call(
        pack_kernel,
        out_shape=jax.ShapeDtypeStruct((peers * SENT, width), F32),
        in_specs=[smem, smem] + [pl.BlockSpec(memory_space=pl.ANY)] * 3,
        out_specs=vmem,
        scratch_shapes=[
            pltpu.VMEM((3, blocks, width), F32),
            pltpu.VMEM((blocks, width), F32),
            pltpu.VMEM((blocks, width), jnp.int32),
            pltpu.SemaphoreType.DMA((3,)),
        ],
        compiler_params=pltpu.CompilerParams(vmem_limit_bytes=65011712),
    )((gz % 2).reshape(1), (gz // 2).reshape(1), coords[:, 0], charges[0], atom_types[0])
    arrived = lax.all_to_all(
        outgoing.reshape(peers, SENT, width), ("gy", "gz"), split_axis=0, concat_axis=0, tiled=True
    )
    steps, ids = tile_lists(tile_list[0, 0, 0], blocks)
    w_home, w_src = weights(lj_sigma, lj_epsilon)
    region = pl.pallas_call(
        unpack_kernel,
        out_shape=jax.ShapeDtypeStruct((NEAR, 8, width), F32),
        in_specs=[vmem],
        out_specs=vmem,
        compiler_params=small,
    )(arrived)
    count = lax.axis_size("gx")
    forward = [(i, (i + 1) % count) for i in range(count)]
    backward = [(target, source) for source, target in forward]
    low = lax.ppermute(region[180:240], "gx", forward)
    high = lax.ppermute(region[:60], "gx", backward)

    def source_scratch(n):
        return [
            pltpu.VMEM((n, NX, 256), BF16),
            pltpu.VMEM((n, NY, 256), BF16),
            pltpu.VMEM((n, 16, 256), BF16),
            pltpu.VMEM((BATCH, 2, 128, 256), F32),
            pltpu.VMEM((BATCH, 2, 128, 256), F32),
        ]

    acc_shape = jax.ShapeDtypeStruct((blocks + 1, 16, width), F32)
    factor_shape = jax.ShapeDtypeStruct((blocks, 128, 128), BF16)
    acc, lx, ly = pl.pallas_call(
        near_kernel,
        out_shape=[acc_shape, factor_shape, factor_shape],
        in_specs=[smem, smem, vmem, vmem, vmem],
        out_specs=[vmem] * 3,
        scratch_shapes=source_scratch(NEAR),
        compiler_params=pltpu.CompilerParams(vmem_limit_bytes=28 << 20),
        cost_estimate=pl.CostEstimate(flops=10**10, bytes_accessed=10**7, transcendentals=10**6),
    )(steps, ids, region, w_home, w_src)
    totals, _ = pl.pallas_call(
        far_kernel,
        out_shape=[jax.ShapeDtypeStruct((peers, 12, width), F32), acc_shape],
        in_specs=[smem, smem] + [vmem] * 7,
        out_specs=[vmem] * 2,
        scratch_shapes=source_scratch(120),
        input_output_aliases={8: 1},
        compiler_params=pltpu.CompilerParams(vmem_limit_bytes=24 << 20),
    )(steps, ids, low, high, region, w_src, lx, ly, acc)
    back = lax.all_to_all(totals, ("gy", "gz"), split_axis=0, concat_axis=0, tiled=True)
    return back.reshape(peers, 4, 3, width).transpose(2, 1, 0, 3).reshape(3, 1, blocks, width)


def solution(mesh):
    return jax.shard_map(
        per_device,
        mesh=mesh,
        in_specs=(
            P(None, "gx", ("gy", "gz"), None),
            P("gx", ("gy", "gz"), None),
            P("gx", ("gy", "gz"), None),
            P(),
            P(),
            P("gx", "gy", "gz", None, None),
        ),
        out_specs=P(None, "gx", ("gy", "gz"), None),
        check_vma=False,
    )
```

```python
import math

import jax
import jax.numpy as jnp
import numpy as np
from jax import lax
from jax.experimental import pallas as pl
from jax.experimental.pallas import tpu as pltpu
from jax.sharding import PartitionSpec as P

F32 = jnp.float32
BF16 = jnp.bfloat16

GRID = 4
LAYERS = 8
CELL = 11.0
LIMIT = 97.0
SCALE = LIMIT**-0.5
SOFT = 16.0 / LIMIT
COULOMB = 332.0636 / LIMIT
FACTOR_12 = 48.0 * LIMIT**-6.5
FACTOR_6 = 24.0 * LIMIT**-3.5

ROW_X, ROW_Y, ROW_Z, ROW_C, ROW_TYPE, ROW_Q, ROW_ONE, ROW_CC = range(8)
ROW_SOFT = ROW_TYPE
TYPES = 64
ORDER = 13
NX = 32
NY = 48
NZ = TYPES + 32
BATCH = 4
SIZES = (8, 4, 2, 1)
GROUP = 8
FAR_GROUP = 10
NEAR = 240
SENT = 56


def placements():
    home = np.zeros((32, NX), np.float32)
    src_w = np.zeros((NX, 32), np.float32)
    src_c = np.zeros((NX, 32), np.float32)
    at = 0

    def term(row, part):
        return part * 8 + row

    for row in (ROW_X, ROW_Y, ROW_Z):
        for i, j in ((0, 0), (0, 1), (1, 0), (1, 1), (0, 2), (2, 0)):
            home[term(row, i), at] = 1.0
            src_w[at, term(row, j)] = -2.0
            at += 1
    for part in range(3):
        home[term(ROW_SOFT, part), at] = 1.0
        src_w[at, term(ROW_ONE, 0)] = 1.0
        at += 1
    for part in range(3):
        home[term(ROW_ONE, 0), at] = 1.0
        src_w[at, term(ROW_Q, part)] = 1.0
        at += 1
    for i, j in ((0, 0), (0, 1), (1, 0), (1, 1), (0, 2), (2, 0)):
        home[term(ROW_CC, i), at] = 1.0
        src_c[at, term(ROW_C, j)] = 1.0
        at += 1
    place_r = np.zeros((16, 32), np.float32)
    for k, row in enumerate((ROW_X, ROW_Y, ROW_Z)):
        for part in range(3):
            place_r[4 * part + k, term(row, part)] = 1.0
    place_r[3, term(ROW_ONE, 0)] = 1.0
    return home, src_w, src_c, place_r


def weights(lj_sigma, lj_epsilon):
    root = jnp.sqrt(lj_epsilon)
    half = 0.5 * lj_sigma
    powers = [jnp.ones_like(half)]
    for _ in range(ORDER - 1):
        powers.append(powers[-1] * half)

    def halves(table):
        high = lax.reduce_precision(table, 8, 7)
        return high, table - high

    h_high, h_low = halves(jnp.stack([root * p for p in powers]))
    zero = jnp.zeros_like(half)
    p12 = jnp.stack([root * powers[12 - k] * (FACTOR_12 * math.comb(12, k)) for k in range(ORDER)])
    p6 = jnp.stack(
        [root * powers[6 - k] * (FACTOR_6 * math.comb(6, k)) if k <= 6 else zero for k in range(ORDER)]
    )
    pad = jnp.zeros((NY - 3 * ORDER, TYPES), F32)
    home_y = jnp.concatenate([h_high, h_high, h_low, pad])
    src_y = []
    for table in (p12, p6):
        high, low = halves(table)
        src_y += [high, low, high, pad]
    home_x, src_w, src_c, place_r = placements()
    home_x = np.pad(home_x, ((TYPES, 0), (0, 128 - NX)))
    home = jnp.concatenate([home_x, jnp.pad(home_y.T, ((0, NZ - TYPES), (0, 128 - NY)))], 1)
    fixed = jnp.concatenate([jnp.zeros((2 * NX + 16, TYPES)), np.concatenate([src_w, src_c, place_r])], 1)
    lj = jnp.concatenate([jnp.concatenate(src_y), jnp.zeros((2 * NY, 32), F32)], 1)
    source = jnp.concatenate([fixed, lj])
    return home.astype(BF16), source.astype(BF16)


def pack_kernel(half_hi, side, coords_in, charges_in, types_in, out, coords, charges, types, sems):
    copies = [
        pltpu.make_async_copy(source, target, sems.at[i])
        for i, (source, target) in enumerate(
            ((coords_in, coords), (charges_in, charges), (types_in, types))
        )
    ]
    for copy in copies:
        copy.start()
    for copy in copies:
        copy.wait()
    upper = half_hi[0] == 1
    back_y = side[0] == 3
    kinds = types[...].astype(F32)

    def next_y(value):
        ahead = jnp.concatenate([value[8:], value[:8]])
        behind = jnp.concatenate([value[24:], value[:24]])
        return jnp.where(back_y, behind, ahead)

    for q in range(5):
        for cell in range(5):

            def rows(k):
                if q < 3:
                    return coords[q, 32 * k : 32 * k + 32]
                return charges[32 * k : 32 * k + 32] if q == 3 else kinds[32 * k : 32 * k + 32]

            if cell < 4:
                value = rows(cell)
            else:
                ahead = pltpu.roll(rows(0).reshape(4, 8, 128), 7, 1)
                behind = pltpu.roll(rows(3).reshape(4, 8, 128), 1, 1)
                value = jnp.where(upper, behind, ahead).reshape(32, 128)
            out[pl.ds(5 * cell + q, 32, stride=SENT), :] = value
            out[pl.ds(25 + 5 * cell + q, 32, stride=SENT), :] = next_y(value)


def unpack_kernel(arrived, out):
    row = lax.broadcasted_iota(jnp.int32, (8, 128), 0)
    scale = jnp.where(row < 3, SCALE, 1.0)

    def body(cell_x, carry):
        off_x = (cell_x.astype(F32) - 2) * (CELL * SCALE)
        for s in range(8):
            cell_y, upper = s // 2, s % 2
            for c in range(10 if cell_y in (0, GRID - 1) else 5):
                place_y = cell_y + 1
                if c >= 5:
                    place_y = GRID + 1 if cell_y == 0 else 0
                place_z = upper * 4 + c % 5 + 1 if c % 5 < 4 else (1 - upper) * (LAYERS + 1)
                off_y = (place_y - 3) * (CELL * SCALE)
                off_z = (place_z - 5) * (CELL * SCALE)
                off = jnp.where(row == ROW_Y, off_y, jnp.where(row == ROW_Z, off_z, 0.0))
                off = jnp.where(row == ROW_X, off_x, off)
                rows = arrived[8 * cell_x + s, 5 * c : 5 * c + 5]
                block = jnp.concatenate([rows, jnp.zeros((3, 128), F32)]) * scale + off
                out[(cell_x * (GRID + 2) + place_y) * (LAYERS + 2) + place_z] = block
        return carry

    lax.fori_loop(0, GRID, body, 0)


def factors(block, off_x=None):
    row = lax.broadcasted_iota(jnp.int32, (8, 128), 0)
    kind = lax.broadcasted_iota(jnp.int32, (TYPES, 128), 0)
    moved = block if off_x is None else block + jnp.where(row == ROW_X, off_x, 0.0)
    square = jnp.sum(jnp.where(row < 3, moved * moved, 0.0), axis=0, keepdims=True)
    moved = jnp.where(row == ROW_Q, square, jnp.where(row == ROW_ONE, 1.0, moved))
    moved = jnp.where(row == ROW_SOFT, square + SOFT, moved)
    moved = jnp.where(row == ROW_CC, COULOMB * block[ROW_C : ROW_C + 1], moved)
    high = moved.astype(BF16).astype(F32)
    rest = moved - high
    mid = rest.astype(BF16).astype(F32)
    hot = jnp.where(block[ROW_TYPE : ROW_TYPE + 1].astype(jnp.int32) == kind, 1.0, 0.0)
    return jnp.concatenate([hot, high, mid, rest - mid, jnp.zeros((8, 128), F32)]).astype(BF16)


def store_source(places, z, w_src, rx, ry, rr):
    made = jnp.dot(w_src[...], z, preferred_element_type=F32).astype(BF16)
    for g, p in enumerate(places):
        own = made[:, 128 * g : 128 * g + 128]
        rx[p, :, :128] = own[:NX]
        rx[p, :, 128:] = own[NX : 2 * NX]
        rr[p, :, :128] = own[2 * NX : 2 * NX + 16]
        rr[p, :, 128:] = own[2 * NX : 2 * NX + 16]
        at = 2 * NX + 16
        ry[p, :, :128] = own[at : at + NY]
        ry[p, :, 128:] = own[at + NY :]


def store_home(first, z, w_home, lx, ly):
    made = lax.dot_general(z, w_home[...], (((0,), (0,)), ((), ())), preferred_element_type=F32)
    made = made.astype(BF16)
    for g in range(GROUP):
        own = made[128 * g : 128 * g + 128]
        lx[first + g] = own[:, :128]
        ly[first + g] = own[:, 128:]


def all_tiles(sizes, first, pairs, ids, lx, ly, rx, ry, rr, acc, buf_a, buf_b):
    def quantities(buf, batch, q):
        h, j = ids[0, batch * BATCH + q], ids[1, batch * BATCH + q]
        buf[q, 0] = jnp.dot(lx[h][:, :NX], rx[j], preferred_element_type=F32)
        buf[q, 1] = jnp.dot(ly[h][:, :NY], ry[j], preferred_element_type=F32)

    def forces(buf, batch, q):
        j, h = ids[1, batch * BATCH + q], ids[2, batch * BATCH + q]

        def part(i, side):
            return buf[q, i, :, 128 * side : 128 * side + 128].reshape(16, 8, 128)

        w = jnp.minimum(part(0, 0), 1.0)
        u = lax.rsqrt(w)
        inv = u * u
        inv3 = inv * inv * inv
        c12, c6, charge = part(1, 0), part(1, 1), part(0, 1)
        push = inv * (inv3 * (inv3 * c12 - c6) + u * charge) - ((c12 - c6) + charge)
        push = push.reshape(128, 128)
        high = push.astype(BF16)
        low = (push - high.astype(F32)).astype(BF16)
        once = lax.dot_general(
            rr[j],
            jnp.concatenate([high, low], 1),
            (((1,), (1,)), ((), ())),
            preferred_element_type=F32,
        )
        acc[h] += once * ids[3, batch * BATCH + q].astype(F32)

    def both(buf_next, buf_now, batch_next, batch_now):
        for q in range(BATCH):
            quantities(buf_next, batch_next, q)
            forces(buf_now, batch_now, q)

    @pl.when(pairs > 0)
    def _():
        last = 2 * (first + pairs) - 1
        for q in range(BATCH):
            quantities(buf_a, 2 * first, q)

        def body(i, carry):
            both(buf_b, buf_a, 2 * i + 1, 2 * i)
            both(buf_a, buf_b, jnp.minimum(2 * i + 2, last), 2 * i + 1)
            return carry

        at = first
        for size in sizes:

            def several(i, carry, size=size, at=at):
                for k in range(size):
                    body(at + i * size + k, carry)
                return carry

            steps = (first + pairs - at) // size
            lax.fori_loop(0, steps, several, 0)
            at = at + steps * size


def near_place(b):
    return (b // (GRID * LAYERS) * (GRID + 2) + b // LAYERS % GRID + 1) * (LAYERS + 2) + b % LAYERS + 1


def near_kernel(steps, ids, region, w_home, w_src, acc, lx, ly, rx, ry, rr, buf_a, buf_b):
    def owned(i, carry):
        first = near_place(i * GROUP)
        places = [first + g for g in range(GROUP)]
        z = jnp.concatenate([factors(region[p]) for p in places], 1)
        store_source(places, z, w_src, rx, ry, rr)
        store_home(i * GROUP, z, w_home, lx, ly)
        return carry

    def rim_place(i):
        side, at = i // 28, i % 28
        place_y = jnp.where(at < 10, 0, jnp.where(at < 20, GRID + 1, 1 + (at - 20) // 2))
        place_z = jnp.where(at < 20, at % 10, (at - 20) % 2 * (LAYERS + 1))
        return (side * (GRID + 2) + place_y) * (LAYERS + 2) + place_z

    def rim(i, carry):
        places = [rim_place(i * GROUP + g) for g in range(GROUP)]
        z = jnp.concatenate([factors(region[p]) for p in places], 1)
        store_source(places, z, w_src, rx, ry, rr)
        return carry

    lax.fori_loop(0, 128 // GROUP, owned, 0, unroll=8)
    lax.fori_loop(0, 112 // GROUP, rim, 0, unroll=14)
    acc[...] = jnp.zeros_like(acc)
    all_tiles(SIZES, 0, steps[0], ids, lx, ly, rx, ry, rr, acc, buf_a, buf_b)


def far_kernel(steps, ids, low, high, region, w_src, lx, ly, acc, out, acc_out, rx, ry, rr, buf_a, buf_b):
    def prepare(i, carry):
        for k, (plane, off_x) in enumerate(((low, -44.0), (high, 44.0))):
            places = [i * FAR_GROUP + g for g in range(FAR_GROUP)]
            z = jnp.concatenate([factors(plane[p], off_x * SCALE) for p in places], 1)
            store_source([p + 60 * k for p in places], z, w_src, rx, ry, rr)
        return carry

    lax.fori_loop(0, 60 // FAR_GROUP, prepare, 0, unroll=6)
    all_tiles(SIZES, steps[0], steps[1], ids, lx, ly, rx, ry, rr, acc_out, buf_a, buf_b)

    def finish(s, carry):
        first = near_place(4 * s)
        for k in range(4):
            sums = acc_out[4 * s + k]
            head, tail = sums[:8], sums[8:]
            weighed = head + pltpu.roll(head, 4, 0) + tail
            out[s, 3 * k : 3 * k + 3] = (region[first + k] * head[3:4] - weighed)[:3]
        return carry

    lax.fori_loop(0, 32, finish, 0, unroll=8)


def tile_lists(tiles, blocks):
    home, source = tiles[0], tiles[1]
    slot, member = source // blocks, source % blocks
    step_x = slot // 9 - 1
    place_y = member // LAYERS % GRID + (slot // 3 % 3 - 1) * GRID + 1
    place_z = member % LAYERS + (slot % 3 - 1) * LAYERS + 1
    plane = place_y * (LAYERS + 2) + place_z
    side = jnp.where(step_x == 0, member // (GRID * LAYERS), (step_x + 1) // 2)
    listed = home >= 0
    unit = 2 * BATCH
    order = jnp.arange(home.shape[0])
    upto = order[None, :] <= order[:, None]
    key = home * (27 * blocks) + source
    same = key[None, :] == key[:, None]
    times = jnp.sum(jnp.where(same, 1, 0), 1)
    first = jnp.sum(jnp.where(same & upto, 1, 0), 1) == 1
    near = listed & first & (step_x == 0)
    far = listed & first & (step_x != 0)
    near_at = jnp.sum(jnp.where(upto & near[None, :], 1, 0), 1)
    far_at = jnp.sum(jnp.where(upto & far[None, :], 1, 0), 1)
    near_steps = (jnp.sum(near.astype(jnp.int32)) + unit - 1) // unit
    far_steps = (jnp.sum(far.astype(jnp.int32)) + unit - 1) // unit
    at = jnp.where(near, near_at - 1, jnp.where(far, near_steps * unit + far_at - 1, -1))
    code = home * 256 + side * 60 + plane + 1
    slots = jnp.arange(home.shape[0] + 2 * unit)
    found = jnp.sum(jnp.where(slots[:, None] == at[None, :], code[None, :], 0), 1)
    times = jnp.sum(jnp.where(slots[:, None] == at[None, :], times[None, :], 0), 1)
    real = found > 0
    code = jnp.maximum(found - 1, 0)
    ids = jnp.stack([code // 256, code % 256, jnp.where(real, code // 256, blocks), times])
    return jnp.stack([near_steps, far_steps]), ids


def per_device(coords, charges, atom_types, lj_sigma, lj_epsilon, tile_list):
    blocks, width = coords.shape[2], coords.shape[3]
    peers = lax.axis_size("gy") * lax.axis_size("gz")
    vmem = pl.BlockSpec(memory_space=pltpu.VMEM)
    smem = pl.BlockSpec(memory_space=pltpu.SMEM)
    gz = lax.axis_index("gz")
    small = pltpu.CompilerParams(vmem_limit_bytes=8 << 20)
    outgoing = pl.pallas_call(
        pack_kernel,
        out_shape=jax.ShapeDtypeStruct((peers * SENT, width), F32),
        in_specs=[smem, smem] + [pl.BlockSpec(memory_space=pl.ANY)] * 3,
        out_specs=vmem,
        scratch_shapes=[
            pltpu.VMEM((3, blocks, width), F32),
            pltpu.VMEM((blocks, width), F32),
            pltpu.VMEM((blocks, width), jnp.int32),
            pltpu.SemaphoreType.DMA((3,)),
        ],
        compiler_params=pltpu.CompilerParams(vmem_limit_bytes=65011712),
    )((gz % 2).reshape(1), (gz // 2).reshape(1), coords[:, 0], charges[0], atom_types[0])
    arrived = lax.all_to_all(
        outgoing.reshape(peers, SENT, width), ("gy", "gz"), split_axis=0, concat_axis=0, tiled=True
    )
    steps, ids = tile_lists(tile_list[0, 0, 0], blocks)
    w_home, w_src = weights(lj_sigma, lj_epsilon)
    region = pl.pallas_call(
        unpack_kernel,
        out_shape=jax.ShapeDtypeStruct((NEAR, 8, width), F32),
        in_specs=[vmem],
        out_specs=vmem,
        compiler_params=small,
    )(arrived)
    count = lax.axis_size("gx")
    forward = [(i, (i + 1) % count) for i in range(count)]
    backward = [(target, source) for source, target in forward]
    low = lax.ppermute(region[180:240], "gx", forward)
    high = lax.ppermute(region[:60], "gx", backward)

    def source_scratch(n):
        return [
            pltpu.VMEM((n, NX, 256), BF16),
            pltpu.VMEM((n, NY, 256), BF16),
            pltpu.VMEM((n, 16, 256), BF16),
            pltpu.VMEM((BATCH, 2, 128, 256), F32),
            pltpu.VMEM((BATCH, 2, 128, 256), F32),
        ]

    acc_shape = jax.ShapeDtypeStruct((blocks + 1, 16, width), F32)
    factor_shape = jax.ShapeDtypeStruct((blocks, 128, 128), BF16)
    acc, lx, ly = pl.pallas_call(
        near_kernel,
        out_shape=[acc_shape, factor_shape, factor_shape],
        in_specs=[smem, smem, vmem, vmem, vmem],
        out_specs=[vmem] * 3,
        scratch_shapes=source_scratch(NEAR),
        compiler_params=pltpu.CompilerParams(vmem_limit_bytes=28 << 20),
        cost_estimate=pl.CostEstimate(flops=10**10, bytes_accessed=10**7, transcendentals=10**6),
    )(steps, ids, region, w_home, w_src)
    totals, _ = pl.pallas_call(
        far_kernel,
        out_shape=[jax.ShapeDtypeStruct((peers, 12, width), F32), acc_shape],
        in_specs=[smem, smem] + [vmem] * 7,
        out_specs=[vmem] * 2,
        scratch_shapes=source_scratch(120),
        input_output_aliases={8: 1},
        compiler_params=pltpu.CompilerParams(vmem_limit_bytes=24 << 20),
    )(steps, ids, low, high, region, w_src, lx, ly, acc)
    back = lax.all_to_all(totals, ("gy", "gz"), split_axis=0, concat_axis=0, tiled=True)
    return back.reshape(peers, 4, 3, width).transpose(2, 1, 0, 3).reshape(3, 1, blocks, width)


def solution(mesh):
    return jax.shard_map(
        per_device,
        mesh=mesh,
        in_specs=(
            P(None, "gx", ("gy", "gz"), None),
            P("gx", ("gy", "gz"), None),
            P("gx", ("gy", "gz"), None),
            P(),
            P(),
            P("gx", "gy", "gz", None, None),
        ),
        out_specs=P(None, "gx", ("gy", "gz"), None),
        check_vma=False,
    )
```
